128 devices in a mesh: row: 16 (over x, z), col: 8 (over y, core).
Axes of the slice: x: 4, y: 4, z: 4, core: 2. Of those that a mesh axis runs over, the one named last changes fastest.
Arguments:
- depth_old: float32 [384, 256, 256], P(('row', 'col')), may hold values from 0 to 1.2
- flow_x_old: float32 [384, 256, 256], P(('row', 'col')), may hold values from -4 to 4
- flow_y_old: float32 [384, 256, 256], P(('row', 'col')), may hold values from -4 to 4
- floor_old: bfloat16 [384, 256, 256], P(('row', 'col')), may hold values from 0 to 0.29882812
- width_old: bfloat16 [384, 256, 256], P(('row', 'col')), may hold values from 0.5 to 4
- chan_old: bfloat16 [384, 256, 256], P(('row', 'col')), may hold values from 0.5 to 1
- rough_old: bfloat16 [384, 256, 256], P(('row', 'col')), may hold values from 0.019897461 to 0.099609375
- route: int32 [384, 3], replicated, may hold values from 0 to 15, as said below
- wet_tiles: int32 [16, 24], P('row', 'col'), may hold values 0 or 1
Outputs:
- depth_new: float32 [4096, 6144], P('row', 'col')
- flow_x_new: float32 [4096, 6144], P('row', 'col')
- flow_y_new: float32 [4096, 6144], P('row', 'col')
The draws below stay inside these ranges and needn't reach their ends.
Inputs may be any that keep to these rules, and one draw needn't show every extreme that they name: route is a bijection of old slots onto new slots. Exactly 3 tiles leave each device and 3 arrive; those leaving one device go to distinct mesh rows and distinct mesh columns, and those arriving at one device come from distinct mesh rows and distinct mesh columns.
All inputs are finite; a program needn't handle non-finite values. No bound on the sum of `wet_tiles` on one device may be relied on, other than what follows from the above.
Results may differ from the reference program's by a relative error of at most 0.0003.
Values may be sent and summed in bfloat16 or wider, within the bound.
A program may use at most 128 MiB of HBM per device.

```python
import math
import jax
import jax.numpy as jnp
from jax import lax

TS = 256
SR = 1
SC = 3
ITERS = 4
MOVES = 3
SLOTS = 3
TILES = 384
NTR = 16
NTC = 24
N_ROW = 16
N_COL = 8


def draw_route(key, part):
    key = jax.random.fold_in(key, 11)
    keys = jax.random.split(key, 6)
    perm_rows = jax.random.permutation(keys[0], N_ROW).astype(jnp.int32)
    perm_cols = jax.random.permutation(keys[1], N_COL).astype(jnp.int32)
    inv_rows = jnp.argsort(perm_rows).astype(jnp.int32)
    inv_cols = jnp.argsort(perm_cols).astype(jnp.int32)
    shift_rows = 1 + jax.random.permutation(keys[2], N_ROW - 1).astype(jnp.int32)[:MOVES]
    shift_cols = jax.random.permutation(keys[3], N_COL).astype(jnp.int32)[:MOVES]
    full_rows = jnp.concatenate([shift_rows, jnp.zeros((SLOTS - MOVES,), jnp.int32)])
    full_cols = jnp.concatenate([shift_cols, jnp.zeros((SLOTS - MOVES,), jnp.int32)])
    row_ids = jnp.arange(N_ROW, dtype=jnp.int32)[:, None, None]
    col_ids = jnp.arange(N_COL, dtype=jnp.int32)[None, :, None]
    move_ids = jnp.arange(SLOTS, dtype=jnp.int32)[None, None, :]
    moving = move_ids < MOVES
    full = (N_ROW, N_COL, SLOTS)
    dest_row = jnp.broadcast_to(jnp.where(moving, perm_rows[(inv_rows[row_ids] + full_rows[move_ids]) % N_ROW], row_ids), full)
    dest_col = jnp.broadcast_to(jnp.where(moving, perm_cols[(inv_cols[col_ids] + full_cols[move_ids]) % N_COL], col_ids), full)
    slot_keys = jax.random.split(keys[4], N_ROW * N_COL)
    sigma = jax.vmap(lambda k: jax.random.permutation(k, SLOTS))(slot_keys).astype(jnp.int32).reshape(full)
    dest_slot = sigma[dest_row, dest_col, jnp.broadcast_to(move_ids, full)]
    old_keys = jax.random.split(keys[5], N_ROW * N_COL)
    anchor = jax.vmap(lambda k: jax.random.permutation(k, SLOTS))(old_keys).astype(jnp.int32).reshape(full)
    inverse = jnp.argsort(anchor, axis=-1).astype(jnp.int32)
    stacked = jnp.stack([dest_row, dest_col, dest_slot], -1)
    ordered = jnp.take_along_axis(stacked, inverse[..., None], axis=2)
    return ordered.reshape(TILES, 3).astype(jnp.int32)


def set_ends(array, key, least, largest):
    extent = array.shape
    spot = [jax.random.randint(jax.random.fold_in(key, axis), (), 0, extent[axis]) for axis in range(len(extent))]
    array = array.at[tuple(spot)].set(least)
    longest = extent.index(max(extent))
    spot[longest] = (spot[longest] + 1) % extent[longest]
    return array.at[tuple(spot)].set(largest)


def steps_of(stream_key, dims, cuts, low, largest):
    factor_of = 1.0
    for dim, blocks in cuts:
        steps = jax.random.uniform(jax.random.fold_in(jax.random.fold_in(stream_key, 6), dim), (blocks,), jnp.float32, low / len(cuts), largest / len(cuts))
        factor_of = factor_of * jnp.repeat(jnp.exp(steps), dims[dim] // blocks).reshape((-1,) + (1,) * (len(dims) - 1 - dim))
    return factor_of


def centred(key, dims, scale, most, pieces=(), kind=jnp.bfloat16):
    gain = steps_of(key, dims, pieces, -0.22, 0.18) if pieces else 1.0
    entries = jax.random.normal(key, dims, jnp.float32) * scale * gain
    return jnp.minimum(jnp.maximum(entries, -most), most).astype(kind)


def setup_inputs(seed: int = 0) -> dict:
    key_list = jax.random.split(jax.random.key(seed), 10)
    depth_old = jnp.clip(1.2 * jax.random.uniform(key_list[0], (TILES, TS, TS), jnp.float32) ** steps_of(key_list[0], (TILES, TS, TS), ((0, 128),), -0.2, 0.2), 0.0, 1.2)
    flow_x_old = centred(key_list[1], (TILES, TS, TS), 1.0, 4.0, ((0, 128),), jnp.float32)
    flow_y_old = centred(key_list[2], (TILES, TS, TS), 1.0, 4.0, ((0, 128),), jnp.float32)
    floor_old = jnp.clip(0.29882812 * jax.random.uniform(key_list[3], (TILES, TS, TS), jnp.float32) ** steps_of(key_list[3], (TILES, TS, TS), ((0, 128),), -0.2, 0.2), 0.0, 0.29882812).astype(jnp.bfloat16)
    width_old = jnp.clip(0.5 + 3.5 * jax.random.uniform(key_list[4], (TILES, TS, TS), jnp.float32) ** steps_of(key_list[4], (TILES, TS, TS), ((0, 128),), -0.2, 0.2), 0.5, 4.0).astype(jnp.bfloat16)
    chan_old = jnp.clip(0.5 + 0.5 * jax.random.uniform(key_list[5], (TILES, TS, TS), jnp.float32) ** steps_of(key_list[5], (TILES, TS, TS), ((0, 128),), -0.2, 0.2), 0.5, 1.0).astype(jnp.bfloat16)
    rough_old = jnp.clip(jnp.exp(math.log(0.099609375) - 1.61066415 * jax.random.uniform(key_list[6], (TILES, TS, TS), jnp.float32) ** steps_of(key_list[6], (TILES, TS, TS), ((0, 128),), -0.2, 0.2)), 0.019897461, 0.099609375).astype(jnp.bfloat16)
    route = draw_route(jax.random.fold_in(key_list[9], 71), 0)
    wet_tiles = set_ends((jax.random.randint(key_list[8], (NTR, NTC), 0, 5) < 4).astype(jnp.int32), jax.random.fold_in(key_list[8], 1), 0, 1)
    return dict(depth_old=depth_old, flow_x_old=flow_x_old, flow_y_old=flow_y_old, floor_old=floor_old, width_old=width_old, chan_old=chan_old, rough_old=rough_old, route=route, wet_tiles=wet_tiles)


GRAV = 9.81
CELL = 5.0
STEP = 0.1
RMIN = 0.1


def shift_east(values):
    return jnp.pad(values[:, 1:], ((0, 0), (0, 1)))


def shift_west(values):
    return jnp.pad(values[:, :-1], ((0, 0), (1, 0)))


def shift_south(values):
    return jnp.pad(values[1:, :], ((0, 1), (0, 0)))


def shift_north(values):
    return jnp.pad(values[:-1, :], ((1, 0), (0, 0)))


def face_flow(flow, surface, channel_bed, width, chan, rough, wetness, shifter):
    surface_n = shifter(surface)
    bed_n = shifter(channel_bed)
    crest = jnp.maximum(surface, surface_n) - jnp.maximum(channel_bed, bed_n)
    face_width = jnp.minimum(width, shifter(width))
    face_chan = jnp.minimum(chan, shifter(chan))
    flow_area = face_width * crest + (CELL - face_width) * jnp.maximum(crest - face_chan, 0.0)
    face_rough = 0.5 * (rough + shifter(rough))
    radius = jnp.maximum(flow_area / CELL, RMIN)
    slope = (surface_n - surface) / CELL
    updated = (flow - GRAV * STEP * flow_area * slope) / (
        1.0 + GRAV * STEP * face_rough * face_rough * jnp.abs(flow) / (CELL * radius ** (7.0 / 3.0)))
    return jnp.where(wetness * shifter(wetness) > 0, updated, 0.0)


def advance(water, along_x, along_y, floor, width, chan, rough, wetness):
    channel_bed = floor - chan
    surface = channel_bed + water
    new_x = face_flow(along_x, surface, channel_bed, width, chan, rough, wetness, shift_east)
    new_y = face_flow(along_y, surface, channel_bed, width, chan, rough, wetness, shift_south)
    volume = CELL * width * jnp.minimum(water, chan) + CELL * CELL * jnp.maximum(water - chan, 0.0)
    inflow = shift_west(new_x) - new_x + shift_north(new_y) - new_y
    volume = jnp.maximum(volume + STEP * inflow, 0.0)
    cap_volume = CELL * width * chan
    water_new = jnp.minimum(volume, cap_volume) / (CELL * width) + jnp.maximum(volume - cap_volume, 0.0) / (CELL * CELL)
    return water_new, new_x, new_y


def to_grid(flat):
    shaped = flat.reshape(N_ROW, N_COL, SR, SC, TS, TS).transpose(0, 2, 4, 1, 3, 5)
    return shaped.reshape(N_ROW * SR * TS, N_COL * SC * TS)


def reference(depth_old, flow_x_old, flow_y_old, floor_old, width_old, chan_old, rough_old, route, wet_tiles):
    target = ((route[:, 0] * N_COL + route[:, 1]) * SLOTS + route[:, 2]).astype(jnp.int32)

    def place(values):
        return to_grid(jnp.zeros_like(values).at[target].set(values))

    water = place(depth_old)
    along_x = place(flow_x_old)
    along_y = place(flow_y_old)
    floor = place(floor_old).astype(jnp.float32)
    width = place(width_old).astype(jnp.float32)
    chan = place(chan_old).astype(jnp.float32)
    rough = place(rough_old).astype(jnp.float32)
    wetness = jnp.repeat(jnp.repeat(wet_tiles, TS, 0), TS, 1).astype(jnp.float32)

    def one_step(index, carry):
        return advance(carry[0], carry[1], carry[2], floor, width, chan, rough, wetness)

    water, along_x, along_y = lax.fori_loop(0, ITERS, one_step, (water, along_x, along_y))
    return water, along_x, along_y
```

```python
import jax
import jax.numpy as jnp
from jax import lax
from jax.experimental import pallas as pl
from jax.experimental.pallas import tpu as pltpu
from jax.sharding import PartitionSpec as P

ITERS = 4
GRAV = 9.81
CELL = 5.0
STEP = 0.1
RMIN = 0.1

NX, NZ, NC = 4, 4, 8
DEVICES = NX * NZ * NC
SLOTS = 3
HALVES = 2
CHUNKS = SLOTS * HALVES
TILE = 256
BLOCK = 16
LANES = 128
FIRST = ("yxz", "xzy", "zyx") * 2
SECOND = ("zxy", "yzx", "xyz") * 2
PIECES = (CHUNKS, NX, NZ, NC, BLOCK, LANES)

PAD = 8
ROWS = TILE + 2 * PAD
COLS = SLOTS * TILE
WIDE = COLS + LANES
STRIPS = ROWS // 8
REACH = 4
FIELDS = 7
WATER, FLOW_X, FLOW_Y, BED, WIDTH, CHAN, ROUGH = range(FIELDS)
F32 = jnp.float32


def to_code(values):
    return values.astype(jnp.int32).astype(jnp.int16)


def flow_code(flow):
    root = jnp.sqrt(jnp.sqrt(jnp.abs(flow) * 0.25))
    size = jnp.minimum(root * 32767.0 + 0.5, 32767.0).astype(jnp.int32)
    return jnp.where(flow < 0, -size, size).astype(jnp.int16)


def flow_value(code):
    return (code * code) * (code * jnp.abs(code)) * (4.0 / 32767.0**4)


def floor_code(floor):
    coarse = (floor * 65536.0).astype(jnp.int32)
    fine = -((floor * 16777216.0 + 0.5).astype(jnp.int32))
    return jnp.where(floor < 2.0**-9, fine, coarse).astype(jnp.int16)


def floor_value(code):
    return jnp.where(code < 0, code * -(2.0**-24), code * 2.0**-16)


def part(ref, chunk, axis, index):
    if axis == "x":
        return ref.at[chunk, index]
    if axis == "z":
        return ref.at[chunk, :, index]
    return ref.at[chunk, :, :, index]


def migrate_and_route(
    depth_ref, fx_ref, fy_ref, floor_ref, width_ref, chan_ref, rough_ref, source_ref, wet_ref,
    water_out, fx_out, fy_out,
    coded, first_a, first_b, middle, sorted_, second_a, second_b, arrived,
    fields, sent_w, sent_e, got_e, got_w, level, volume, cap, inverse,
    bed_x, wide_x, deep_x, drag_x, bed_y, wide_y, deep_y, drag_y,
    send_sem, recv_sem, local_sem, rim_send, rim_recv,
):
    row = lax.axis_index("row")
    col = lax.axis_index("col")
    own_x = row // NZ
    own_z = row % NZ

    def place(x, z, c):
        return (x * NZ + z, c)

    west = (row, (col + NC - 1) % NC)
    east = (row, (col + 1) % NC)
    north = ((row + NX * NZ - 1) % (NX * NZ), col)
    south = ((row + 1) % (NX * NZ), col)

    barrier = pltpu.get_barrier_semaphore()
    greeted = [place((own_x + d) % NX, own_z, col) for d in (1, 2, 3)]
    greeted += [place(own_x, (own_z + d) % NZ, col) for d in (1, 2, 3)]
    greeted += [place(own_x, own_z, (col + d) % NC) for d in range(1, NC)]
    greeted += [north, south]
    for device in greeted:
        pl.semaphore_signal(barrier, inc=1, device_id=device, device_id_type=pl.DeviceIdType.MESH)

    def encode(chunk):
        slot, half = chunk // HALVES, chunk % HALVES
        lanes = pl.ds(half * LANES, LANES)

        def block(b, _):
            rows = pl.ds(pl.multiple_of(b * BLOCK, BLOCK), BLOCK)

            def put(plane, code):
                coded[chunk, b // NZ, b % NZ, plane] = code

            depth = depth_ref[slot, rows, lanes] * 16384.0
            high = depth.astype(jnp.int32)
            low = ((depth - high.astype(F32)) * 65536.0).astype(jnp.int32) - 32768
            put(0, high.astype(jnp.int16))
            put(1, low.astype(jnp.int16))
            put(2, flow_code(fx_ref[slot, rows, lanes]))
            put(3, flow_code(fy_ref[slot, rows, lanes]))
            put(4, floor_code(floor_ref[slot, rows, lanes].astype(F32)))
            put(5, to_code(width_ref[slot, rows, lanes].astype(F32) * 256.0))
            put(6, to_code(chan_ref[slot, rows, lanes].astype(F32) * 256.0))
            put(7, to_code(rough_ref[slot, rows, lanes].astype(F32) * 8192.0))
            return 0

        lax.fori_loop(0, TILE // BLOCK, block, 0)

    def decode(chunk):
        slot, half = chunk // HALVES, chunk % HALVES
        lanes = pl.ds(slot * TILE + half * LANES, LANES)
        wet = wet_ref[0, slot].astype(F32)

        def block(b, _):
            rows = pl.ds(pl.multiple_of(PAD + b * BLOCK, 8), BLOCK)

            def get(plane):
                return arrived[chunk, b // NZ, b % NZ, plane].astype(jnp.int32).astype(F32)

            chan = get(6) * (1.0 / 256.0)
            fields[WATER, rows, lanes] = get(0) * 2.0**-14 + (get(1) + 32768.0) * 2.0**-30
            fields[FLOW_X, rows, lanes] = flow_value(get(2))
            fields[FLOW_Y, rows, lanes] = flow_value(get(3))
            fields[BED, rows, lanes] = floor_value(get(4)) - chan
            fields[WIDTH, rows, lanes] = get(5) * (1.0 / 256.0)
            fields[CHAN, rows, lanes] = chan
            fields[ROUGH, rows, lanes] = get(7) * (1.0 / 8192.0) * wet - (1.0 - wet)
            return 0

        lax.fori_loop(0, TILE // BLOCK, block, 0)

    def copies(stage, chunk, axis, source, target):
        base = (stage * CHUNKS + chunk) * 8
        remote = []
        if axis == "y":
            me = col
            steps = [4, 5, 2, 3, 6, 7, 1]
            partners = [((col + (d // 2) * 2) % NC) // 2 * 2 + (col + d % 2) % 2 for d in steps]
            devices = [place(own_x, own_z, c) for c in partners]
        elif axis == "x":
            me = own_x
            partners = [(own_x + d) % NX for d in (2, 1, 3)]
            devices = [place(x, own_z, col) for x in partners]
        else:
            me = own_z
            partners = [(own_z + d) % NZ for d in (2, 1, 3)]
            devices = [place(own_x, z, col) for z in partners]
        for q, (partner, device) in enumerate(zip(partners, devices)):
            remote.append(
                pltpu.make_async_remote_copy(
                    src_ref=part(source, chunk, axis, partner),
                    dst_ref=part(target, chunk, axis, me),
                    send_sem=send_sem.at[base + q],
                    recv_sem=recv_sem.at[base + q],
                    device_id=device,
                    device_id_type=pl.DeviceIdType.MESH,
                )
            )
        local = pltpu.make_async_copy(
            part(source, chunk, axis, me),
            part(target, chunk, axis, me),
            local_sem.at[stage * CHUNKS + chunk],
        )
        return remote, local

    started = []

    def launch(stage, chunk, axis, source, target):
        remote, local = copies(stage, chunk, axis, source, target)
        for copy in remote:
            copy.start()
        local.start()
        started.extend(remote)
        return remote, local

    def landed(pair):
        remote, local = pair
        for copy in remote:
            copy.wait_recv()
        local.wait()

    encode(0)
    pl.semaphore_wait(barrier, len(greeted))
    flying = []
    for chunk in range(CHUNKS):
        if chunk > 0:
            encode(chunk)
        flying.append(launch(0, chunk, FIRST[chunk][0], coded, first_a))
    for stage, source, target in ((1, first_a, first_b), (2, first_b, middle)):
        for chunk in range(CHUNKS):
            landed(flying[chunk])
            flying[chunk] = launch(stage, chunk, FIRST[chunk][stage], source, target)
    for chunk in range(CHUNKS):
        landed(flying[chunk])

    taken = middle.reshape(CHUNKS * DEVICES, BLOCK, LANES)
    ordered = sorted_.reshape(CHUNKS * DEVICES, BLOCK, LANES)
    for chunk in range(CHUNKS):
        slot, half = chunk // HALVES, chunk % HALVES

        def move(k, _):
            for u in range(8):
                d = k * 8 + u
                ordered[chunk * DEVICES + d] = taken[source_ref[slot * DEVICES + d] + half * DEVICES]
            return 0

        lax.fori_loop(0, DEVICES // 8, move, 0)
        flying[chunk] = launch(3, chunk, SECOND[chunk][0], sorted_, second_a)
    for stage, source, target in ((4, second_a, second_b), (5, second_b, arrived)):
        for chunk in range(CHUNKS):
            landed(flying[chunk])
            flying[chunk] = launch(stage, chunk, SECOND[chunk][stage - 3], source, target)
    for chunk in range(CHUNKS):
        landed(flying[chunk])
        decode(chunk)

    lane = lax.broadcasted_iota(jnp.int32, (8, LANES), 1)

    def pack(k, _):
        rows = pl.ds(pl.multiple_of(PAD + k * 8, 8), 8)
        left = jnp.zeros((8, LANES), F32)
        right = jnp.zeros((8, LANES), F32)
        for f in range(FIELDS):
            here = (lane >= REACH * f) & (lane < REACH * (f + 1))
            low = fields[f, rows, pl.ds(0, LANES)]
            high = fields[f, rows, pl.ds(COLS - LANES, LANES)]
            left = jnp.where(here, pltpu.roll(low, REACH * f, 1) if f else low, left)
            right = jnp.where(here, pltpu.roll(high, REACH * (f + 1), 1), right)
        out = pl.ds(pl.multiple_of(k * 8, 8), 8)
        sent_w[out, :] = left
        sent_e[out, :] = right
        return 0

    lax.fori_loop(0, TILE // 8, pack, 0)

    def rim(number, source, target, device):
        copy = pltpu.make_async_remote_copy(
            src_ref=source, dst_ref=target, send_sem=rim_send.at[number],
            recv_sem=rim_recv.at[number], device_id=device,
            device_id_type=pl.DeviceIdType.MESH,
        )
        copy.start()
        started.append(copy)
        return copy

    side = [rim(0, sent_w, got_e, west), rim(1, sent_e, got_w, east)]
    for copy in side:
        copy.wait_recv()

    at_east = col == NC - 1
    at_west = col == 0

    def unpack(k, _):
        source = pl.ds(pl.multiple_of(k * 8, 8), 8)
        rows = pl.ds(pl.multiple_of(PAD + k * 8, 8), 8)
        from_e = got_e[source, :]
        from_w = got_w[source, :]
        for f in range(FIELDS):
            low = pltpu.roll(from_e, LANES - REACH * f, 1) if f else from_e
            high = pltpu.roll(from_w, LANES - REACH * (f + 1), 1)
            if f == ROUGH:
                low = jnp.where(at_east, -1.0, low)
                high = jnp.where(at_west, -1.0, high)
            fill = 1.0 if f in (WIDTH, CHAN) else (-1.0 if f == ROUGH else 0.0)
            mixed = jnp.where(lane < REACH, low, jnp.where(lane >= LANES - REACH, high, fill))
            fields[f, rows, pl.ds(COLS, LANES)] = mixed
        return 0

    lax.fori_loop(0, TILE // 8, unpack, 0)

    ends = [
        rim(2, fields.at[:, pl.ds(PAD, 8), :], fields.at[:, pl.ds(PAD + TILE, 8), :], north),
        rim(3, fields.at[:, pl.ds(TILE, 8), :], fields.at[:, pl.ds(0, 8), :], south),
    ]
    for copy in ends:
        copy.wait_recv()
    for copy in started:
        copy.wait_send()
    first = fields[ROUGH, pl.ds(0, 8), :]
    fields[ROUGH, pl.ds(0, 8), :] = jnp.where(row == 0, -1.0, first)
    last = fields[ROUGH, pl.ds(PAD + TILE, 8), :]
    fields[ROUGH, pl.ds(PAD + TILE, 8), :] = jnp.where(row == NX * NZ - 1, -1.0, last)

    bottom = lax.broadcasted_iota(jnp.int32, (8, WIDE), 0) == 7
    top = lax.broadcasted_iota(jnp.int32, (8, WIDE), 0) == 0

    def strip(k):
        return pl.ds(pl.multiple_of(k * 8, 8), 8)

    def to_east(values):
        return pltpu.roll(values, WIDE - 1, 1)

    def to_west(values):
        return pltpu.roll(values, 1, 1)

    def to_south(values, after):
        return jnp.where(bottom, pltpu.roll(after, 7, 0), pltpu.roll(values, 7, 0))

    def faces(k, _):
        here = strip(k)
        there = strip(jnp.minimum(k + 1, STRIPS - 1))
        water = fields[WATER, here, :]
        bed, width = fields[BED, here, :], fields[WIDTH, here, :]
        chan, rough = fields[CHAN, here, :], fields[ROUGH, here, :]
        level[here, :] = bed + water
        volume[here, :] = CELL * width * jnp.minimum(water, chan) + CELL * CELL * jnp.maximum(
            water - chan, 0.0
        )
        cap[here, :] = CELL * width * chan
        inverse[here, :] = 1.0 / (CELL * width)
        for shift, bed_f, wide_f, deep_f, drag_f in (
            (lambda f, v: to_east(v), bed_x, wide_x, deep_x, drag_x),
            (lambda f, v: to_south(v, fields[f, there, :]), bed_y, wide_y, deep_y, drag_y),
        ):
            bed_f[here, :] = jnp.maximum(bed, shift(BED, bed))
            wide_f[here, :] = jnp.minimum(width, shift(WIDTH, width))
            deep_f[here, :] = jnp.minimum(chan, shift(CHAN, chan))
            rough_n = shift(ROUGH, rough)
            mean = 0.5 * (rough + rough_n)
            drag_f[here, :] = jnp.where(
                jnp.minimum(rough, rough_n) > 0, (GRAV * STEP / CELL) * mean * mean, -1.0
            )
        return 0

    lax.fori_loop(0, STRIPS, faces, 0)

    def face_flow(flow, surface, surface_n, bed_f, wide_f, deep_f, drag_f):
        crest = jnp.maximum(surface, surface_n) - bed_f
        area = wide_f * crest + (CELL - wide_f) * jnp.maximum(crest - deep_f, 0.0)
        radius = jnp.maximum(area * (1.0 / CELL), RMIN)
        friction = drag_f * jnp.abs(flow) * jnp.exp(jnp.log(radius) * (-7.0 / 3.0))
        updated = (flow - (GRAV * STEP / CELL) * area * (surface_n - surface)) / (1.0 + friction)
        return jnp.where(drag_f > 0, updated, 0.0)

    for step in range(ITERS):
        final = step == ITERS - 1

        def sweep(k, above):
            here = strip(k)
            there = strip(jnp.minimum(k + 1, STRIPS - 1))
            surface = level[here, :]
            surface_s = to_south(surface, level[there, :])
            new_x = face_flow(
                fields[FLOW_X, here, :], surface, to_east(surface),
                bed_x[here, :], wide_x[here, :], deep_x[here, :], drag_x[here, :],
            )
            new_y = face_flow(
                fields[FLOW_Y, here, :], surface, surface_s,
                bed_y[here, :], wide_y[here, :], deep_y[here, :], drag_y[here, :],
            )
            rolled = pltpu.roll(new_y, 1, 0)
            inflow = to_west(new_x) - new_x + jnp.where(top, above, rolled) - new_y
            held = jnp.maximum(volume[here, :] + STEP * inflow, 0.0)
            most = cap[here, :]
            water = jnp.minimum(held, most) * inverse[here, :] + jnp.maximum(
                held - most, 0.0
            ) * (1.0 / (CELL * CELL))
            if final:
                out = strip(jnp.clip(k - PAD // 8, 0, TILE // 8 - 1))
                water_out[out, :] = water[:, :COLS]
                fx_out[out, :] = new_x[:, :COLS]
                fy_out[out, :] = new_y[:, :COLS]
            else:
                fields[FLOW_X, here, :] = new_x
                fields[FLOW_Y, here, :] = new_y
                volume[here, :] = held
                level[here, :] = fields[BED, here, :] + water
            return rolled

        stop = (PAD + TILE) // 8 if final else STRIPS
        lax.fori_loop(0, stop, sweep, jnp.zeros((8, WIDE), F32))


def body(depth, flow_x, flow_y, floor, width, chan, rough, route, wet_tiles):
    target = (route[:, 0] * NC + route[:, 1]) * SLOTS + route[:, 2]
    old = jnp.arange(DEVICES * SLOTS, dtype=jnp.int32)
    where_held = (old % SLOTS) * (HALVES * DEVICES) + old // SLOTS
    slot_major = (old % DEVICES) * SLOTS + old // DEVICES
    source = jnp.sum(
        jnp.where(slot_major[:, None] == target[None, :], where_held[None, :], 0), axis=1
    )
    vmem = pl.BlockSpec(memory_space=pltpu.VMEM)
    smem = pl.BlockSpec(memory_space=pltpu.SMEM)
    pieces = pltpu.VMEM(PIECES, jnp.int16)
    grid = pltpu.VMEM((ROWS, WIDE), F32)
    edge = pltpu.VMEM((TILE, LANES), F32)
    out = jax.ShapeDtypeStruct((TILE, COLS), F32)
    return pl.pallas_call(
        migrate_and_route,
        out_shape=(out, out, out),
        in_specs=[vmem] * 7 + [smem] * 2,
        out_specs=(vmem, vmem, vmem),
        scratch_shapes=[pieces] * 8
        + [pltpu.VMEM((FIELDS, ROWS, WIDE), F32)]
        + [edge] * 4
        + [grid] * 12
        + [
            pltpu.SemaphoreType.DMA((6 * CHUNKS * 8,)),
            pltpu.SemaphoreType.DMA((6 * CHUNKS * 8,)),
            pltpu.SemaphoreType.DMA((6 * CHUNKS,)),
            pltpu.SemaphoreType.DMA((4,)),
            pltpu.SemaphoreType.DMA((4,)),
        ],
        compiler_params=pltpu.CompilerParams(
            collective_id=0, has_side_effects=True, vmem_limit_bytes=58 * 2**20
        ),
    )(depth, flow_x, flow_y, floor, width, chan, rough, source, wet_tiles)


def solution(mesh):
    tiles = P(("row", "col"), None, None)
    block = P("row", "col")
    return jax.shard_map(
        body,
        mesh=mesh,
        in_specs=(tiles,) * 7 + (P(), block),
        out_specs=(block, block, block),
        check_vma=False,
    )
```

```python
import jax
import jax.numpy as jnp
from jax import lax
from jax.experimental import pallas as pl
from jax.experimental.pallas import tpu as pltpu
from jax.sharding import PartitionSpec as P

ITERS = 4
GRAV = 9.81
CELL = 5.0
STEP = 0.1
RMIN = 0.1

NX, NZ, NC = 4, 4, 8
DEVICES = NX * NZ * NC
SLOTS = 3
HALVES = 2
CHUNKS = SLOTS * HALVES
TILE = 256
BLOCK = 16
LANES = 128
FIRST = ("yxz", "xzy", "zyx") * 2
SECOND = ("zxy", "yzx", "xyz") * 2
PIECES = (CHUNKS, NX, NZ, NC, BLOCK, LANES)

PAD = 8
ROWS = TILE + 2 * PAD
COLS = SLOTS * TILE
WIDE = COLS + LANES
STRIPS = ROWS // 8
REACH = 4
FIELDS = 7
BLOCKS = WIDE // LANES
PARTS = 4
LOG2_E = 1.4426950408889634
WATER, FLOW_X, FLOW_Y, BED, WIDTH, CHAN, ROUGH = range(FIELDS)
F32 = jnp.float32


def to_code(values):
    return values.astype(jnp.int32).astype(jnp.int16)


def flow_code(flow):
    root = jnp.sqrt(jnp.sqrt(jnp.abs(flow) * 0.25))
    size = jnp.minimum(root * 32767.0 + 0.5, 32767.0).astype(jnp.int32)
    return jnp.where(flow < 0, -size, size).astype(jnp.int16)


def flow_value(code):
    return (code * code) * (code * jnp.abs(code)) * (4.0 / 32767.0**4)


def floor_code(floor):
    coarse = (floor * 65536.0).astype(jnp.int32)
    fine = -((floor * 16777216.0 + 0.5).astype(jnp.int32))
    return jnp.where(floor < 2.0**-9, fine, coarse).astype(jnp.int16)


def floor_value(code):
    return jnp.where(code < 0, code * -(2.0**-24), code * 2.0**-16)


def part(ref, chunk, axis, index):
    if axis == "x":
        return ref.at[chunk, index]
    if axis == "z":
        return ref.at[chunk, :, index]
    return ref.at[chunk, :, :, index]


def migrate_and_route(
    depth_hbm, fx_hbm, fy_hbm, floor_hbm, width_hbm, chan_hbm, rough_hbm, source_ref, wet_ref,
    water_hbm, fx_out_hbm, fy_out_hbm,
    depth_ref, fx_ref, fy_ref, floor_ref, width_ref, chan_ref, rough_ref,
    water_out, fx_out, fy_out,
    coded, first_a, first_b, middle, second_a, second_b, arrived,
    fields, sent_w, sent_e, got_e, got_w, level, volume, cap, inverse, flow_x, flow_y,
    bed_x, part_x, deep_x, drag_x, gate_x, bed_y, part_y, deep_y, drag_y, gate_y,
    send_sem, recv_sem, local_sem, rim_send, rim_recv, in_sem, out_sem,
):
    row = lax.axis_index("row")
    col = lax.axis_index("col")
    own_x = row // NZ
    own_z = row % NZ

    def place(x, z, c):
        return (x * NZ + z, c)

    west = (row, (col + NC - 1) % NC)
    east = (row, (col + 1) % NC)
    north = ((row + NX * NZ - 1) % (NX * NZ), col)
    south = ((row + 1) % (NX * NZ), col)

    loads = []
    for slot in range(SLOTS):
        pairs = (
            (depth_hbm, depth_ref), (fx_hbm, fx_ref), (fy_hbm, fy_ref), (floor_hbm, floor_ref),
            (width_hbm, width_ref), (chan_hbm, chan_ref), (rough_hbm, rough_ref),
        )
        group = [
            pltpu.make_async_copy(hbm.at[slot], ref.at[slot], in_sem.at[slot * FIELDS + n])
            for n, (hbm, ref) in enumerate(pairs)
        ]
        for copy in group:
            copy.start()
        loads.append(group)

    barrier = pltpu.get_barrier_semaphore()
    greeted = [place((own_x + d) % NX, own_z, col) for d in (1, 2, 3)]
    greeted += [place(own_x, (own_z + d) % NZ, col) for d in (1, 2, 3)]
    greeted += [place(own_x, own_z, (col + d) % NC) for d in range(1, NC)]
    greeted += [north, south]
    for device in greeted:
        pl.semaphore_signal(barrier, inc=1, device_id=device, device_id_type=pl.DeviceIdType.MESH)

    def encode(chunk):
        slot, half = chunk // HALVES, chunk % HALVES
        lanes = pl.ds(half * LANES, LANES)
        if half == 0:
            for copy in loads[slot]:
                copy.wait()

        def block(b, _):
            rows = pl.ds(pl.multiple_of(b * BLOCK, BLOCK), BLOCK)

            def put(plane, code):
                coded[chunk, b // NZ, b % NZ, plane] = code

            depth = depth_ref[slot, rows, lanes] * 16384.0
            high = depth.astype(jnp.int32)
            low = ((depth - high.astype(F32)) * 65536.0).astype(jnp.int32) - 32768
            put(0, high.astype(jnp.int16))
            put(1, low.astype(jnp.int16))
            put(2, flow_code(fx_ref[slot, rows, lanes]))
            put(3, flow_code(fy_ref[slot, rows, lanes]))
            put(4, floor_code(floor_ref[slot, rows, lanes].astype(F32)))
            put(5, to_code(width_ref[slot, rows, lanes].astype(F32) * 256.0))
            put(6, to_code(chan_ref[slot, rows, lanes].astype(F32) * 256.0))
            put(7, to_code(rough_ref[slot, rows, lanes].astype(F32) * 8192.0))
            return 0

        lax.fori_loop(0, TILE // BLOCK, block, 0)

    def decode(chunk):
        slot, half = chunk // HALVES, chunk % HALVES
        lanes = pl.ds(slot * TILE + half * LANES, LANES)
        wet = wet_ref[0, slot].astype(F32)

        def block(b, _):
            rows = pl.ds(pl.multiple_of(PAD + b * BLOCK, 8), BLOCK)

            def get(plane):
                return arrived[chunk, b // NZ, b % NZ, plane].astype(jnp.int32).astype(F32)

            chan = get(6) * (1.0 / 256.0)
            fields[WATER, rows, lanes] = get(0) * 2.0**-14 + (get(1) + 32768.0) * 2.0**-30
            fields[FLOW_X, rows, lanes] = flow_value(get(2))
            fields[FLOW_Y, rows, lanes] = flow_value(get(3))
            fields[BED, rows, lanes] = floor_value(get(4)) - chan
            fields[WIDTH, rows, lanes] = get(5) * (1.0 / 256.0)
            fields[CHAN, rows, lanes] = chan
            fields[ROUGH, rows, lanes] = get(7) * (1.0 / 8192.0) * wet - (1.0 - wet)
            return 0

        lax.fori_loop(0, TILE // BLOCK, block, 0)

    def copies(stage, chunk, axis, source, target):
        base = (stage * CHUNKS + chunk) * 8
        remote = []
        if axis == "y":
            me = col
            steps = [4, 5, 2, 3, 6, 7, 1]
            partners = [((col + (d // 2) * 2) % NC) // 2 * 2 + (col + d % 2) % 2 for d in steps]
            devices = [place(own_x, own_z, c) for c in partners]
        elif axis == "x":
            me = own_x
            partners = [(own_x + d) % NX for d in (2, 1, 3)]
            devices = [place(x, own_z, col) for x in partners]
        else:
            me = own_z
            partners = [(own_z + d) % NZ for d in (2, 1, 3)]
            devices = [place(own_x, z, col) for z in partners]
        for q, (partner, device) in enumerate(zip(partners, devices)):
            remote.append(
                pltpu.make_async_remote_copy(
                    src_ref=part(source, chunk, axis, partner),
                    dst_ref=part(target, chunk, axis, me),
                    send_sem=send_sem.at[base + q],
                    recv_sem=recv_sem.at[base + q],
                    device_id=device,
                    device_id_type=pl.DeviceIdType.MESH,
                )
            )
        local = pltpu.make_async_copy(
            part(source, chunk, axis, me),
            part(target, chunk, axis, me),
            local_sem.at[stage * CHUNKS + chunk],
        )
        return remote, local

    started = []

    def launch(stage, chunk, axis, source, target):
        remote, local = copies(stage, chunk, axis, source, target)
        for copy in remote:
            copy.start()
        local.start()
        started.extend(remote)
        return remote, local

    def landed(pair):
        remote, local = pair
        for copy in remote:
            copy.wait_recv()
        local.wait()

    encode(0)
    pl.semaphore_wait(barrier, len(greeted))
    flying = []
    for chunk in range(CHUNKS):
        if chunk > 0:
            encode(chunk)
        flying.append(launch(0, chunk, FIRST[chunk][0], coded, first_a))
    for stage, source, target in ((1, first_a, first_b), (2, first_b, middle)):
        for chunk in range(CHUNKS):
            landed(flying[chunk])
            flying[chunk] = launch(stage, chunk, FIRST[chunk][stage], source, target)
    for chunk in range(CHUNKS):
        landed(flying[chunk])

    for copy in started:
        copy.wait_send()
    started.clear()
    taken = middle.reshape(CHUNKS * DEVICES, BLOCK, LANES)
    ordered = coded.reshape(CHUNKS * DEVICES, BLOCK, LANES)
    for chunk in range(CHUNKS):
        slot, half = chunk // HALVES, chunk % HALVES

        def move(k, _):
            for u in range(8):
                d = k * 8 + u
                ordered[chunk * DEVICES + d] = taken[source_ref[slot * DEVICES + d] + half * DEVICES]
            return 0

        lax.fori_loop(0, DEVICES // 8, move, 0)
        flying[chunk] = launch(3, chunk, SECOND[chunk][0], coded, second_a)
    for stage, source, target in ((4, second_a, second_b), (5, second_b, arrived)):
        for chunk in range(CHUNKS):
            landed(flying[chunk])
            flying[chunk] = launch(stage, chunk, SECOND[chunk][stage - 3], source, target)
    for chunk in range(CHUNKS):
        landed(flying[chunk])
        decode(chunk)

    lane = lax.broadcasted_iota(jnp.int32, (8, LANES), 1)

    def pack(k, _):
        rows = pl.ds(pl.multiple_of(PAD + k * 8, 8), 8)
        left = jnp.zeros((8, LANES), F32)
        right = jnp.zeros((8, LANES), F32)
        for f in range(FIELDS):
            here = (lane >= REACH * f) & (lane < REACH * (f + 1))
            low = fields[f, rows, pl.ds(0, LANES)]
            high = fields[f, rows, pl.ds(COLS - LANES, LANES)]
            left = jnp.where(here, pltpu.roll(low, REACH * f, 1) if f else low, left)
            right = jnp.where(here, pltpu.roll(high, REACH * (f + 1), 1), right)
        out = pl.ds(pl.multiple_of(k * 8, 8), 8)
        sent_w[out, :] = left
        sent_e[out, :] = right
        return 0

    lax.fori_loop(0, TILE // 8, pack, 0)

    def rim(number, source, target, device):
        copy = pltpu.make_async_remote_copy(
            src_ref=source, dst_ref=target, send_sem=rim_send.at[number],
            recv_sem=rim_recv.at[number], device_id=device,
            device_id_type=pl.DeviceIdType.MESH,
        )
        copy.start()
        started.append(copy)
        return copy

    side = [rim(0, sent_w, got_e, west), rim(1, sent_e, got_w, east)]
    inner = pl.ds(0, COLS)
    outer = pl.ds(COLS, LANES)
    ends = [
        rim(2, fields.at[:, pl.ds(PAD, 8), inner], fields.at[:, pl.ds(PAD + TILE, 8), inner], north),
        rim(3, fields.at[:, pl.ds(TILE, 8), inner], fields.at[:, pl.ds(0, 8), inner], south),
    ]

    row_of = lax.broadcasted_iota(jnp.int32, (8, LANES), 0)
    bottom = row_of == 7
    top = row_of == 0
    right_end = lane == LANES - 1
    left_end = lane == 0

    def strip(k):
        return pl.ds(pl.multiple_of(k * 8, 8), 8)

    def block(c):
        return pl.ds((c % BLOCKS) * LANES, LANES)

    def faces(k, c):
        here = strip(k)
        there = strip(jnp.minimum(k + 1, STRIPS - 1))
        water = fields[WATER, here, block(c)]
        bed, width = fields[BED, here, block(c)], fields[WIDTH, here, block(c)]
        chan, rough = fields[CHAN, here, block(c)], fields[ROUGH, here, block(c)]
        level[here, block(c)] = bed + water
        volume[here, block(c)] = CELL * width * jnp.minimum(water, chan) + CELL * CELL * (
            jnp.maximum(water - chan, 0.0)
        )
        cap[here, block(c)] = CELL * width * chan
        inverse[here, block(c)] = 1.0 / (CELL * width) - 1.0 / (CELL * CELL)

        def to_east(f, v):
            after = pltpu.roll(fields[f, here, block(c + 1)], LANES - 1, 1)
            return jnp.where(right_end, after, pltpu.roll(v, LANES - 1, 1))

        def to_south(f, v):
            after = pltpu.roll(fields[f, there, block(c)], 7, 0)
            return jnp.where(bottom, after, pltpu.roll(v, 7, 0))

        for shift, bed_f, part_f, deep_f, drag_f, gate_f, f, flow in (
            (to_east, bed_x, part_x, deep_x, drag_x, gate_x, FLOW_X, flow_x),
            (to_south, bed_y, part_y, deep_y, drag_y, gate_y, FLOW_Y, flow_y),
        ):
            bed_f[here, block(c)] = jnp.maximum(bed, shift(BED, bed))
            part_f[here, block(c)] = 1.0 - jnp.minimum(width, shift(WIDTH, width)) * (1.0 / CELL)
            deep_f[here, block(c)] = jnp.minimum(chan, shift(CHAN, chan))
            rough_n = shift(ROUGH, rough)
            mean = 0.5 * (rough + rough_n)
            wet = jnp.minimum(rough, rough_n) > 0
            drag_f[here, block(c)] = jnp.where(wet, (GRAV * STEP / CELL) * mean * mean, 0.0)
            gate_f[here, block(c)] = jnp.where(wet, GRAV * STEP, 0.0)
            flow[here, block(c)] = jnp.where(wet, fields[f, here, block(c)], 0.0)

    def many_faces(start, stop, blocks):
        def one(k, _):
            for c in blocks:
                faces(k, c)
            return 0

        lax.fori_loop(start, stop, one, 0)

    many_faces(1, STRIPS - 2, range(BLOCKS - 2))

    for copy in side:
        copy.wait_recv()
    at_east = col == NC - 1
    at_west = col == 0

    def unpack(k, _):
        source = pl.ds(pl.multiple_of(k * 8, 8), 8)
        rows = pl.ds(pl.multiple_of(PAD + k * 8, 8), 8)
        from_e = got_e[source, :]
        from_w = got_w[source, :]
        for f in range(FIELDS):
            low = pltpu.roll(from_e, LANES - REACH * f, 1) if f else from_e
            high = pltpu.roll(from_w, LANES - REACH * (f + 1), 1)
            if f == ROUGH:
                low = jnp.where(at_east, -1.0, low)
                high = jnp.where(at_west, -1.0, high)
            fill = 1.0 if f in (WIDTH, CHAN) else (-1.0 if f == ROUGH else 0.0)
            mixed = jnp.where(lane < REACH, low, jnp.where(lane >= LANES - REACH, high, fill))
            fields[f, rows, outer] = mixed
        return 0

    lax.fori_loop(0, TILE // 8, unpack, 0)
    ends += [
        rim(4, fields.at[:, pl.ds(PAD, 8), outer], fields.at[:, pl.ds(PAD + TILE, 8), outer], north),
        rim(5, fields.at[:, pl.ds(TILE, 8), outer], fields.at[:, pl.ds(0, 8), outer], south),
    ]
    many_faces(1, STRIPS - 2, range(BLOCKS - 2, BLOCKS))
    for copy in ends:
        copy.wait_recv()
    first = fields[ROUGH, pl.ds(0, 8), :]
    fields[ROUGH, pl.ds(0, 8), :] = jnp.where(row == 0, -1.0, first)
    last = fields[ROUGH, pl.ds(PAD + TILE, 8), :]
    fields[ROUGH, pl.ds(PAD + TILE, 8), :] = jnp.where(row == NX * NZ - 1, -1.0, last)
    many_faces(0, 1, range(BLOCKS))
    many_faces(STRIPS - 2, STRIPS, range(BLOCKS))

    def face_flow(flow, surface, surface_n, bed_f, part_f, deep_f, drag_f, gate_f):
        crest = jnp.maximum(surface, surface_n) - bed_f
        depth = crest - part_f * jnp.minimum(crest, deep_f)
        power = jnp.exp2(jnp.log(jnp.maximum(depth, RMIN)) * (-7.0 / 3.0 * LOG2_E))
        below = 1.0 + drag_f * jnp.abs(flow) * power
        guess = pl.reciprocal(below, approx=True)
        guess = guess * (2.0 - below * guess)
        return (flow - gate_f * depth * (surface_n - surface)) * guess

    every = range(BLOCKS)
    for step in range(ITERS):
        final = step == ITERS - 1

        def sweep(k, carry):
            rolled, above = carry
            here = strip(k)
            there = strip(jnp.minimum(k + 1, STRIPS - 1))
            surface = [level[here, block(c)] for c in every]
            turned = [pltpu.roll(v, LANES - 1, 1) for v in surface]
            ahead = [pltpu.roll(level[there, block(c)], 7, 0) for c in every]
            new_x, new_y = [], []
            for c in every:
                b = block(c)
                surface_e = jnp.where(right_end, turned[(c + 1) % BLOCKS], turned[c])
                surface_s = jnp.where(bottom, ahead[c], rolled[c])
                new_x.append(
                    face_flow(
                        flow_x[here, b], surface[c], surface_e, bed_x[here, b], part_x[here, b],
                        deep_x[here, b], drag_x[here, b], gate_x[here, b],
                    )
                )
                new_y.append(
                    face_flow(
                        flow_y[here, b], surface[c], surface_s, bed_y[here, b], part_y[here, b],
                        deep_y[here, b], drag_y[here, b], gate_y[here, b],
                    )
                )
            sunk = [pltpu.roll(v, 1, 0) for v in new_y]
            passed = [pltpu.roll(v, 1, 1) for v in new_x]
            for c in every:
                b = block(c)
                if final and c == BLOCKS - 1:
                    continue
                from_w = jnp.where(left_end, passed[c - 1], passed[c])
                from_n = jnp.where(top, above[c], sunk[c])
                inflow = from_w - new_x[c] + from_n - new_y[c]
                held = jnp.maximum(volume[here, b] + STEP * inflow, 0.0)
                water = jnp.minimum(held, cap[here, b]) * inverse[here, b] + held * (
                    1.0 / (CELL * CELL)
                )
                if final:
                    out = strip(jnp.maximum(k - PAD // 8, 0))
                    water_out[out, b] = water
                    fx_out[out, b] = new_x[c]
                    fy_out[out, b] = new_y[c]
                else:
                    flow_x[here, b] = new_x[c]
                    flow_y[here, b] = new_y[c]
                    volume[here, b] = held
                    level[here, b] = fields[BED, here, b] + water
            return tuple(ahead), tuple(sunk)

        carry = (
            tuple(pltpu.roll(level[pl.ds(0, 8), block(c)], 7, 0) for c in every),
            tuple(jnp.zeros((8, LANES), F32) for c in every),
        )
        if not final:
            lax.fori_loop(0, STRIPS, sweep, carry)

    stores = []
    begin = 0
    for piece in range(PARTS):
        end = PAD // 8 + (piece + 1) * (TILE // 8 // PARTS)
        carry = lax.fori_loop(begin, end, sweep, carry)
        begin = end
        rows = pl.ds(piece * (TILE // PARTS), TILE // PARTS)
        for n, (ref, hbm) in enumerate(
            ((water_out, water_hbm), (fx_out, fx_out_hbm), (fy_out, fy_out_hbm))
        ):
            copy = pltpu.make_async_copy(ref.at[rows], hbm.at[rows], out_sem.at[piece * 3 + n])
            copy.start()
            stores.append(copy)
    for copy in stores:
        copy.wait()
    for copy in started:
        copy.wait_send()


def body(depth, flow_x, flow_y, floor, width, chan, rough, route, wet_tiles):
    target = (route[:, 0] * NC + route[:, 1]) * SLOTS + route[:, 2]
    old = jnp.arange(DEVICES * SLOTS, dtype=jnp.int32)
    where_held = (old % SLOTS) * (HALVES * DEVICES) + old // SLOTS
    slot_major = (old % DEVICES) * SLOTS + old // DEVICES
    source = jnp.sum(
        jnp.where(slot_major[:, None] == target[None, :], where_held[None, :], 0), axis=1
    )
    whole = pl.BlockSpec(memory_space=pl.ANY)
    smem = pl.BlockSpec(memory_space=pltpu.SMEM)
    pieces = pltpu.VMEM(PIECES, jnp.int16)
    grid = pltpu.VMEM((ROWS, WIDE), F32)
    edge = pltpu.VMEM((TILE, LANES), F32)
    out = jax.ShapeDtypeStruct((TILE, COLS), F32)
    operands = (depth, flow_x, flow_y, floor, width, chan, rough)
    return pl.pallas_call(
        migrate_and_route,
        out_shape=(out, out, out),
        in_specs=[whole] * 7 + [smem] * 2,
        out_specs=(whole, whole, whole),
        scratch_shapes=[pltpu.VMEM(a.shape, a.dtype) for a in operands]
        + [pltpu.VMEM((TILE, COLS), F32)] * 3
        + [pieces] * 7
        + [pltpu.VMEM((FIELDS, ROWS, WIDE), F32)]
        + [edge] * 4
        + [grid] * 16
        + [
            pltpu.SemaphoreType.DMA((6 * CHUNKS * 8,)),
            pltpu.SemaphoreType.DMA((6 * CHUNKS * 8,)),
            pltpu.SemaphoreType.DMA((6 * CHUNKS,)),
            pltpu.SemaphoreType.DMA((6,)),
            pltpu.SemaphoreType.DMA((6,)),
            pltpu.SemaphoreType.DMA((SLOTS * FIELDS,)),
            pltpu.SemaphoreType.DMA((PARTS * 3,)),
        ],
        compiler_params=pltpu.CompilerParams(
            collective_id=0, has_side_effects=True, vmem_limit_bytes=58 * 2**20
        ),
    )(*operands, source, wet_tiles)


def solution(mesh):
    tiles = P(("row", "col"), None, None)
    block = P("row", "col")
    return jax.shard_map(
        body,
        mesh=mesh,
        in_specs=(tiles,) * 7 + (P(), block),
        out_specs=(block, block, block),
        check_vma=False,
    )
```

```python
import jax
import jax.numpy as jnp
from jax import lax
from jax.experimental import pallas as pl
from jax.experimental.pallas import tpu as pltpu
from jax.sharding import PartitionSpec as P

ITERS = 4
GRAV = 9.81
CELL = 5.0
STEP = 0.1
RMIN = 0.1

NX, NZ, NC = 4, 4, 8
DEVICES = NX * NZ * NC
SLOTS = 3
HALVES = 2
CHUNKS = SLOTS * HALVES
TILE = 256
BLOCK = 16
LANES = 128
FIRST = ("yxz", "xzy", "zyx") * 2
SECOND = ("zxy", "yzx", "xyz") * 2
PIECES = (CHUNKS, NX, NZ, NC, BLOCK, LANES)

PAD = 8
HIGH = 72
STRIPS = -(-(TILE + 2 * PAD) // HIGH)
ROWS = STRIPS * HIGH
EDGE = 1
SAFE = (TILE + PAD - 1) // HIGH
COLS = SLOTS * TILE
WIDE = COLS + LANES
REACH = 4
FIELDS = 7
BLOCKS = WIDE // LANES
PARTS = 4
TALL = 64
LOG2_E = 1.4426950408889634
WATER, FLOW_X, FLOW_Y, BED, WIDTH, CHAN, ROUGH = range(FIELDS)
F32 = jnp.float32


def to_code(values):
    return values.astype(jnp.int32).astype(jnp.int16)


def flow_code(flow):
    root = jnp.sqrt(jnp.sqrt(jnp.abs(flow) * 0.25))
    size = jnp.minimum(root * 32767.0 + 0.5, 32767.0).astype(jnp.int32)
    return jnp.where(flow < 0, -size, size).astype(jnp.int16)


def flow_value(code):
    return (code * code) * (code * jnp.abs(code)) * (4.0 / 32767.0**4)


def floor_code(floor):
    coarse = (floor * 65536.0).astype(jnp.int32)
    fine = -((floor * 16777216.0 + 0.5).astype(jnp.int32))
    return jnp.where(floor < 2.0**-9, fine, coarse).astype(jnp.int16)


def floor_value(code):
    return jnp.where(code < 0, code * -(2.0**-24), code * 2.0**-16)


def part(ref, chunk, axis, index):
    if axis == "x":
        return ref.at[chunk, index]
    if axis == "z":
        return ref.at[chunk, :, index]
    return ref.at[chunk, :, :, index]


def migrate_and_route(
    depth_hbm, fx_hbm, fy_hbm, floor_hbm, width_hbm, chan_hbm, rough_hbm, source_ref, wet_ref,
    water_hbm, fx_out_hbm, fy_out_hbm,
    depth_ref, fx_ref, fy_ref, floor_ref, width_ref, chan_ref, rough_ref,
    water_out, fx_out, fy_out,
    coded, first_a, first_b, middle, second_a, second_b, arrived,
    fields, sent_w, sent_e, got_e, got_w, level, volume, cap, inverse, flow_x, flow_y,
    bed_x, part_x, deep_x, drag_x, gate_x, bed_y, part_y, deep_y, drag_y, gate_y,
    send_sem, recv_sem, local_sem, rim_send, rim_recv, in_sem, out_sem,
):
    row = lax.axis_index("row")
    col = lax.axis_index("col")
    own_x = row // NZ
    own_z = row % NZ

    def place(x, z, c):
        return (x * NZ + z, c)

    west = (row, (col + NC - 1) % NC)
    east = (row, (col + 1) % NC)
    north = ((row + NX * NZ - 1) % (NX * NZ), col)
    south = ((row + 1) % (NX * NZ), col)

    loads = []
    for slot in range(SLOTS):
        pairs = (
            (depth_hbm, depth_ref), (fx_hbm, fx_ref), (fy_hbm, fy_ref), (floor_hbm, floor_ref),
            (width_hbm, width_ref), (chan_hbm, chan_ref), (rough_hbm, rough_ref),
        )
        group = [
            pltpu.make_async_copy(hbm.at[slot], ref.at[slot], in_sem.at[slot * FIELDS + n])
            for n, (hbm, ref) in enumerate(pairs)
        ]
        for copy in group:
            copy.start()
        loads.append(group)

    barrier = pltpu.get_barrier_semaphore()
    greeted = [place((own_x + d) % NX, own_z, col) for d in (1, 2, 3)]
    greeted += [place(own_x, (own_z + d) % NZ, col) for d in (1, 2, 3)]
    greeted += [place(own_x, own_z, (col + d) % NC) for d in range(1, NC)]
    greeted += [north, south]
    for device in greeted:
        pl.semaphore_signal(barrier, inc=1, device_id=device, device_id_type=pl.DeviceIdType.MESH)

    def encode(chunk):
        slot, half = chunk // HALVES, chunk % HALVES
        lanes = pl.ds(half * LANES, LANES)
        if half == 0:
            for copy in loads[slot]:
                copy.wait()

        def block(b, _):
            rows = pl.ds(pl.multiple_of(b * BLOCK, BLOCK), BLOCK)

            def put(plane, code):
                coded[chunk, b // NZ, b % NZ, plane] = code

            depth = depth_ref[slot, rows, lanes] * 16384.0
            high = depth.astype(jnp.int32)
            low = ((depth - high.astype(F32)) * 65536.0).astype(jnp.int32) - 32768
            put(0, high.astype(jnp.int16))
            put(1, low.astype(jnp.int16))
            put(2, flow_code(fx_ref[slot, rows, lanes]))
            put(3, flow_code(fy_ref[slot, rows, lanes]))
            put(4, floor_code(floor_ref[slot, rows, lanes].astype(F32)))
            put(5, to_code(width_ref[slot, rows, lanes].astype(F32) * 256.0))
            put(6, to_code(chan_ref[slot, rows, lanes].astype(F32) * 256.0))
            put(7, to_code(rough_ref[slot, rows, lanes].astype(F32) * 8192.0))
            return 0

        lax.fori_loop(0, TILE // BLOCK, block, 0)

    def decode(chunk):
        slot, half = chunk // HALVES, chunk % HALVES
        lanes = pl.ds(slot * TILE + half * LANES, LANES)
        wet = wet_ref[0, slot].astype(F32)

        def block(b, _):
            rows = pl.ds(pl.multiple_of(PAD + b * BLOCK, 8), BLOCK)

            def get(plane):
                return arrived[chunk, b // NZ, b % NZ, plane].astype(jnp.int32).astype(F32)

            chan = get(6) * (1.0 / 256.0)
            fields[WATER, rows, lanes] = get(0) * 2.0**-14 + (get(1) + 32768.0) * 2.0**-30
            fields[FLOW_X, rows, lanes] = flow_value(get(2))
            fields[FLOW_Y, rows, lanes] = flow_value(get(3))
            fields[BED, rows, lanes] = floor_value(get(4)) - chan
            fields[WIDTH, rows, lanes] = get(5) * (1.0 / 256.0)
            fields[CHAN, rows, lanes] = chan
            fields[ROUGH, rows, lanes] = get(7) * (1.0 / 8192.0) * wet - (1.0 - wet)
            return 0

        lax.fori_loop(0, TILE // BLOCK, block, 0)

    def copies(stage, chunk, axis, source, target):
        base = (stage * CHUNKS + chunk) * 8
        remote = []
        if axis == "y":
            me = col
            steps = [4, 5, 2, 3, 6, 7, 1]
            partners = [((col + (d // 2) * 2) % NC) // 2 * 2 + (col + d % 2) % 2 for d in steps]
            devices = [place(own_x, own_z, c) for c in partners]
        elif axis == "x":
            me = own_x
            partners = [(own_x + d) % NX for d in (2, 1, 3)]
            devices = [place(x, own_z, col) for x in partners]
        else:
            me = own_z
            partners = [(own_z + d) % NZ for d in (2, 1, 3)]
            devices = [place(own_x, z, col) for z in partners]
        for q, (partner, device) in enumerate(zip(partners, devices)):
            remote.append(
                pltpu.make_async_remote_copy(
                    src_ref=part(source, chunk, axis, partner),
                    dst_ref=part(target, chunk, axis, me),
                    send_sem=send_sem.at[base + q],
                    recv_sem=recv_sem.at[base + q],
                    device_id=device,
                    device_id_type=pl.DeviceIdType.MESH,
                )
            )
        local = pltpu.make_async_copy(
            part(source, chunk, axis, me),
            part(target, chunk, axis, me),
            local_sem.at[stage * CHUNKS + chunk],
        )
        return remote, local

    started = []

    def launch(stage, chunk, axis, source, target):
        remote, local = copies(stage, chunk, axis, source, target)
        for copy in remote:
            copy.start()
        local.start()
        started.extend(remote)
        return remote, local

    def landed(pair):
        remote, local = pair
        for copy in remote:
            copy.wait_recv()
        local.wait()

    encode(0)
    pl.semaphore_wait(barrier, len(greeted))
    flying = []
    for chunk in range(CHUNKS):
        if chunk > 0:
            encode(chunk)
        flying.append(launch(0, chunk, FIRST[chunk][0], coded, first_a))
    for stage, source, target in ((1, first_a, first_b), (2, first_b, middle)):
        for chunk in range(CHUNKS):
            landed(flying[chunk])
            flying[chunk] = launch(stage, chunk, FIRST[chunk][stage], source, target)
    for chunk in range(CHUNKS):
        landed(flying[chunk])

    for copy in started:
        copy.wait_send()
    started.clear()
    taken = middle.reshape(CHUNKS * DEVICES, BLOCK, LANES)
    ordered = coded.reshape(CHUNKS * DEVICES, BLOCK, LANES)
    for chunk in range(CHUNKS):
        slot, half = chunk // HALVES, chunk % HALVES

        def move(k, _):
            for u in range(8):
                d = k * 8 + u
                ordered[chunk * DEVICES + d] = taken[source_ref[slot * DEVICES + d] + half * DEVICES]
            return 0

        lax.fori_loop(0, DEVICES // 8, move, 0)
        flying[chunk] = launch(3, chunk, SECOND[chunk][0], coded, second_a)
    for stage, source, target in ((4, second_a, second_b), (5, second_b, arrived)):
        for chunk in range(CHUNKS):
            landed(flying[chunk])
            flying[chunk] = launch(stage, chunk, SECOND[chunk][stage - 3], source, target)
    for chunk in range(CHUNKS):
        landed(flying[chunk])
        decode(chunk)

    lane = lax.broadcasted_iota(jnp.int32, (TALL, LANES), 1)

    def pack(k, _):
        rows = pl.ds(pl.multiple_of(PAD + k * TALL, 8), TALL)
        left = jnp.zeros((TALL, LANES), F32)
        right = jnp.zeros((TALL, LANES), F32)
        for f in range(FIELDS):
            here = (lane >= REACH * f) & (lane < REACH * (f + 1))
            low = fields[f, rows, pl.ds(0, LANES)]
            high = fields[f, rows, pl.ds(COLS - LANES, LANES)]
            left = jnp.where(here, pltpu.roll(low, REACH * f, 1) if f else low, left)
            right = jnp.where(here, pltpu.roll(high, REACH * (f + 1), 1), right)
        out = pl.ds(pl.multiple_of(k * TALL, 8), TALL)
        sent_w[out, :] = left
        sent_e[out, :] = right
        return 0

    lax.fori_loop(0, TILE // TALL, pack, 0)

    def rim(number, source, target, device):
        copy = pltpu.make_async_remote_copy(
            src_ref=source, dst_ref=target, send_sem=rim_send.at[number],
            recv_sem=rim_recv.at[number], device_id=device,
            device_id_type=pl.DeviceIdType.MESH,
        )
        copy.start()
        started.append(copy)
        return copy

    side = [rim(0, sent_w, got_e, west), rim(1, sent_e, got_w, east)]
    inner = pl.ds(0, COLS)
    outer = pl.ds(COLS, LANES)
    ends = [
        rim(2, fields.at[:, pl.ds(PAD, 8), inner], fields.at[:, pl.ds(PAD + TILE, 8), inner], north),
        rim(3, fields.at[:, pl.ds(TILE, 8), inner], fields.at[:, pl.ds(0, 8), inner], south),
    ]

    row_of = lax.broadcasted_iota(jnp.int32, (8, LANES), 0)
    bottom = row_of == 7
    top = row_of == 0
    lanes_high = lax.broadcasted_iota(jnp.int32, (HIGH, LANES), 1)
    right_end = lanes_high == LANES - 1
    left_end = lanes_high == 0

    def strip(k):
        return pl.ds(pl.multiple_of(k * HIGH, 8), HIGH)

    def below_strip(k):
        return pl.ds(pl.multiple_of(jnp.minimum((k + 1) * HIGH, ROWS - 8), 8), 8)

    def from_south(values, after):
        moved = pltpu.roll(values, HIGH - 1, 0)
        end = jnp.where(bottom, pltpu.roll(after, 7, 0), moved[HIGH - 8 :])
        return jnp.concatenate([moved[: HIGH - 8], end], 0) if HIGH > 8 else end

    def from_north(values, before):
        moved = pltpu.roll(values, 1, 0)
        start = jnp.where(top, before, moved[:8])
        return (jnp.concatenate([start, moved[8:]], 0) if HIGH > 8 else start), moved[:8]

    def block(c):
        return pl.ds((c % BLOCKS) * LANES, LANES)

    def faces(k, c):
        here = strip(k)
        there = below_strip(k)
        water = fields[WATER, here, block(c)]
        bed, width = fields[BED, here, block(c)], fields[WIDTH, here, block(c)]
        chan, rough = fields[CHAN, here, block(c)], fields[ROUGH, here, block(c)]
        level[here, block(c)] = bed + water
        volume[here, block(c)] = CELL * width * jnp.minimum(water, chan) + CELL * CELL * (
            jnp.maximum(water - chan, 0.0)
        )
        cap[here, block(c)] = CELL * width * chan
        inverse[here, block(c)] = 1.0 / (CELL * width) - 1.0 / (CELL * CELL)

        def to_east(f, v):
            after = pltpu.roll(fields[f, here, block(c + 1)], LANES - 1, 1)
            return jnp.where(right_end, after, pltpu.roll(v, LANES - 1, 1))

        def to_south(f, v):
            return from_south(v, fields[f, there, block(c)])

        for shift, bed_f, part_f, deep_f, drag_f, gate_f, f, flow in (
            (to_east, bed_x, part_x, deep_x, drag_x, gate_x, FLOW_X, flow_x),
            (to_south, bed_y, part_y, deep_y, drag_y, gate_y, FLOW_Y, flow_y),
        ):
            bed_f[here, block(c)] = jnp.maximum(bed, shift(BED, bed))
            part_f[here, block(c)] = 1.0 - jnp.minimum(width, shift(WIDTH, width)) * (1.0 / CELL)
            deep_f[here, block(c)] = jnp.minimum(chan, shift(CHAN, chan))
            rough_n = shift(ROUGH, rough)
            mean = 0.5 * (rough + rough_n)
            wet = jnp.minimum(rough, rough_n) > 0
            drag_f[here, block(c)] = jnp.where(wet, (GRAV * STEP / CELL) * mean * mean, 0.0)
            gate_f[here, block(c)] = jnp.where(wet, GRAV * STEP, 0.0)
            flow[here, block(c)] = jnp.where(wet, fields[f, here, block(c)], 0.0)

    def many_faces(start, stop, blocks):
        def one(k, _):
            for c in blocks:
                faces(k, c)
            return 0

        lax.fori_loop(start, stop, one, 0)

    many_faces(EDGE, SAFE, range(BLOCKS - 2))

    for copy in side:
        copy.wait_recv()
    at_east = col == NC - 1
    at_west = col == 0

    def unpack(k, _):
        source = pl.ds(pl.multiple_of(k * TALL, 8), TALL)
        rows = pl.ds(pl.multiple_of(PAD + k * TALL, 8), TALL)
        from_e = got_e[source, :]
        from_w = got_w[source, :]
        for f in range(FIELDS):
            low = pltpu.roll(from_e, LANES - REACH * f, 1) if f else from_e
            high = pltpu.roll(from_w, LANES - REACH * (f + 1), 1)
            if f == ROUGH:
                low = jnp.where(at_east, -1.0, low)
                high = jnp.where(at_west, -1.0, high)
            fill = 1.0 if f in (WIDTH, CHAN) else (-1.0 if f == ROUGH else 0.0)
            mixed = jnp.where(lane < REACH, low, jnp.where(lane >= LANES - REACH, high, fill))
            fields[f, rows, outer] = mixed
        return 0

    lax.fori_loop(0, TILE // TALL, unpack, 0)
    ends += [
        rim(4, fields.at[:, pl.ds(PAD, 8), outer], fields.at[:, pl.ds(PAD + TILE, 8), outer], north),
        rim(5, fields.at[:, pl.ds(TILE, 8), outer], fields.at[:, pl.ds(0, 8), outer], south),
    ]
    many_faces(EDGE, SAFE, range(BLOCKS - 2, BLOCKS))
    for copy in ends:
        copy.wait_recv()
    first = fields[ROUGH, pl.ds(0, 8), :]
    fields[ROUGH, pl.ds(0, 8), :] = jnp.where(row == 0, -1.0, first)
    last = fields[ROUGH, pl.ds(PAD + TILE, 8), :]
    fields[ROUGH, pl.ds(PAD + TILE, 8), :] = jnp.where(row == NX * NZ - 1, -1.0, last)
    many_faces(0, EDGE, range(BLOCKS))
    many_faces(SAFE, STRIPS, range(BLOCKS))

    def face_flow(flow, surface, surface_n, bed_f, part_f, deep_f, drag_f, gate_f):
        crest = jnp.maximum(surface, surface_n) - bed_f
        depth = crest - part_f * jnp.minimum(crest, deep_f)
        power = jnp.exp2(jnp.log(jnp.maximum(depth, RMIN)) * (-7.0 / 3.0 * LOG2_E))
        below = 1.0 + drag_f * jnp.abs(flow) * power
        guess = pl.reciprocal(below, approx=True)
        guess = guess * (2.0 - below * guess)
        return (flow - gate_f * depth * (surface_n - surface)) * guess

    every = range(BLOCKS)
    for step in range(ITERS):
        final = step == ITERS - 1

        def sweep(k, above):
            here = strip(k)
            there = below_strip(k)
            surface = [level[here, block(c)] for c in every]
            turned = [pltpu.roll(v, LANES - 1, 1) for v in surface]
            new_x = []
            for c in every:
                b = block(c)
                surface_e = jnp.where(right_end, turned[(c + 1) % BLOCKS], turned[c])
                new_x.append(
                    face_flow(
                        flow_x[here, b], surface[c], surface_e, bed_x[here, b], part_x[here, b],
                        deep_x[here, b], drag_x[here, b], gate_x[here, b],
                    )
                )
            passed = [pltpu.roll(v, 1, 1) for v in new_x]
            sunk = []
            for c in every:
                b = block(c)
                surface_s = from_south(surface[c], level[there, b])
                new_y = face_flow(
                    flow_y[here, b], surface[c], surface_s, bed_y[here, b], part_y[here, b],
                    deep_y[here, b], drag_y[here, b], gate_y[here, b],
                )
                from_n, end = from_north(new_y, above[c])
                sunk.append(end)
                from_w = jnp.where(left_end, passed[c - 1], passed[c])
                inflow = from_w - new_x[c] + from_n - new_y
                held = jnp.maximum(volume[here, b] + STEP * inflow, 0.0)
                water = jnp.minimum(held, cap[here, b]) * inverse[here, b] + held * (
                    1.0 / (CELL * CELL)
                )
                if not final:
                    flow_x[here, b] = new_x[c]
                    flow_y[here, b] = new_y
                    volume[here, b] = held
                    level[here, b] = fields[BED, here, b] + water
                elif c < BLOCKS - 1:
                    water_out[here, b] = water
                    fx_out[here, b] = new_x[c]
                    fy_out[here, b] = new_y
            return tuple(sunk)

        carry = tuple(jnp.zeros((8, LANES), F32) for c in every)
        if not final:
            lax.fori_loop(0, STRIPS, sweep, carry)

    stores = []
    begin = 0
    sent = 0
    for piece in range(PARTS):
        end = -(-(PAD + (piece + 1) * (TILE // PARTS)) // HIGH)
        carry = lax.fori_loop(begin, end, sweep, carry)
        begin = end
        until = min(TILE, end * HIGH - PAD) if piece < PARTS - 1 else TILE
        size = until - sent
        for n, (ref, hbm) in enumerate(
            ((water_out, water_hbm), (fx_out, fx_out_hbm), (fy_out, fy_out_hbm))
        ):
            copy = pltpu.make_async_copy(
                ref.at[pl.ds(PAD + sent, size)], hbm.at[pl.ds(sent, size)], out_sem.at[piece * 3 + n]
            )
            copy.start()
            stores.append(copy)
        sent = until
    for copy in stores:
        copy.wait()
    for copy in started:
        copy.wait_send()


def body(depth, flow_x, flow_y, floor, width, chan, rough, route, wet_tiles):
    target = (route[:, 0] * NC + route[:, 1]) * SLOTS + route[:, 2]
    old = jnp.arange(DEVICES * SLOTS, dtype=jnp.int32)
    where_held = (old % SLOTS) * (HALVES * DEVICES) + old // SLOTS
    slot_major = (old % DEVICES) * SLOTS + old // DEVICES
    source = jnp.sum(
        jnp.where(slot_major[:, None] == target[None, :], where_held[None, :], 0), axis=1
    )
    whole = pl.BlockSpec(memory_space=pl.ANY)
    smem = pl.BlockSpec(memory_space=pltpu.SMEM)
    pieces = pltpu.VMEM(PIECES, jnp.int16)
    grid = pltpu.VMEM((ROWS, WIDE), F32)
    edge = pltpu.VMEM((TILE, LANES), F32)
    out = jax.ShapeDtypeStruct((TILE, COLS), F32)
    operands = (depth, flow_x, flow_y, floor, width, chan, rough)
    return pl.pallas_call(
        migrate_and_route,
        out_shape=(out, out, out),
        in_specs=[whole] * 7 + [smem] * 2,
        out_specs=(whole, whole, whole),
        scratch_shapes=[pltpu.VMEM(a.shape, a.dtype) for a in operands]
        + [pltpu.VMEM((ROWS, COLS), F32)] * 3
        + [pieces] * 7
        + [pltpu.VMEM((FIELDS, ROWS, WIDE), F32)]
        + [edge] * 4
        + [grid] * 16
        + [
            pltpu.SemaphoreType.DMA((6 * CHUNKS * 8,)),
            pltpu.SemaphoreType.DMA((6 * CHUNKS * 8,)),
            pltpu.SemaphoreType.DMA((6 * CHUNKS,)),
            pltpu.SemaphoreType.DMA((6,)),
            pltpu.SemaphoreType.DMA((6,)),
            pltpu.SemaphoreType.DMA((SLOTS * FIELDS,)),
            pltpu.SemaphoreType.DMA((PARTS * 3,)),
        ],
        compiler_params=pltpu.CompilerParams(
            collective_id=0, has_side_effects=True, vmem_limit_bytes=58 * 2**20
        ),
    )(*operands, source, wet_tiles)


def solution(mesh):
    tiles = P(("row", "col"), None, None)
    block = P("row", "col")
    return jax.shard_map(
        body,
        mesh=mesh,
        in_specs=(tiles,) * 7 + (P(), block),
        out_specs=(block, block, block),
        check_vma=False,
    )
```

```python
import jax
import jax.numpy as jnp
from jax import lax
from jax.experimental import pallas as pl
from jax.experimental.pallas import tpu as pltpu
from jax.sharding import PartitionSpec as P

ITERS = 4
GRAV = 9.81
CELL = 5.0
STEP = 0.1
RMIN = 0.1

NX, NZ, NC = 4, 4, 8
DEVICES = NX * NZ * NC
SLOTS = 3
HALVES = 2
CHUNKS = SLOTS * HALVES
TILE = 256
BLOCK = 16
LANES = 128
FIRST = ("yxz", "xzy", "zyx") * 2
SECOND = ("zxy", "yzx", "xyz") * 2
PIECES = (CHUNKS, NX, NZ, NC, BLOCK, LANES)

PAD = 8
HIGH = 72
STRIPS = -(-(TILE + 2 * PAD) // HIGH)
ROWS = STRIPS * HIGH
COLS = SLOTS * TILE
WIDE = COLS + LANES
REACH = 4
FIELDS = 7
BLOCKS = WIDE // LANES
PARTS = 4
TALL = 64
FACE_HIGH = 32
PAIRS = (FIELDS + 1) // 2
LOG2_E = 1.4426950408889634
WATER, FLOW_X, FLOW_Y, BED, WIDTH, CHAN, ROUGH = range(FIELDS)
F32 = jnp.float32


def to_code(values):
    return values.astype(jnp.int32).astype(jnp.int16)


def flow_code(flow):
    root = jnp.sqrt(jnp.sqrt(jnp.abs(flow) * 0.25))
    size = jnp.minimum(root * 32767.0 + 0.5, 32767.0).astype(jnp.int32)
    return jnp.where(flow < 0, -size, size).astype(jnp.int16)


def flow_value(code):
    return (code * code) * (code * jnp.abs(code)) * (4.0 / 32767.0**4)


def floor_code(floor):
    coarse = (floor * 65536.0).astype(jnp.int32)
    fine = -((floor * 16777216.0 + 0.5).astype(jnp.int32))
    return jnp.where(floor < 2.0**-9, fine, coarse).astype(jnp.int16)


def floor_value(code):
    return jnp.where(code < 0, code * -(2.0**-24), code * 2.0**-16)


def part(ref, chunk, axis, index):
    if axis == "x":
        return ref.at[chunk, index]
    if axis == "z":
        return ref.at[chunk, :, index]
    return ref.at[chunk, :, :, index]


def migrate_and_route(
    depth_hbm, fx_hbm, fy_hbm, floor_hbm, width_hbm, chan_hbm, rough_hbm, source_ref, wet_ref,
    water_hbm, fx_out_hbm, fy_out_hbm,
    depth_ref, fx_ref, fy_ref, floor_ref, width_ref, chan_ref, rough_ref,
    water_out, fx_out, fy_out,
    coded, first_a, first_b, middle, second_a, second_b, arrived,
    fields, sent_w, sent_e, got_e, got_w, sent_n, sent_s, got_n, got_s, level, volume, cap, inverse, flow_x, flow_y,
    bed_x, part_x, deep_x, drag_x, gate_x, bed_y, part_y, deep_y, drag_y, gate_y,
    send_sem, recv_sem, local_sem, rim_send, rim_recv, in_sem, out_sem,
):
    row = lax.axis_index("row")
    col = lax.axis_index("col")
    own_x = row // NZ
    own_z = row % NZ

    def place(x, z, c):
        return (x * NZ + z, c)

    west = (row, (col + NC - 1) % NC)
    east = (row, (col + 1) % NC)
    north = ((row + NX * NZ - 1) % (NX * NZ), col)
    south = ((row + 1) % (NX * NZ), col)

    corners = [(north[0], west[1]), (north[0], east[1]), (south[0], west[1]), (south[0], east[1])]

    loads = []
    for slot in range(SLOTS):
        pairs = (
            (depth_hbm, depth_ref), (fx_hbm, fx_ref), (fy_hbm, fy_ref), (floor_hbm, floor_ref),
            (width_hbm, width_ref), (chan_hbm, chan_ref), (rough_hbm, rough_ref),
        )
        group = [
            pltpu.make_async_copy(hbm.at[slot], ref.at[slot], in_sem.at[slot * FIELDS + n])
            for n, (hbm, ref) in enumerate(pairs)
        ]
        for copy in group:
            copy.start()
        loads.append(group)

    barrier = pltpu.get_barrier_semaphore()
    greeted = [place((own_x + d) % NX, own_z, col) for d in (1, 2, 3)]
    greeted += [place(own_x, (own_z + d) % NZ, col) for d in (1, 2, 3)]
    greeted += [place(own_x, own_z, (col + d) % NC) for d in range(1, NC)]
    greeted += [north, south] + corners
    for device in greeted:
        pl.semaphore_signal(barrier, inc=1, device_id=device, device_id_type=pl.DeviceIdType.MESH)

    def encode(chunk):
        slot, half = chunk // HALVES, chunk % HALVES
        lanes = pl.ds(half * LANES, LANES)
        if half == 0:
            for copy in loads[slot]:
                copy.wait()

        def block(b, _):
            rows = pl.ds(pl.multiple_of(b * BLOCK, BLOCK), BLOCK)

            def put(plane, code):
                coded[chunk, b // NZ, b % NZ, plane] = code

            depth = depth_ref[slot, rows, lanes] * 16384.0
            high = depth.astype(jnp.int32)
            low = ((depth - high.astype(F32)) * 65536.0).astype(jnp.int32) - 32768
            put(0, high.astype(jnp.int16))
            put(1, low.astype(jnp.int16))
            put(2, flow_code(fx_ref[slot, rows, lanes]))
            put(3, flow_code(fy_ref[slot, rows, lanes]))
            put(4, floor_code(floor_ref[slot, rows, lanes].astype(F32)))
            put(5, to_code(width_ref[slot, rows, lanes].astype(F32) * 256.0))
            put(6, to_code(chan_ref[slot, rows, lanes].astype(F32) * 256.0))
            put(7, to_code(rough_ref[slot, rows, lanes].astype(F32) * 8192.0))
            return 0

        lax.fori_loop(0, TILE // BLOCK, block, 0)

    def decode(chunk):
        slot, half = chunk // HALVES, chunk % HALVES
        lanes = pl.ds(slot * TILE + half * LANES, LANES)
        wet = wet_ref[0, slot].astype(F32)

        def block(b, _):
            rows = pl.ds(pl.multiple_of(PAD + b * BLOCK, 8), BLOCK)

            def get(plane):
                return arrived[chunk, b // NZ, b % NZ, plane].astype(jnp.int32).astype(F32)

            chan = get(6) * (1.0 / 256.0)
            fields[WATER, rows, lanes] = get(0) * 2.0**-14 + (get(1) + 32768.0) * 2.0**-30
            fields[FLOW_X, rows, lanes] = flow_value(get(2))
            fields[FLOW_Y, rows, lanes] = flow_value(get(3))
            fields[BED, rows, lanes] = floor_value(get(4)) - chan
            fields[WIDTH, rows, lanes] = get(5) * (1.0 / 256.0)
            fields[CHAN, rows, lanes] = chan
            fields[ROUGH, rows, lanes] = get(7) * (1.0 / 8192.0) * wet - (1.0 - wet)
            return 0

        lax.fori_loop(0, TILE // BLOCK, block, 0)

    def copies(stage, chunk, axis, source, target):
        base = (stage * CHUNKS + chunk) * 8
        remote = []
        if axis == "y":
            me = col
            steps = [4, 5, 2, 3, 6, 7, 1]
            partners = [((col + (d // 2) * 2) % NC) // 2 * 2 + (col + d % 2) % 2 for d in steps]
            devices = [place(own_x, own_z, c) for c in partners]
        elif axis == "x":
            me = own_x
            partners = [(own_x + d) % NX for d in (2, 1, 3)]
            devices = [place(x, own_z, col) for x in partners]
        else:
            me = own_z
            partners = [(own_z + d) % NZ for d in (2, 1, 3)]
            devices = [place(own_x, z, col) for z in partners]
        for q, (partner, device) in enumerate(zip(partners, devices)):
            remote.append(
                pltpu.make_async_remote_copy(
                    src_ref=part(source, chunk, axis, partner),
                    dst_ref=part(target, chunk, axis, me),
                    send_sem=send_sem.at[base + q],
                    recv_sem=recv_sem.at[base + q],
                    device_id=device,
                    device_id_type=pl.DeviceIdType.MESH,
                )
            )
        local = pltpu.make_async_copy(
            part(source, chunk, axis, me),
            part(target, chunk, axis, me),
            local_sem.at[stage * CHUNKS + chunk],
        )
        return remote, local

    started = []

    def launch(stage, chunk, axis, source, target):
        remote, local = copies(stage, chunk, axis, source, target)
        for copy in remote:
            copy.start()
        local.start()
        started.extend(remote)
        return remote, local

    def landed(pair):
        remote, local = pair
        for copy in remote:
            copy.wait_recv()
        local.wait()

    encode(0)
    pl.semaphore_wait(barrier, len(greeted))
    flying = []
    for chunk in range(CHUNKS):
        if chunk > 0:
            encode(chunk)
        flying.append(launch(0, chunk, FIRST[chunk][0], coded, first_a))
    for stage, source, target in ((1, first_a, first_b), (2, first_b, middle)):
        for chunk in range(CHUNKS):
            landed(flying[chunk])
            flying[chunk] = launch(stage, chunk, FIRST[chunk][stage], source, target)
    for chunk in range(CHUNKS):
        landed(flying[chunk])

    for copy in started:
        copy.wait_send()
    started.clear()
    taken = middle.reshape(CHUNKS * DEVICES, BLOCK, LANES)
    ordered = coded.reshape(CHUNKS * DEVICES, BLOCK, LANES)
    for chunk in range(CHUNKS):
        slot, half = chunk // HALVES, chunk % HALVES

        def move(k, _):
            for u in range(8):
                d = k * 8 + u
                ordered[chunk * DEVICES + d] = taken[source_ref[slot * DEVICES + d] + half * DEVICES]
            return 0

        lax.fori_loop(0, DEVICES // 8, move, 0)
        flying[chunk] = launch(3, chunk, SECOND[chunk][0], coded, second_a)
    for stage, source, target in ((4, second_a, second_b), (5, second_b, arrived)):
        for chunk in range(CHUNKS):
            landed(flying[chunk])
            flying[chunk] = launch(stage, chunk, SECOND[chunk][stage - 3], source, target)
    for chunk in range(CHUNKS):
        landed(flying[chunk])
        decode(chunk)

    def rim(number, source, target, device):
        copy = pltpu.make_async_remote_copy(
            src_ref=source, dst_ref=target, send_sem=rim_send.at[number],
            recv_sem=rim_recv.at[number], device_id=device,
            device_id_type=pl.DeviceIdType.MESH,
        )
        copy.start()
        started.append(copy)
        return copy

    inner = pl.ds(0, COLS)
    outer = pl.ds(COLS, LANES)
    upper = lax.broadcasted_iota(jnp.int32, (PAD, COLS), 0) < REACH
    top_rows, bottom_rows = pl.ds(PAD, PAD), pl.ds(TILE, PAD)
    for pair in range(PAIRS):
        f, g = 2 * pair, min(2 * pair + 1, FIELDS - 1)
        turned = pltpu.roll(fields[g, top_rows, inner], REACH, 0)
        sent_n[pair] = jnp.where(upper, fields[f, top_rows, inner], turned)
        turned = pltpu.roll(fields[g, bottom_rows, inner], REACH, 0)
        sent_s[pair] = jnp.where(upper, turned, fields[f, bottom_rows, inner])
    ends = [rim(2, sent_n, got_s, north), rim(3, sent_s, got_n, south)]

    def pack(k, _):
        lane = lax.broadcasted_iota(jnp.int32, (TALL, LANES), 1)
        rows = pl.ds(pl.multiple_of(PAD + k * TALL, 8), TALL)
        left = jnp.zeros((TALL, LANES), F32)
        right = jnp.zeros((TALL, LANES), F32)
        for f in range(FIELDS):
            here = (lane >= REACH * f) & (lane < REACH * (f + 1))
            low = fields[f, rows, pl.ds(0, LANES)]
            high = fields[f, rows, pl.ds(COLS - LANES, LANES)]
            left = jnp.where(here, pltpu.roll(low, REACH * f, 1) if f else low, left)
            right = jnp.where(here, pltpu.roll(high, REACH * (f + 1), 1), right)
        out = pl.ds(pl.multiple_of(k * TALL, 8), TALL)
        sent_w[out, :] = left
        sent_e[out, :] = right
        return 0

    lax.fori_loop(0, TILE // TALL, pack, 0)
    middle_rows, early, late = pl.ds(PAD, TILE), pl.ds(0, PAD), pl.ds(PAD + TILE, PAD)
    final_rows = pl.ds(TILE - PAD, PAD)
    side = [
        rim(0, sent_w, got_e.at[middle_rows], west),
        rim(1, sent_e, got_w.at[middle_rows], east),
        rim(4, sent_w.at[early], got_e.at[late], corners[0]),
        rim(5, sent_e.at[early], got_w.at[late], corners[1]),
        rim(6, sent_w.at[final_rows], got_e.at[early], corners[2]),
        rim(7, sent_e.at[final_rows], got_w.at[early], corners[3]),
    ]

    row_of = lax.broadcasted_iota(jnp.int32, (8, LANES), 0)
    bottom = row_of == 7
    top = row_of == 0
    lanes_high = lax.broadcasted_iota(jnp.int32, (HIGH, LANES), 1)
    right_end = lanes_high == LANES - 1
    left_end = lanes_high == 0

    def strip(k, high=HIGH):
        return pl.ds(pl.multiple_of(k * high, 8), high)

    def below_strip(k, high=HIGH):
        return pl.ds(pl.multiple_of(jnp.minimum((k + 1) * high, ROWS - 8), 8), 8)

    def from_south(values, after):
        high = values.shape[0]
        moved = pltpu.roll(values, high - 1, 0)
        end = jnp.where(bottom, pltpu.roll(after, 7, 0), moved[high - 8 :])
        return jnp.concatenate([moved[: high - 8], end], 0) if high > 8 else end

    def from_north(values, before):
        moved = pltpu.roll(values, 1, 0)
        start = jnp.where(top, before, moved[:8])
        return (jnp.concatenate([start, moved[8:]], 0) if HIGH > 8 else start), moved[:8]

    def block(c):
        return pl.ds((c % BLOCKS) * LANES, LANES)

    def faces(k, c):
        here = strip(k, FACE_HIGH)
        there = below_strip(k, FACE_HIGH)
        last_lane = lax.broadcasted_iota(jnp.int32, (FACE_HIGH, LANES), 1) == LANES - 1
        water = fields[WATER, here, block(c)]
        bed, width = fields[BED, here, block(c)], fields[WIDTH, here, block(c)]
        chan, rough = fields[CHAN, here, block(c)], fields[ROUGH, here, block(c)]
        level[here, block(c)] = bed + water
        volume[here, block(c)] = CELL * width * jnp.minimum(water, chan) + CELL * CELL * (
            jnp.maximum(water - chan, 0.0)
        )
        cap[here, block(c)] = CELL * width * chan
        inverse[here, block(c)] = 1.0 / (CELL * width) - 1.0 / (CELL * CELL)

        def to_east(f, v):
            after = pltpu.roll(fields[f, here, block(c + 1)], LANES - 1, 1)
            return jnp.where(last_lane, after, pltpu.roll(v, LANES - 1, 1))

        def to_south(f, v):
            return from_south(v, fields[f, there, block(c)])

        for shift, bed_f, part_f, deep_f, drag_f, gate_f, f, flow in (
            (to_east, bed_x, part_x, deep_x, drag_x, gate_x, FLOW_X, flow_x),
            (to_south, bed_y, part_y, deep_y, drag_y, gate_y, FLOW_Y, flow_y),
        ):
            bed_f[here, block(c)] = jnp.maximum(bed, shift(BED, bed))
            part_f[here, block(c)] = 1.0 - jnp.minimum(width, shift(WIDTH, width)) * (1.0 / CELL)
            deep_f[here, block(c)] = jnp.minimum(chan, shift(CHAN, chan))
            rough_n = shift(ROUGH, rough)
            mean = 0.5 * (rough + rough_n)
            wet = jnp.minimum(rough, rough_n) > 0
            drag_f[here, block(c)] = jnp.where(wet, (GRAV * STEP / CELL) * mean * mean, 0.0)
            gate_f[here, block(c)] = jnp.where(wet, GRAV * STEP, 0.0)
            flow[here, block(c)] = jnp.where(wet, fields[f, here, block(c)], 0.0)

    def many_faces(start, stop, blocks):
        def one(k, _):
            for c in blocks:
                faces(k, c)
            return 0

        lax.fori_loop(start, stop, one, 0)

    many_faces(1, TILE // FACE_HIGH, range(BLOCKS - 2))

    for copy in side:
        copy.wait_recv()
    at_east = col == NC - 1
    at_west = col == 0

    half = (TILE + 2 * PAD) // 2

    def unpack(k, _):
        lane = lax.broadcasted_iota(jnp.int32, (half, LANES), 1)
        rows = pl.ds(pl.multiple_of(k * half, 8), half)
        from_e = got_e[rows, :]
        from_w = got_w[rows, :]
        for f in range(FIELDS):
            low = pltpu.roll(from_e, LANES - REACH * f, 1) if f else from_e
            high = pltpu.roll(from_w, LANES - REACH * (f + 1), 1)
            if f == ROUGH:
                low = jnp.where(at_east, -1.0, low)
                high = jnp.where(at_west, -1.0, high)
            fill = 1.0 if f in (WIDTH, CHAN) else (-1.0 if f == ROUGH else 0.0)
            mixed = jnp.where(lane < REACH, low, jnp.where(lane >= LANES - REACH, high, fill))
            fields[f, rows, outer] = mixed
        return 0

    lax.fori_loop(0, 2, unpack, 0)
    many_faces(1, TILE // FACE_HIGH, range(BLOCKS - 2, BLOCKS))
    for copy in ends:
        copy.wait_recv()
    for pair in range(PAIRS):
        for got, rows in ((got_n, early), (got_s, late)):
            fields[2 * pair, rows, inner] = got[pair]
            if 2 * pair + 1 < FIELDS:
                fields[2 * pair + 1, rows, inner] = pltpu.roll(got[pair], REACH, 0)
    first = fields[ROUGH, pl.ds(0, 8), :]
    fields[ROUGH, pl.ds(0, 8), :] = jnp.where(row == 0, -1.0, first)
    last = fields[ROUGH, pl.ds(PAD + TILE, 8), :]
    fields[ROUGH, pl.ds(PAD + TILE, 8), :] = jnp.where(row == NX * NZ - 1, -1.0, last)
    many_faces(0, 1, range(BLOCKS))
    many_faces(TILE // FACE_HIGH, ROWS // FACE_HIGH, range(BLOCKS))

    def face_flow(flow, surface, surface_n, bed_f, part_f, deep_f, drag_f, gate_f):
        crest = jnp.maximum(surface, surface_n) - bed_f
        depth = crest - part_f * jnp.minimum(crest, deep_f)
        power = jnp.exp2(jnp.log(jnp.maximum(depth, RMIN)) * (-7.0 / 3.0 * LOG2_E))
        below = 1.0 + drag_f * jnp.abs(flow) * power
        guess = pl.reciprocal(below, approx=True)
        guess = guess * (2.0 - below * guess)
        return (flow - gate_f * depth * (surface_n - surface)) * guess

    every = range(BLOCKS)
    for step in range(ITERS):
        final = step == ITERS - 1

        def sweep(k, above):
            here = strip(k)
            there = below_strip(k)
            surface = [level[here, block(c)] for c in every]
            turned = [pltpu.roll(v, LANES - 1, 1) for v in surface]
            new_x = []
            for c in every:
                b = block(c)
                surface_e = jnp.where(right_end, turned[(c + 1) % BLOCKS], turned[c])
                new_x.append(
                    face_flow(
                        flow_x[here, b], surface[c], surface_e, bed_x[here, b], part_x[here, b],
                        deep_x[here, b], drag_x[here, b], gate_x[here, b],
                    )
                )
            passed = [pltpu.roll(v, 1, 1) for v in new_x]
            sunk = []
            for c in every:
                b = block(c)
                surface_s = from_south(surface[c], level[there, b])
                new_y = face_flow(
                    flow_y[here, b], surface[c], surface_s, bed_y[here, b], part_y[here, b],
                    deep_y[here, b], drag_y[here, b], gate_y[here, b],
                )
                from_n, end = from_north(new_y, above[c])
                sunk.append(end)
                from_w = jnp.where(left_end, passed[c - 1], passed[c])
                inflow = from_w - new_x[c] + from_n - new_y
                held = jnp.maximum(volume[here, b] + STEP * inflow, 0.0)
                water = jnp.minimum(held, cap[here, b]) * inverse[here, b] + held * (
                    1.0 / (CELL * CELL)
                )
                if not final:
                    flow_x[here, b] = new_x[c]
                    flow_y[here, b] = new_y
                    volume[here, b] = held
                    level[here, b] = fields[BED, here, b] + water
                elif c < BLOCKS - 1:
                    water_out[here, b] = water
                    fx_out[here, b] = new_x[c]
                    fy_out[here, b] = new_y
            return tuple(sunk)

        carry = tuple(jnp.zeros((8, LANES), F32) for c in every)
        if not final:
            lax.fori_loop(0, STRIPS, sweep, carry)

    stores = []
    begin = 0
    sent = 0
    for piece in range(PARTS):
        end = -(-(PAD + (piece + 1) * (TILE // PARTS)) // HIGH)
        carry = lax.fori_loop(begin, end, sweep, carry)
        begin = end
        until = min(TILE, end * HIGH - PAD) if piece < PARTS - 1 else TILE
        size = until - sent
        for n, (ref, hbm) in enumerate(
            ((water_out, water_hbm), (fx_out, fx_out_hbm), (fy_out, fy_out_hbm))
        ):
            copy = pltpu.make_async_copy(
                ref.at[pl.ds(PAD + sent, size)], hbm.at[pl.ds(sent, size)], out_sem.at[piece * 3 + n]
            )
            copy.start()
            stores.append(copy)
        sent = until
    for copy in stores:
        copy.wait()
    for copy in started:
        copy.wait_send()


def body(depth, flow_x, flow_y, floor, width, chan, rough, route, wet_tiles):
    target = (route[:, 0] * NC + route[:, 1]) * SLOTS + route[:, 2]
    old = jnp.arange(DEVICES * SLOTS, dtype=jnp.int32)
    where_held = (old % SLOTS) * (HALVES * DEVICES) + old // SLOTS
    slot_major = (old % DEVICES) * SLOTS + old // DEVICES
    source = jnp.sum(
        jnp.where(slot_major[:, None] == target[None, :], where_held[None, :], 0), axis=1
    )
    whole = pl.BlockSpec(memory_space=pl.ANY)
    smem = pl.BlockSpec(memory_space=pltpu.SMEM)
    pieces = pltpu.VMEM(PIECES, jnp.int16)
    grid = pltpu.VMEM((ROWS, WIDE), F32)
    edge = pltpu.VMEM((TILE, LANES), F32)
    out = jax.ShapeDtypeStruct((TILE, COLS), F32)
    operands = (depth, flow_x, flow_y, floor, width, chan, rough)
    return pl.pallas_call(
        migrate_and_route,
        out_shape=(out, out, out),
        in_specs=[whole] * 7 + [smem] * 2,
        out_specs=(whole, whole, whole),
        scratch_shapes=[pltpu.VMEM(a.shape, a.dtype) for a in operands]
        + [pltpu.VMEM((ROWS, COLS), F32)] * 3
        + [pieces] * 7
        + [pltpu.VMEM((FIELDS, ROWS, WIDE), F32)]
        + [edge] * 2
        + [pltpu.VMEM((TILE + 2 * PAD, LANES), F32)] * 2
        + [pltpu.VMEM((PAIRS, PAD, COLS), F32)] * 4
        + [grid] * 16
        + [
            pltpu.SemaphoreType.DMA((6 * CHUNKS * 8,)),
            pltpu.SemaphoreType.DMA((6 * CHUNKS * 8,)),
            pltpu.SemaphoreType.DMA((6 * CHUNKS,)),
            pltpu.SemaphoreType.DMA((8,)),
            pltpu.SemaphoreType.DMA((8,)),
            pltpu.SemaphoreType.DMA((SLOTS * FIELDS,)),
            pltpu.SemaphoreType.DMA((PARTS * 3,)),
        ],
        compiler_params=pltpu.CompilerParams(
            collective_id=0, has_side_effects=True, vmem_limit_bytes=58 * 2**20
        ),
    )(*operands, source, wet_tiles)


def solution(mesh):
    tiles = P(("row", "col"), None, None)
    block = P("row", "col")
    return jax.shard_map(
        body,
        mesh=mesh,
        in_specs=(tiles,) * 7 + (P(), block),
        out_specs=(block, block, block),
        check_vma=False,
    )
```

```python
import jax
import jax.numpy as jnp
from jax import lax
from jax.experimental import pallas as pl
from jax.experimental.pallas import tpu as pltpu
from jax.sharding import PartitionSpec as P

ITERS = 4
GRAV = 9.81
CELL = 5.0
STEP = 0.1
RMIN = 0.1

NX, NZ, NC = 4, 4, 8
DEVICES = NX * NZ * NC
SLOTS = 3
HALVES = 2
CHUNKS = SLOTS * HALVES
TILE = 256
BLOCK = 16
LANES = 128
FIRST = ("yxz", "xzy", "zyx")
SECOND = ("zxy", "yzx", "xyz")
PIECES = (CHUNKS, NX, NZ, NC, BLOCK, LANES)

PAD = 8
HIGH = 72
STRIPS = -(-(TILE + 2 * PAD) // HIGH)
ROWS = STRIPS * HIGH
COLS = SLOTS * TILE
WIDE = COLS + LANES
REACH = 4
FIELDS = 7
BLOCKS = WIDE // LANES
PARTS = 4
TALL = 64
FACE_HIGH = 32
PAIRS = (FIELDS + 1) // 2
LOG2_E = 1.4426950408889634
WATER, FLOW_X, FLOW_Y, BED, WIDTH, CHAN, ROUGH = range(FIELDS)
F32 = jnp.float32


def to_code(values):
    return values.astype(jnp.int32).astype(jnp.int16)


def flow_code(flow):
    root = jnp.sqrt(jnp.sqrt(jnp.abs(flow) * 0.25))
    size = jnp.minimum(root * 32767.0 + 0.5, 32767.0).astype(jnp.int32)
    return jnp.where(flow < 0, -size, size).astype(jnp.int16)


def flow_value(code):
    return (code * code) * (code * jnp.abs(code)) * (4.0 / 32767.0**4)


def floor_code(floor):
    coarse = (floor * 65536.0).astype(jnp.int32)
    fine = -((floor * 16777216.0 + 0.5).astype(jnp.int32))
    return jnp.where(floor < 2.0**-9, fine, coarse).astype(jnp.int16)


def floor_value(code):
    return jnp.where(code < 0, code * -(2.0**-24), code * 2.0**-16)


def part(ref, chunk, axis, index):
    if axis == "x":
        return ref.at[chunk, index]
    if axis == "z":
        return ref.at[chunk, :, index]
    return ref.at[chunk, :, :, index]


def migrate_and_route(
    depth_hbm, fx_hbm, fy_hbm, floor_hbm, width_hbm, chan_hbm, rough_hbm, source_ref, wet_ref,
    water_hbm, fx_out_hbm, fy_out_hbm,
    depth_ref, fx_ref, fy_ref, floor_ref, width_ref, chan_ref, rough_ref,
    water_out, fx_out, fy_out,
    coded, first_a, first_b, middle_l, middle_r, second_a, second_b, arrived,
    fields, sent_w, sent_e, got_e, got_w, sent_n, sent_s, got_n, got_s, level, volume, cap, inverse, flow_x, flow_y,
    bed_x, part_x, deep_x, drag_x, gate_x, bed_y, part_y, deep_y, drag_y, gate_y,
    send_sem, recv_sem, local_sem, rim_send, rim_recv, in_sem, out_sem,
):
    row = lax.axis_index("row")
    col = lax.axis_index("col")
    own_x = row // NZ
    own_z = row % NZ

    def place(x, z, c):
        return (x * NZ + z, c)

    west = (row, (col + NC - 1) % NC)
    east = (row, (col + 1) % NC)
    north = ((row + NX * NZ - 1) % (NX * NZ), col)
    south = ((row + 1) % (NX * NZ), col)

    corners = [(north[0], west[1]), (north[0], east[1]), (south[0], west[1]), (south[0], east[1])]

    barrier = pltpu.get_barrier_semaphore()
    greeted = [place((own_x + d) % NX, own_z, col) for d in (1, 2, 3)]
    greeted += [place(own_x, (own_z + d) % NZ, col) for d in (1, 2, 3)]
    greeted += [place(own_x, own_z, (col + d) % NC) for d in range(1, NC)]
    greeted += [north, south] + corners
    for device in greeted:
        pl.semaphore_signal(barrier, inc=1, device_id=device, device_id_type=pl.DeviceIdType.MESH)

    chunks = [slot * HALVES + half for half in range(HALVES) for slot in range(SLOTS)]
    pairs = (
        (depth_hbm, depth_ref), (fx_hbm, fx_ref), (fy_hbm, fy_ref), (floor_hbm, floor_ref),
        (width_hbm, width_ref), (chan_hbm, chan_ref), (rough_hbm, rough_ref),
    )
    loads = {}
    for chunk in chunks:
        slot, lanes = chunk // HALVES, pl.ds(chunk % HALVES * LANES, LANES)
        loads[chunk] = [
            pltpu.make_async_copy(
                hbm.at[slot, :, lanes], ref.at[slot, :, lanes], in_sem.at[chunk * FIELDS + n]
            )
            for n, (hbm, ref) in enumerate(pairs)
        ]
        for copy in loads[chunk]:
            copy.start()

    def encode(chunk):
        slot, half = chunk // HALVES, chunk % HALVES
        lanes = pl.ds(half * LANES, LANES)
        for copy in loads[chunk]:
            copy.wait()

        def block(b, _):
            rows = pl.ds(pl.multiple_of(b * BLOCK, BLOCK), BLOCK)

            def put(plane, code):
                coded[chunk, b // NZ, b % NZ, plane] = code

            depth = depth_ref[slot, rows, lanes] * 16384.0
            high = depth.astype(jnp.int32)
            low = ((depth - high.astype(F32)) * 65536.0).astype(jnp.int32) - 32768
            put(0, high.astype(jnp.int16))
            put(1, low.astype(jnp.int16))
            put(2, flow_code(fx_ref[slot, rows, lanes]))
            put(3, flow_code(fy_ref[slot, rows, lanes]))
            put(4, floor_code(floor_ref[slot, rows, lanes].astype(F32)))
            put(5, to_code(width_ref[slot, rows, lanes].astype(F32) * 256.0))
            put(6, to_code(chan_ref[slot, rows, lanes].astype(F32) * 256.0))
            put(7, to_code(rough_ref[slot, rows, lanes].astype(F32) * 8192.0))
            return 0

        lax.fori_loop(0, TILE // BLOCK, block, 0)

    def decode(chunk):
        slot, half = chunk // HALVES, chunk % HALVES
        lanes = pl.ds(slot * TILE + half * LANES, LANES)
        wet = wet_ref[0, slot].astype(F32)

        def block(b, _):
            rows = pl.ds(pl.multiple_of(PAD + b * BLOCK, 8), BLOCK)

            def get(plane):
                return arrived[chunk, b // NZ, b % NZ, plane].astype(jnp.int32).astype(F32)

            chan = get(6) * (1.0 / 256.0)
            fields[WATER, rows, lanes] = get(0) * 2.0**-14 + (get(1) + 32768.0) * 2.0**-30
            fields[FLOW_X, rows, lanes] = flow_value(get(2))
            fields[FLOW_Y, rows, lanes] = flow_value(get(3))
            fields[BED, rows, lanes] = floor_value(get(4)) - chan
            fields[WIDTH, rows, lanes] = get(5) * (1.0 / 256.0)
            fields[CHAN, rows, lanes] = chan
            fields[ROUGH, rows, lanes] = get(7) * (1.0 / 8192.0) * wet - (1.0 - wet)
            return 0

        lax.fori_loop(0, TILE // BLOCK, block, 0)

    def copies(stage, chunk, axis, source, target, taken, put):
        base = (stage * CHUNKS + chunk) * 8
        remote = []
        if axis == "y":
            me = col
            steps = [4, 5, 2, 3, 6, 7, 1]
            partners = [((col + (d // 2) * 2) % NC) // 2 * 2 + (col + d % 2) % 2 for d in steps]
            devices = [place(own_x, own_z, c) for c in partners]
        elif axis == "x":
            me = own_x
            partners = [(own_x + d) % NX for d in (2, 1, 3)]
            devices = [place(x, own_z, col) for x in partners]
        else:
            me = own_z
            partners = [(own_z + d) % NZ for d in (2, 1, 3)]
            devices = [place(own_x, z, col) for z in partners]
        for q, (partner, device) in enumerate(zip(partners, devices)):
            remote.append(
                pltpu.make_async_remote_copy(
                    src_ref=part(source, taken, axis, partner),
                    dst_ref=part(target, put, axis, me),
                    send_sem=send_sem.at[base + q],
                    recv_sem=recv_sem.at[base + q],
                    device_id=device,
                    device_id_type=pl.DeviceIdType.MESH,
                )
            )
        local = pltpu.make_async_copy(
            part(source, taken, axis, me),
            part(target, put, axis, me),
            local_sem.at[stage * CHUNKS + chunk],
        )
        return remote, local

    started = []

    def launch(stage, chunk, axis, source, target, put=None):
        put = chunk if put is None else put
        remote, local = copies(stage, chunk, axis, source, target, chunk, put)
        for copy in remote:
            copy.start()
        local.start()
        started.extend(remote)
        return remote, local

    def landed(pair):
        remote, local = pair
        for copy in remote:
            copy.wait_recv()
        local.wait()

    middles = (middle_l, middle_r)
    encode(chunks[0])
    pl.semaphore_wait(barrier, len(greeted))
    flying = {}
    for chunk in chunks:
        if chunk != chunks[0]:
            encode(chunk)
        flying[chunk] = launch(0, chunk, FIRST[chunk // HALVES][0], coded, first_a)
    opening = list(started)
    started.clear()
    for chunk in chunks:
        landed(flying[chunk])
        flying[chunk] = launch(1, chunk, FIRST[chunk // HALVES][1], first_a, first_b)
    for chunk in chunks:
        landed(flying[chunk])
        flying[chunk] = launch(
            2, chunk, FIRST[chunk // HALVES][2], first_b, middles[chunk % HALVES], chunk // HALVES
        )
    for copy in opening:
        copy.wait_send()
    ordered = coded.reshape(CHUNKS * DEVICES, BLOCK, LANES)
    for half in range(HALVES):
        group = chunks[half * SLOTS : (half + 1) * SLOTS]
        held = middles[half].reshape(SLOTS * DEVICES, BLOCK, LANES)
        for chunk in group:
            landed(flying[chunk])
        for chunk in group:
            slot = chunk // HALVES

            def move(k, _):
                for u in range(8):
                    d = k * 8 + u
                    ordered[chunk * DEVICES + d] = held[source_ref[slot * DEVICES + d]]
                return 0

            lax.fori_loop(0, DEVICES // 8, move, 0)
            flying[chunk] = launch(3, chunk, SECOND[slot][0], coded, second_a)
    for stage, source, target in ((4, second_a, second_b), (5, second_b, arrived)):
        for chunk in chunks:
            landed(flying[chunk])
            flying[chunk] = launch(stage, chunk, SECOND[chunk // HALVES][stage - 3], source, target)
    for chunk in chunks:
        landed(flying[chunk])
        decode(chunk)

    def rim(number, source, target, device):
        copy = pltpu.make_async_remote_copy(
            src_ref=source, dst_ref=target, send_sem=rim_send.at[number],
            recv_sem=rim_recv.at[number], device_id=device,
            device_id_type=pl.DeviceIdType.MESH,
        )
        copy.start()
        started.append(copy)
        return copy

    inner = pl.ds(0, COLS)
    outer = pl.ds(COLS, LANES)
    upper = lax.broadcasted_iota(jnp.int32, (PAD, COLS), 0) < REACH
    top_rows, bottom_rows = pl.ds(PAD, PAD), pl.ds(TILE, PAD)
    for pair in range(PAIRS):
        f, g = 2 * pair, min(2 * pair + 1, FIELDS - 1)
        turned = pltpu.roll(fields[g, top_rows, inner], REACH, 0)
        sent_n[pair] = jnp.where(upper, fields[f, top_rows, inner], turned)
        turned = pltpu.roll(fields[g, bottom_rows, inner], REACH, 0)
        sent_s[pair] = jnp.where(upper, turned, fields[f, bottom_rows, inner])
    ends = [rim(2, sent_n, got_s, north), rim(3, sent_s, got_n, south)]

    def pack(k, _):
        lane = lax.broadcasted_iota(jnp.int32, (TALL, LANES), 1)
        rows = pl.ds(pl.multiple_of(PAD + k * TALL, 8), TALL)
        left = jnp.zeros((TALL, LANES), F32)
        right = jnp.zeros((TALL, LANES), F32)
        for f in range(FIELDS):
            here = (lane >= REACH * f) & (lane < REACH * (f + 1))
            low = fields[f, rows, pl.ds(0, LANES)]
            high = fields[f, rows, pl.ds(COLS - LANES, LANES)]
            left = jnp.where(here, pltpu.roll(low, REACH * f, 1) if f else low, left)
            right = jnp.where(here, pltpu.roll(high, REACH * (f + 1), 1), right)
        out = pl.ds(pl.multiple_of(k * TALL, 8), TALL)
        sent_w[out, :] = left
        sent_e[out, :] = right
        return 0

    lax.fori_loop(0, TILE // TALL, pack, 0)
    middle_rows, early, late = pl.ds(PAD, TILE), pl.ds(0, PAD), pl.ds(PAD + TILE, PAD)
    final_rows = pl.ds(TILE - PAD, PAD)
    side = [
        rim(0, sent_w, got_e.at[middle_rows], west),
        rim(1, sent_e, got_w.at[middle_rows], east),
        rim(4, sent_w.at[early], got_e.at[late], corners[0]),
        rim(5, sent_e.at[early], got_w.at[late], corners[1]),
        rim(6, sent_w.at[final_rows], got_e.at[early], corners[2]),
        rim(7, sent_e.at[final_rows], got_w.at[early], corners[3]),
    ]

    row_of = lax.broadcasted_iota(jnp.int32, (8, LANES), 0)
    bottom = row_of == 7
    top = row_of == 0
    lanes_high = lax.broadcasted_iota(jnp.int32, (HIGH, LANES), 1)
    right_end = lanes_high == LANES - 1
    left_end = lanes_high == 0

    def strip(k, high=HIGH):
        return pl.ds(pl.multiple_of(k * high, 8), high)

    def below_strip(k, high=HIGH):
        return pl.ds(pl.multiple_of(jnp.minimum((k + 1) * high, ROWS - 8), 8), 8)

    def from_south(values, after):
        high = values.shape[0]
        moved = pltpu.roll(values, high - 1, 0)
        end = jnp.where(bottom, pltpu.roll(after, 7, 0), moved[high - 8 :])
        return jnp.concatenate([moved[: high - 8], end], 0) if high > 8 else end

    def from_north(values, before):
        moved = pltpu.roll(values, 1, 0)
        start = jnp.where(top, before, moved[:8])
        return (jnp.concatenate([start, moved[8:]], 0) if HIGH > 8 else start), moved[:8]

    def block(c):
        return pl.ds((c % BLOCKS) * LANES, LANES)

    def faces(k, c):
        here = strip(k, FACE_HIGH)
        there = below_strip(k, FACE_HIGH)
        last_lane = lax.broadcasted_iota(jnp.int32, (FACE_HIGH, LANES), 1) == LANES - 1
        water = fields[WATER, here, block(c)]
        bed, width = fields[BED, here, block(c)], fields[WIDTH, here, block(c)]
        chan, rough = fields[CHAN, here, block(c)], fields[ROUGH, here, block(c)]
        level[here, block(c)] = bed + water
        volume[here, block(c)] = CELL * width * jnp.minimum(water, chan) + CELL * CELL * (
            jnp.maximum(water - chan, 0.0)
        )
        cap[here, block(c)] = CELL * width * chan
        inverse[here, block(c)] = 1.0 / (CELL * width) - 1.0 / (CELL * CELL)

        def to_east(f, v):
            after = pltpu.roll(fields[f, here, block(c + 1)], LANES - 1, 1)
            return jnp.where(last_lane, after, pltpu.roll(v, LANES - 1, 1))

        def to_south(f, v):
            return from_south(v, fields[f, there, block(c)])

        for shift, bed_f, part_f, deep_f, drag_f, gate_f, f, flow in (
            (to_east, bed_x, part_x, deep_x, drag_x, gate_x, FLOW_X, flow_x),
            (to_south, bed_y, part_y, deep_y, drag_y, gate_y, FLOW_Y, flow_y),
        ):
            bed_f[here, block(c)] = jnp.maximum(bed, shift(BED, bed))
            part_f[here, block(c)] = 1.0 - jnp.minimum(width, shift(WIDTH, width)) * (1.0 / CELL)
            deep_f[here, block(c)] = jnp.minimum(chan, shift(CHAN, chan))
            rough_n = shift(ROUGH, rough)
            mean = 0.5 * (rough + rough_n)
            wet = jnp.minimum(rough, rough_n) > 0
            drag_f[here, block(c)] = jnp.where(wet, (GRAV * STEP / CELL) * mean * mean, 0.0)
            gate_f[here, block(c)] = jnp.where(wet, GRAV * STEP, 0.0)
            flow[here, block(c)] = jnp.where(wet, fields[f, here, block(c)], 0.0)

    def many_faces(start, stop, blocks):
        def one(k, _):
            for c in blocks:
                faces(k, c)
            return 0

        lax.fori_loop(start, stop, one, 0)

    many_faces(1, TILE // FACE_HIGH, range(BLOCKS - 2))

    for copy in side:
        copy.wait_recv()
    at_east = col == NC - 1
    at_west = col == 0

    half = (TILE + 2 * PAD) // 2

    def unpack(k, _):
        lane = lax.broadcasted_iota(jnp.int32, (half, LANES), 1)
        rows = pl.ds(pl.multiple_of(k * half, 8), half)
        from_e = got_e[rows, :]
        from_w = got_w[rows, :]
        for f in range(FIELDS):
            low = pltpu.roll(from_e, LANES - REACH * f, 1) if f else from_e
            high = pltpu.roll(from_w, LANES - REACH * (f + 1), 1)
            if f == ROUGH:
                low = jnp.where(at_east, -1.0, low)
                high = jnp.where(at_west, -1.0, high)
            fill = 1.0 if f in (WIDTH, CHAN) else (-1.0 if f == ROUGH else 0.0)
            mixed = jnp.where(lane < REACH, low, jnp.where(lane >= LANES - REACH, high, fill))
            fields[f, rows, outer] = mixed
        return 0

    lax.fori_loop(0, 2, unpack, 0)
    many_faces(1, TILE // FACE_HIGH, range(BLOCKS - 2, BLOCKS))
    for copy in ends:
        copy.wait_recv()
    for pair in range(PAIRS):
        for got, rows in ((got_n, early), (got_s, late)):
            fields[2 * pair, rows, inner] = got[pair]
            if 2 * pair + 1 < FIELDS:
                fields[2 * pair + 1, rows, inner] = pltpu.roll(got[pair], REACH, 0)
    first = fields[ROUGH, pl.ds(0, 8), :]
    fields[ROUGH, pl.ds(0, 8), :] = jnp.where(row == 0, -1.0, first)
    last = fields[ROUGH, pl.ds(PAD + TILE, 8), :]
    fields[ROUGH, pl.ds(PAD + TILE, 8), :] = jnp.where(row == NX * NZ - 1, -1.0, last)
    many_faces(0, 1, range(BLOCKS))
    many_faces(TILE // FACE_HIGH, ROWS // FACE_HIGH, range(BLOCKS))

    def face_flow(flow, surface, surface_n, bed_f, part_f, deep_f, drag_f, gate_f):
        crest = jnp.maximum(surface, surface_n) - bed_f
        depth = crest - part_f * jnp.minimum(crest, deep_f)
        power = jnp.exp2(jnp.log(jnp.maximum(depth, RMIN)) * (-7.0 / 3.0 * LOG2_E))
        below = 1.0 + drag_f * jnp.abs(flow) * power
        guess = pl.reciprocal(below, approx=True)
        guess = guess * (2.0 - below * guess)
        return (flow - gate_f * depth * (surface_n - surface)) * guess

    every = range(BLOCKS)
    for step in range(ITERS):
        final = step == ITERS - 1

        def sweep(k, above):
            here = strip(k)
            there = below_strip(k)
            surface = [level[here, block(c)] for c in every]
            turned = [pltpu.roll(v, LANES - 1, 1) for v in surface]
            new_x = []
            for c in every:
                b = block(c)
                surface_e = jnp.where(right_end, turned[(c + 1) % BLOCKS], turned[c])
                new_x.append(
                    face_flow(
                        flow_x[here, b], surface[c], surface_e, bed_x[here, b], part_x[here, b],
                        deep_x[here, b], drag_x[here, b], gate_x[here, b],
                    )
                )
            passed = [pltpu.roll(v, 1, 1) for v in new_x]
            sunk = []
            for c in every:
                b = block(c)
                surface_s = from_south(surface[c], level[there, b])
                new_y = face_flow(
                    flow_y[here, b], surface[c], surface_s, bed_y[here, b], part_y[here, b],
                    deep_y[here, b], drag_y[here, b], gate_y[here, b],
                )
                from_n, end = from_north(new_y, above[c])
                sunk.append(end)
                from_w = jnp.where(left_end, passed[c - 1], passed[c])
                inflow = from_w - new_x[c] + from_n - new_y
                held = jnp.maximum(volume[here, b] + STEP * inflow, 0.0)
                water = jnp.minimum(held, cap[here, b]) * inverse[here, b] + held * (
                    1.0 / (CELL * CELL)
                )
                if not final:
                    flow_x[here, b] = new_x[c]
                    flow_y[here, b] = new_y
                    volume[here, b] = held
                    level[here, b] = fields[BED, here, b] + water
                elif c < BLOCKS - 1:
                    water_out[here, b] = water
                    fx_out[here, b] = new_x[c]
                    fy_out[here, b] = new_y
            return tuple(sunk)

        carry = tuple(jnp.zeros((8, LANES), F32) for c in every)
        if not final:
            lax.fori_loop(0, STRIPS, sweep, carry)

    stores = []
    begin = 0
    sent = 0
    for piece in range(PARTS):
        end = -(-(PAD + (piece + 1) * (TILE // PARTS)) // HIGH)
        carry = lax.fori_loop(begin, end, sweep, carry)
        begin = end
        until = min(TILE, end * HIGH - PAD) if piece < PARTS - 1 else TILE
        size = until - sent
        for n, (ref, hbm) in enumerate(
            ((water_out, water_hbm), (fx_out, fx_out_hbm), (fy_out, fy_out_hbm))
        ):
            copy = pltpu.make_async_copy(
                ref.at[pl.ds(PAD + sent, size)], hbm.at[pl.ds(sent, size)], out_sem.at[piece * 3 + n]
            )
            copy.start()
            stores.append(copy)
        sent = until
    for copy in stores:
        copy.wait()
    for copy in started:
        copy.wait_send()


def body(depth, flow_x, flow_y, floor, width, chan, rough, route, wet_tiles):
    target = (route[:, 0] * NC + route[:, 1]) * SLOTS + route[:, 2]
    old = jnp.arange(DEVICES * SLOTS, dtype=jnp.int32)
    where_held = (old % SLOTS) * DEVICES + old // SLOTS
    slot_major = (old % DEVICES) * SLOTS + old // DEVICES
    source = jnp.sum(
        jnp.where(slot_major[:, None] == target[None, :], where_held[None, :], 0), axis=1
    )
    whole = pl.BlockSpec(memory_space=pl.ANY)
    smem = pl.BlockSpec(memory_space=pltpu.SMEM)
    pieces = pltpu.VMEM(PIECES, jnp.int16)
    grid = pltpu.VMEM((ROWS, WIDE), F32)
    edge = pltpu.VMEM((TILE, LANES), F32)
    out = jax.ShapeDtypeStruct((TILE, COLS), F32)
    operands = (depth, flow_x, flow_y, floor, width, chan, rough)
    return pl.pallas_call(
        migrate_and_route,
        out_shape=(out, out, out),
        in_specs=[whole] * 7 + [smem] * 2,
        out_specs=(whole, whole, whole),
        scratch_shapes=[pltpu.VMEM(a.shape, a.dtype) for a in operands]
        + [pltpu.VMEM((ROWS, COLS), F32)] * 3
        + [pieces] * 3
        + [pltpu.VMEM((SLOTS,) + PIECES[1:], jnp.int16)] * 2
        + [pieces] * 3
        + [pltpu.VMEM((FIELDS, ROWS, WIDE), F32)]
        + [edge] * 2
        + [pltpu.VMEM((TILE + 2 * PAD, LANES), F32)] * 2
        + [pltpu.VMEM((PAIRS, PAD, COLS), F32)] * 4
        + [grid] * 16
        + [
            pltpu.SemaphoreType.DMA((6 * CHUNKS * 8,)),
            pltpu.SemaphoreType.DMA((6 * CHUNKS * 8,)),
            pltpu.SemaphoreType.DMA((6 * CHUNKS,)),
            pltpu.SemaphoreType.DMA((8,)),
            pltpu.SemaphoreType.DMA((8,)),
            pltpu.SemaphoreType.DMA((CHUNKS * FIELDS,)),
            pltpu.SemaphoreType.DMA((PARTS * 3,)),
        ],
        compiler_params=pltpu.CompilerParams(
            collective_id=0, has_side_effects=True, vmem_limit_bytes=58 * 2**20
        ),
    )(*operands, source, wet_tiles)


def solution(mesh):
    tiles = P(("row", "col"), None, None)
    block = P("row", "col")
    return jax.shard_map(
        body,
        mesh=mesh,
        in_specs=(tiles,) * 7 + (P(), block),
        out_specs=(block, block, block),
        check_vma=False,
    )
```

```python
import jax
import jax.numpy as jnp
from jax import lax
from jax.experimental import pallas as pl
from jax.experimental.pallas import tpu as pltpu
from jax.sharding import PartitionSpec as P

ITERS = 4
GRAV = 9.81
CELL = 5.0
STEP = 0.1
RMIN = 0.1

NX, NZ, NC = 4, 4, 8
DEVICES = NX * NZ * NC
SLOTS = 3
HALVES = 2
CHUNKS = SLOTS * HALVES
TILE = 256
BLOCK = 16
LANES = 128
FIRST = ("yxz", "xzy", "zyx")
SECOND = ("zxy", "yzx", "xyz")
PIECES = (CHUNKS, NX, NZ, NC, BLOCK, LANES)

PAD = 8
HIGH = 72
STRIPS = -(-(TILE + 2 * PAD) // HIGH)
ROWS = STRIPS * HIGH
COLS = SLOTS * TILE
WIDE = COLS + LANES
REACH = 4
FIELDS = 7
BLOCKS = WIDE // LANES
PARTS = 4
TALL = 64
FOLD = 32
FACE_HIGH = 32
PAIRS = (FIELDS + 1) // 2
LOG2_E = 1.4426950408889634
WATER, FLOW_X, FLOW_Y, BED, WIDTH, CHAN, ROUGH = range(FIELDS)
F32 = jnp.float32


def to_code(values):
    return values.astype(jnp.int32).astype(jnp.int16)


def flow_code(flow):
    root = jnp.sqrt(jnp.sqrt(jnp.abs(flow) * 0.25))
    size = jnp.minimum(root * 32767.0 + 0.5, 32767.0).astype(jnp.int32)
    return jnp.where(flow < 0, -size, size).astype(jnp.int16)


def flow_value(code):
    return (code * code) * (code * jnp.abs(code)) * (4.0 / 32767.0**4)


def floor_code(floor):
    coarse = (floor * 65536.0).astype(jnp.int32)
    fine = -((floor * 16777216.0 + 0.5).astype(jnp.int32))
    return jnp.where(floor < 2.0**-9, fine, coarse).astype(jnp.int16)


def floor_value(code):
    return jnp.where(code < 0, code * -(2.0**-24), code * 2.0**-16)


def part(ref, chunk, axis, index):
    if axis == "x":
        return ref.at[chunk, index]
    if axis == "z":
        return ref.at[chunk, :, index]
    return ref.at[chunk, :, :, index]


def migrate_and_route(
    depth_hbm, fx_hbm, fy_hbm, floor_hbm, width_hbm, chan_hbm, rough_hbm, route_ref, wet_ref,
    water_hbm, fx_out_hbm, fy_out_hbm,
    depth_ref, fx_ref, fy_ref, floor_ref, width_ref, chan_ref, rough_ref,
    water_out, fx_out, fy_out,
    coded, first_a, first_b, middle_l, middle_r, second_a, second_b, arrived,
    fields, sent_w, sent_e, got_e, got_w, sent_n, sent_s, got_n, got_s, level, volume, cap, inverse, flow_x, flow_y,
    bed_x, part_x, deep_x, drag_x, gate_x, bed_y, part_y, deep_y, drag_y, gate_y,
    source_rows, source_ref, send_sem, recv_sem, local_sem, rim_send, rim_recv, in_sem, out_sem,
    source_sem,
):
    row = lax.axis_index("row")
    col = lax.axis_index("col")
    own_x = row // NZ
    own_z = row % NZ

    def place(x, z, c):
        return (x * NZ + z, c)

    west = (row, (col + NC - 1) % NC)
    east = (row, (col + 1) % NC)
    north = ((row + NX * NZ - 1) % (NX * NZ), col)
    south = ((row + 1) % (NX * NZ), col)

    corners = [(north[0], west[1]), (north[0], east[1]), (south[0], west[1]), (south[0], east[1])]

    barrier = pltpu.get_barrier_semaphore()
    greeted = [place((own_x + d) % NX, own_z, col) for d in (1, 2, 3)]
    greeted += [place(own_x, (own_z + d) % NZ, col) for d in (1, 2, 3)]
    greeted += [place(own_x, own_z, (col + d) % NC) for d in range(1, NC)]
    greeted += [north, south] + corners
    for device in greeted:
        pl.semaphore_signal(barrier, inc=1, device_id=device, device_id_type=pl.DeviceIdType.MESH)

    chunks = [slot * HALVES + half for half in range(HALVES) for slot in range(SLOTS)]
    pairs = (
        (depth_hbm, depth_ref), (fx_hbm, fx_ref), (fy_hbm, fy_ref), (floor_hbm, floor_ref),
        (width_hbm, width_ref), (chan_hbm, chan_ref), (rough_hbm, rough_ref),
    )
    loads = {}
    for chunk in chunks:
        slot, lanes = chunk // HALVES, pl.ds(chunk % HALVES * LANES, LANES)
        loads[chunk] = [
            pltpu.make_async_copy(
                hbm.at[slot, :, lanes], ref.at[slot, :, lanes], in_sem.at[chunk * FIELDS + n]
            )
            for n, (hbm, ref) in enumerate(pairs)
        ]
        for copy in loads[chunk]:
            copy.start()

    def encode(chunk):
        slot, half = chunk // HALVES, chunk % HALVES
        lanes = pl.ds(half * LANES, LANES)
        for copy in loads[chunk]:
            copy.wait()

        def block(b, _):
            rows = pl.ds(pl.multiple_of(b * BLOCK, BLOCK), BLOCK)

            def put(plane, code):
                coded[chunk, b // NZ, b % NZ, plane] = code

            depth = depth_ref[slot, rows, lanes] * 16384.0
            high = depth.astype(jnp.int32)
            low = ((depth - high.astype(F32)) * 65536.0).astype(jnp.int32) - 32768
            put(0, high.astype(jnp.int16))
            put(1, low.astype(jnp.int16))
            put(2, flow_code(fx_ref[slot, rows, lanes]))
            put(3, flow_code(fy_ref[slot, rows, lanes]))
            put(4, floor_code(floor_ref[slot, rows, lanes].astype(F32)))
            put(5, to_code(width_ref[slot, rows, lanes].astype(F32) * 256.0))
            put(6, to_code(chan_ref[slot, rows, lanes].astype(F32) * 256.0))
            put(7, to_code(rough_ref[slot, rows, lanes].astype(F32) * 8192.0))
            return 0

        lax.fori_loop(0, TILE // BLOCK, block, 0)

    def decode(chunk):
        slot, half = chunk // HALVES, chunk % HALVES
        lanes = pl.ds(slot * TILE + half * LANES, LANES)
        wet = wet_ref[0, slot].astype(F32)

        def block(b, _):
            rows = pl.ds(pl.multiple_of(PAD + b * BLOCK, 8), BLOCK)

            def get(plane):
                return arrived[chunk, b // NZ, b % NZ, plane].astype(jnp.int32).astype(F32)

            chan = get(6) * (1.0 / 256.0)
            fields[WATER, rows, lanes] = get(0) * 2.0**-14 + (get(1) + 32768.0) * 2.0**-30
            fields[FLOW_X, rows, lanes] = flow_value(get(2))
            fields[FLOW_Y, rows, lanes] = flow_value(get(3))
            fields[BED, rows, lanes] = floor_value(get(4)) - chan
            fields[WIDTH, rows, lanes] = get(5) * (1.0 / 256.0)
            fields[CHAN, rows, lanes] = chan
            fields[ROUGH, rows, lanes] = get(7) * (1.0 / 8192.0) * wet - (1.0 - wet)
            return 0

        lax.fori_loop(0, TILE // BLOCK, block, 0)

    def copies(stage, chunk, axis, source, target, taken, put):
        base = (stage * CHUNKS + chunk) * 8
        remote = []
        if axis == "y":
            me = col
            steps = [4, 5, 2, 3, 6, 7, 1]
            partners = [((col + (d // 2) * 2) % NC) // 2 * 2 + (col + d % 2) % 2 for d in steps]
            devices = [place(own_x, own_z, c) for c in partners]
        elif axis == "x":
            me = own_x
            partners = [(own_x + d) % NX for d in (2, 1, 3)]
            devices = [place(x, own_z, col) for x in partners]
        else:
            me = own_z
            partners = [(own_z + d) % NZ for d in (2, 1, 3)]
            devices = [place(own_x, z, col) for z in partners]
        for q, (partner, device) in enumerate(zip(partners, devices)):
            remote.append(
                pltpu.make_async_remote_copy(
                    src_ref=part(source, taken, axis, partner),
                    dst_ref=part(target, put, axis, me),
                    send_sem=send_sem.at[base + q],
                    recv_sem=recv_sem.at[base + q],
                    device_id=device,
                    device_id_type=pl.DeviceIdType.MESH,
                )
            )
        local = pltpu.make_async_copy(
            part(source, taken, axis, me),
            part(target, put, axis, me),
            local_sem.at[stage * CHUNKS + chunk],
        )
        return remote, local

    started = []

    def launch(stage, chunk, axis, source, target, put=None):
        put = chunk if put is None else put
        remote, local = copies(stage, chunk, axis, source, target, chunk, put)
        for copy in remote:
            copy.start()
        local.start()
        started.extend(remote)
        return remote, local

    def landed(pair):
        remote, local = pair
        for copy in remote:
            copy.wait_recv()
        local.wait()

    middles = (middle_l, middle_r)
    encode(chunks[0])
    pl.semaphore_wait(barrier, len(greeted))
    flying = {}
    for chunk in chunks:
        if chunk != chunks[0]:
            encode(chunk)
        flying[chunk] = launch(0, chunk, FIRST[chunk // HALVES][0], coded, first_a)
    route = route_ref[...]
    target = (route[0:1] * NC + route[1:2]) * SLOTS + route[2:3]
    target = jnp.transpose(jnp.broadcast_to(target, (8, SLOTS * DEVICES)))[:, 0:1]
    old = lax.broadcasted_iota(jnp.int32, (SLOTS * DEVICES, LANES), 0)
    new = lax.broadcasted_iota(jnp.int32, (SLOTS * DEVICES, LANES), 1) * SLOTS
    device = jnp.right_shift(old * 171, 9)
    where_held = (old - device * SLOTS) * DEVICES + device
    source_rows[...] = jnp.zeros_like(source_rows)
    for slot in range(SLOTS):
        found = jnp.sum(jnp.where(new + slot == target, where_held, 0), axis=0, keepdims=True)
        source_rows[slot : slot + 1, :] = jnp.minimum(found, SLOTS * DEVICES - 1)
    to_scalars = pltpu.make_async_copy(source_rows, source_ref, source_sem)
    to_scalars.start()
    to_scalars.wait()
    opening = list(started)
    started.clear()
    for chunk in chunks:
        landed(flying[chunk])
        flying[chunk] = launch(1, chunk, FIRST[chunk // HALVES][1], first_a, first_b)
    for chunk in chunks:
        landed(flying[chunk])
        flying[chunk] = launch(
            2, chunk, FIRST[chunk // HALVES][2], first_b, middles[chunk % HALVES], chunk // HALVES
        )
    for copy in opening:
        copy.wait_send()
    ordered = coded.reshape(CHUNKS * DEVICES, BLOCK, LANES)
    for half in range(HALVES):
        group = chunks[half * SLOTS : (half + 1) * SLOTS]
        held = middles[half].reshape(SLOTS * DEVICES, BLOCK, LANES)
        for chunk in group:
            landed(flying[chunk])
        for chunk in group:
            slot = chunk // HALVES

            def move(k, _):
                for u in range(8):
                    d = k * 8 + u
                    ordered[chunk * DEVICES + d] = held[source_ref[slot, d]]
                return 0

            lax.fori_loop(0, DEVICES // 8, move, 0)
            flying[chunk] = launch(3, chunk, SECOND[slot][0], coded, second_a)
    for stage, source, target in ((4, second_a, second_b), (5, second_b, arrived)):
        for chunk in chunks:
            landed(flying[chunk])
            flying[chunk] = launch(stage, chunk, SECOND[chunk // HALVES][stage - 3], source, target)
    for chunk in chunks:
        landed(flying[chunk])
        decode(chunk)

    def rim(number, source, target, device):
        copy = pltpu.make_async_remote_copy(
            src_ref=source, dst_ref=target, send_sem=rim_send.at[number],
            recv_sem=rim_recv.at[number], device_id=device,
            device_id_type=pl.DeviceIdType.MESH,
        )
        copy.start()
        started.append(copy)
        return copy

    inner = pl.ds(0, COLS)
    outer = pl.ds(COLS, LANES)
    upper = lax.broadcasted_iota(jnp.int32, (PAD, COLS), 0) < REACH
    top_rows, bottom_rows = pl.ds(PAD, PAD), pl.ds(TILE, PAD)
    for pair in range(PAIRS):
        f, g = 2 * pair, min(2 * pair + 1, FIELDS - 1)
        turned = pltpu.roll(fields[g, top_rows, inner], REACH, 0)
        sent_n[pair] = jnp.where(upper, fields[f, top_rows, inner], turned)
        turned = pltpu.roll(fields[g, bottom_rows, inner], REACH, 0)
        sent_s[pair] = jnp.where(upper, turned, fields[f, bottom_rows, inner])
    ends = [rim(2, sent_n, got_s, north), rim(3, sent_s, got_n, south)]

    lane = lax.broadcasted_iota(jnp.int32, (TALL, LANES), 1)
    left = jnp.zeros((TALL, LANES), F32)
    right = jnp.zeros((TALL, LANES), F32)
    for k in range(TILE // TALL):
        rows = pl.ds(PAD + k * TALL, TALL)
        for f in range(FIELDS):
            start = FOLD * k + REACH * f
            here = (lane >= start) & (lane < start + REACH)
            low = fields[f, rows, pl.ds(0, LANES)]
            high = fields[f, rows, pl.ds(COLS - LANES, LANES)]
            left = jnp.where(here, pltpu.roll(low, start, 1) if start else low, left)
            right = jnp.where(here, pltpu.roll(high, start + REACH, 1), right)
    sent_w[...] = left
    sent_e[...] = right
    early, late = pl.ds(0, PAD), pl.ds(PAD + TILE, PAD)
    middle_rows, last_rows, next_rows = pl.ds(PAD, TALL), pl.ds(TALL - PAD, PAD), pl.ds(PAD + TALL, PAD)
    side = [
        rim(0, sent_w, got_e.at[middle_rows], west),
        rim(1, sent_e, got_w.at[middle_rows], east),
        rim(4, sent_w.at[early], got_e.at[next_rows], corners[0]),
        rim(5, sent_e.at[early], got_w.at[next_rows], corners[1]),
        rim(6, sent_w.at[last_rows], got_e.at[early], corners[2]),
        rim(7, sent_e.at[last_rows], got_w.at[early], corners[3]),
    ]

    row_of = lax.broadcasted_iota(jnp.int32, (8, LANES), 0)
    bottom = row_of == 7
    top = row_of == 0
    lanes_high = lax.broadcasted_iota(jnp.int32, (HIGH, LANES), 1)
    right_end = lanes_high == LANES - 1
    left_end = lanes_high == 0

    def strip(k, high=HIGH):
        return pl.ds(pl.multiple_of(k * high, 8), high)

    def below_strip(k, high=HIGH):
        return pl.ds(pl.multiple_of(jnp.minimum((k + 1) * high, ROWS - 8), 8), 8)

    def from_south(values, after):
        high = values.shape[0]
        moved = pltpu.roll(values, high - 1, 0)
        end = jnp.where(bottom, pltpu.roll(after, 7, 0), moved[high - 8 :])
        return jnp.concatenate([moved[: high - 8], end], 0) if high > 8 else end

    def from_north(values, before):
        moved = pltpu.roll(values, 1, 0)
        start = jnp.where(top, before, moved[:8])
        return (jnp.concatenate([start, moved[8:]], 0) if HIGH > 8 else start), moved[:8]

    def block(c):
        return pl.ds((c % BLOCKS) * LANES, LANES)

    def faces(k, c):
        here = strip(k, FACE_HIGH)
        there = below_strip(k, FACE_HIGH)
        last_lane = lax.broadcasted_iota(jnp.int32, (FACE_HIGH, LANES), 1) == LANES - 1
        water = fields[WATER, here, block(c)]
        bed, width = fields[BED, here, block(c)], fields[WIDTH, here, block(c)]
        chan, rough = fields[CHAN, here, block(c)], fields[ROUGH, here, block(c)]
        level[here, block(c)] = bed + water
        volume[here, block(c)] = (CELL / STEP) * width * jnp.minimum(water, chan) + (
            CELL * CELL / STEP
        ) * jnp.maximum(water - chan, 0.0)
        cap[here, block(c)] = (CELL / STEP) * width * chan
        inverse[here, block(c)] = (STEP / CELL) / width - STEP / (CELL * CELL)

        def to_east(f, v):
            after = pltpu.roll(fields[f, here, block(c + 1)], LANES - 1, 1)
            return jnp.where(last_lane, after, pltpu.roll(v, LANES - 1, 1))

        def to_south(f, v):
            return from_south(v, fields[f, there, block(c)])

        for shift, bed_f, part_f, deep_f, drag_f, gate_f, f, flow in (
            (to_east, bed_x, part_x, deep_x, drag_x, gate_x, FLOW_X, flow_x),
            (to_south, bed_y, part_y, deep_y, drag_y, gate_y, FLOW_Y, flow_y),
        ):
            bed_f[here, block(c)] = jnp.maximum(bed, shift(BED, bed))
            part_f[here, block(c)] = 1.0 - jnp.minimum(width, shift(WIDTH, width)) * (1.0 / CELL)
            deep_f[here, block(c)] = jnp.minimum(chan, shift(CHAN, chan))
            rough_n = shift(ROUGH, rough)
            mean = 0.5 * (rough + rough_n)
            wet = jnp.minimum(rough, rough_n) > 0
            drag_f[here, block(c)] = jnp.where(wet, (GRAV * STEP / CELL) * mean * mean, 0.0)
            gate_f[here, block(c)] = jnp.where(wet, GRAV * STEP, 0.0)
            flow[here, block(c)] = jnp.where(wet, fields[f, here, block(c)], 0.0)

    def many_faces(start, stop, blocks):
        def one(k, _):
            for c in blocks:
                faces(k, c)
            return 0

        lax.fori_loop(start, stop, one, 0)

    many_faces(1, TILE // FACE_HIGH, range(BLOCKS - 2))

    for copy in side:
        copy.wait_recv()
    at_east = col == NC - 1
    at_west = col == 0

    segments = [(early, early, FOLD * (TILE // TALL - 1)), (late, next_rows, 0)]
    segments += [(pl.ds(PAD + k * TALL, TALL), middle_rows, FOLD * k) for k in range(TILE // TALL)]
    for rows, got, fold in segments:
        from_e, from_w = got_e[got, :], got_w[got, :]
        at = lax.broadcasted_iota(jnp.int32, from_e.shape, 1)
        for f in range(FIELDS):
            start = fold + REACH * f
            low = pltpu.roll(from_e, LANES - start, 1) if start else from_e
            high = pltpu.roll(from_w, LANES - REACH - start, 1) if start < LANES - REACH else from_w
            if f == ROUGH:
                low = jnp.where(at_east, -1.0, low)
                high = jnp.where(at_west, -1.0, high)
            fill = 1.0 if f in (WIDTH, CHAN) else (-1.0 if f == ROUGH else 0.0)
            mixed = jnp.where(at < REACH, low, jnp.where(at >= LANES - REACH, high, fill))
            fields[f, rows, outer] = mixed

    many_faces(1, TILE // FACE_HIGH, range(BLOCKS - 2, BLOCKS))
    for copy in ends:
        copy.wait_recv()
    for pair in range(PAIRS):
        for got, rows in ((got_n, early), (got_s, late)):
            fields[2 * pair, rows, inner] = got[pair]
            if 2 * pair + 1 < FIELDS:
                fields[2 * pair + 1, rows, inner] = pltpu.roll(got[pair], REACH, 0)
    first = fields[ROUGH, pl.ds(0, 8), :]
    fields[ROUGH, pl.ds(0, 8), :] = jnp.where(row == 0, -1.0, first)
    last = fields[ROUGH, pl.ds(PAD + TILE, 8), :]
    fields[ROUGH, pl.ds(PAD + TILE, 8), :] = jnp.where(row == NX * NZ - 1, -1.0, last)
    many_faces(0, 1, range(BLOCKS))
    many_faces(TILE // FACE_HIGH, ROWS // FACE_HIGH, range(BLOCKS))

    def face_flow(flow, surface, surface_n, bed_f, part_f, deep_f, drag_f, gate_f):
        crest = jnp.maximum(surface, surface_n) - bed_f
        depth = crest - part_f * jnp.minimum(crest, deep_f)
        power = jnp.exp2(jnp.log(jnp.maximum(depth, RMIN)) * (-7.0 / 3.0 * LOG2_E))
        below = 1.0 + drag_f * jnp.abs(flow) * power
        guess = pl.reciprocal(below, approx=True)
        guess = guess * (2.0 - below * guess)
        return (flow - gate_f * depth * (surface_n - surface)) * guess

    every = range(BLOCKS)
    for step in range(ITERS):
        final = step == ITERS - 1

        def sweep(k, above):
            here = strip(k)
            there = below_strip(k)
            surface = [level[here, block(c)] for c in every]
            turned = [pltpu.roll(v, LANES - 1, 1) for v in surface]
            new_x = []
            for c in every:
                b = block(c)
                surface_e = jnp.where(right_end, turned[(c + 1) % BLOCKS], turned[c])
                new_x.append(
                    face_flow(
                        flow_x[here, b], surface[c], surface_e, bed_x[here, b], part_x[here, b],
                        deep_x[here, b], drag_x[here, b], gate_x[here, b],
                    )
                )
            passed = [pltpu.roll(v, 1, 1) for v in new_x]
            sunk = []
            for c in every:
                b = block(c)
                surface_s = from_south(surface[c], level[there, b])
                new_y = face_flow(
                    flow_y[here, b], surface[c], surface_s, bed_y[here, b], part_y[here, b],
                    deep_y[here, b], drag_y[here, b], gate_y[here, b],
                )
                from_n, end = from_north(new_y, above[c])
                sunk.append(end)
                from_w = jnp.where(left_end, passed[c - 1], passed[c])
                inflow = from_w - new_x[c] + from_n - new_y
                held = jnp.maximum(volume[here, b] + inflow, 0.0)
                water = jnp.minimum(held, cap[here, b]) * inverse[here, b] + held * (
                    STEP / (CELL * CELL)
                )
                if not final:
                    flow_x[here, b] = new_x[c]
                    flow_y[here, b] = new_y
                    volume[here, b] = held
                    level[here, b] = fields[BED, here, b] + water
                elif c < BLOCKS - 1:
                    water_out[here, b] = water
                    fx_out[here, b] = new_x[c]
                    fy_out[here, b] = new_y
            return tuple(sunk)

        carry = tuple(jnp.zeros((8, LANES), F32) for c in every)
        if not final:
            lax.fori_loop(0, STRIPS, sweep, carry)

    stores = []
    begin = 0
    sent = 0
    for piece in range(PARTS):
        end = -(-(PAD + (piece + 1) * (TILE // PARTS)) // HIGH)
        carry = lax.fori_loop(begin, end, sweep, carry)
        begin = end
        until = min(TILE, end * HIGH - PAD) if piece < PARTS - 1 else TILE
        size = until - sent
        for n, (ref, hbm) in enumerate(
            ((water_out, water_hbm), (fx_out, fx_out_hbm), (fy_out, fy_out_hbm))
        ):
            copy = pltpu.make_async_copy(
                ref.at[pl.ds(PAD + sent, size)], hbm.at[pl.ds(sent, size)], out_sem.at[piece * 3 + n]
            )
            copy.start()
            stores.append(copy)
        sent = until
    for copy in stores:
        copy.wait()
    for copy in started:
        copy.wait_send()


def body(depth, flow_x, flow_y, floor, width, chan, rough, route, wet_tiles):
    whole = pl.BlockSpec(memory_space=pl.ANY)
    smem = pl.BlockSpec(memory_space=pltpu.SMEM)
    pieces = pltpu.VMEM(PIECES, jnp.int16)
    grid = pltpu.VMEM((ROWS, WIDE), F32)
    edge = pltpu.VMEM((TALL, LANES), F32)
    out = jax.ShapeDtypeStruct((TILE, COLS), F32)
    operands = (depth, flow_x, flow_y, floor, width, chan, rough)
    return pl.pallas_call(
        migrate_and_route,
        out_shape=(out, out, out),
        in_specs=[whole] * 7 + [pl.BlockSpec(memory_space=pltpu.VMEM), smem],
        out_specs=(whole, whole, whole),
        scratch_shapes=[pltpu.VMEM(a.shape, a.dtype) for a in operands]
        + [pltpu.VMEM((ROWS, COLS), F32)] * 3
        + [pieces] * 3
        + [pltpu.VMEM((SLOTS,) + PIECES[1:], jnp.int16)] * 2
        + [pieces] * 3
        + [pltpu.VMEM((FIELDS, ROWS, WIDE), F32)]
        + [edge] * 2
        + [pltpu.VMEM((TALL + 2 * PAD, LANES), F32)] * 2
        + [pltpu.VMEM((PAIRS, PAD, COLS), F32)] * 4
        + [grid] * 16
        + [pltpu.VMEM((8, LANES), jnp.int32), pltpu.SMEM((8, LANES), jnp.int32)]
        + [
            pltpu.SemaphoreType.DMA((6 * CHUNKS * 8,)),
            pltpu.SemaphoreType.DMA((6 * CHUNKS * 8,)),
            pltpu.SemaphoreType.DMA((6 * CHUNKS,)),
            pltpu.SemaphoreType.DMA((8,)),
            pltpu.SemaphoreType.DMA((8,)),
            pltpu.SemaphoreType.DMA((CHUNKS * FIELDS,)),
            pltpu.SemaphoreType.DMA((PARTS * 3,)),
            pltpu.SemaphoreType.DMA,
        ],
        compiler_params=pltpu.CompilerParams(
            collective_id=0, has_side_effects=True, vmem_limit_bytes=58 * 2**20
        ),
    )(*operands, route.T, wet_tiles)


def solution(mesh):
    tiles = P(("row", "col"), None, None)
    block = P("row", "col")
    return jax.shard_map(
        body,
        mesh=mesh,
        in_specs=(tiles,) * 7 + (P(), block),
        out_specs=(block, block, block),
        check_vma=False,
    )
```

```python
import jax
import jax.numpy as jnp
from jax import lax
from jax.experimental import pallas as pl
from jax.experimental.pallas import tpu as pltpu
from jax.sharding import PartitionSpec as P

ITERS = 4
GRAV = 9.81
CELL = 5.0
STEP = 0.1
RMIN = 0.1

NX, NZ, NC = 4, 4, 8
DEVICES = NX * NZ * NC
SLOTS = 3
HALVES = 2
CHUNKS = SLOTS * HALVES
TILE = 256
BLOCK = 16
LANES = 128
FIRST = ("yxz", "xzy", "zyx")
SECOND = ("zxy", "yzx", "xyz")
PIECES = (CHUNKS, NX, NZ, NC, BLOCK, LANES)

PAD = 8
HIGH = 96
STRIPS = -(-(TILE + 2 * PAD) // HIGH)
ROWS = STRIPS * HIGH
COLS = SLOTS * TILE
WIDE = COLS + LANES
REACH = 4
FIELDS = 7
BLOCKS = WIDE // LANES
PARTS = 2
TALL = 64
FOLD = 32
FACE_HIGH = 32
PAIRS = (FIELDS + 1) // 2
LOG2_E = 1.4426950408889634
WATER, FLOW_X, FLOW_Y, BED, WIDTH, CHAN, ROUGH = range(FIELDS)
F32 = jnp.float32


def to_code(values):
    return values.astype(jnp.int32).astype(jnp.int16)


def flow_code(flow):
    root = jnp.sqrt(jnp.sqrt(jnp.abs(flow) * 0.25))
    size = jnp.minimum(root * 32767.0 + 0.5, 32767.0).astype(jnp.int32)
    return jnp.where(flow < 0, -size, size).astype(jnp.int16)


def flow_value(code):
    return (code * code) * (code * jnp.abs(code)) * (4.0 / 32767.0**4)


def floor_code(floor):
    coarse = (floor * 65536.0).astype(jnp.int32)
    fine = -((floor * 16777216.0 + 0.5).astype(jnp.int32))
    return jnp.where(floor < 2.0**-9, fine, coarse).astype(jnp.int16)


def floor_value(code):
    return jnp.where(code < 0, code * -(2.0**-24), code * 2.0**-16)


def part(ref, chunk, axis, index):
    if axis == "x":
        return ref.at[chunk, index]
    if axis == "z":
        return ref.at[chunk, :, index]
    return ref.at[chunk, :, :, index]


def migrate_and_route(
    depth_hbm, fx_hbm, fy_hbm, floor_hbm, width_hbm, chan_hbm, rough_hbm, route_ref, wet_ref,
    water_hbm, fx_out_hbm, fy_out_hbm,
    depth_ref, fx_ref, fy_ref, floor_ref, width_ref, chan_ref, rough_ref,
    water_out, fx_out, fy_out,
    coded, first_a, first_b, middle_l, middle_r, second_a, second_b, arrived,
    fields, sent_w, sent_e, got_e, got_w, sent_n, sent_s, got_n, got_s, level, volume, cap, inverse, flow_x, flow_y,
    bed_x, part_x, deep_x, drag_x, gate_x, bed_y, part_y, deep_y, drag_y, gate_y,
    source_rows, source_ref, send_sem, recv_sem, local_sem, rim_send, rim_recv, in_sem, out_sem,
    source_sem,
):
    row = lax.axis_index("row")
    col = lax.axis_index("col")
    own_x = row // NZ
    own_z = row % NZ

    def place(x, z, c):
        return (x * NZ + z, c)

    west = (row, (col + NC - 1) % NC)
    east = (row, (col + 1) % NC)
    north = ((row + NX * NZ - 1) % (NX * NZ), col)
    south = ((row + 1) % (NX * NZ), col)

    corners = [(north[0], west[1]), (north[0], east[1]), (south[0], west[1]), (south[0], east[1])]

    barrier = pltpu.get_barrier_semaphore()
    greeted = [place((own_x + d) % NX, own_z, col) for d in (1, 2, 3)]
    greeted += [place(own_x, (own_z + d) % NZ, col) for d in (1, 2, 3)]
    greeted += [place(own_x, own_z, (col + d) % NC) for d in range(1, NC)]
    greeted += [north, south] + corners
    for device in greeted:
        pl.semaphore_signal(barrier, inc=1, device_id=device, device_id_type=pl.DeviceIdType.MESH)

    chunks = [slot * HALVES + half for half in range(HALVES) for slot in range(SLOTS)]
    pairs = (
        (depth_hbm, depth_ref), (fx_hbm, fx_ref), (fy_hbm, fy_ref), (floor_hbm, floor_ref),
        (width_hbm, width_ref), (chan_hbm, chan_ref), (rough_hbm, rough_ref),
    )
    loads = {}
    for chunk in chunks:
        slot, lanes = chunk // HALVES, pl.ds(chunk % HALVES * LANES, LANES)
        loads[chunk] = [
            pltpu.make_async_copy(
                hbm.at[slot, :, lanes], ref.at[slot, :, lanes], in_sem.at[chunk * FIELDS + n]
            )
            for n, (hbm, ref) in enumerate(pairs)
        ]
        for copy in loads[chunk]:
            copy.start()

    def encode(chunk):
        slot, half = chunk // HALVES, chunk % HALVES
        lanes = pl.ds(half * LANES, LANES)
        for copy in loads[chunk]:
            copy.wait()

        def block(b, _):
            rows = pl.ds(pl.multiple_of(b * BLOCK, BLOCK), BLOCK)

            def put(plane, code):
                coded[chunk, b // NZ, b % NZ, plane] = code

            depth = depth_ref[slot, rows, lanes] * 16384.0
            high = depth.astype(jnp.int32)
            low = ((depth - high.astype(F32)) * 65536.0).astype(jnp.int32) - 32768
            put(0, high.astype(jnp.int16))
            put(1, low.astype(jnp.int16))
            put(2, flow_code(fx_ref[slot, rows, lanes]))
            put(3, flow_code(fy_ref[slot, rows, lanes]))
            put(4, floor_code(floor_ref[slot, rows, lanes].astype(F32)))
            put(5, to_code(width_ref[slot, rows, lanes].astype(F32) * 256.0))
            put(6, to_code(chan_ref[slot, rows, lanes].astype(F32) * 256.0))
            put(7, to_code(rough_ref[slot, rows, lanes].astype(F32) * 8192.0))
            return 0

        lax.fori_loop(0, TILE // BLOCK, block, 0, unroll=2)

    def decode(chunk):
        slot, half = chunk // HALVES, chunk % HALVES
        lanes = pl.ds(slot * TILE + half * LANES, LANES)
        wet = wet_ref[0, slot].astype(F32)

        def block(b, _):
            rows = pl.ds(pl.multiple_of(PAD + b * BLOCK, 8), BLOCK)

            def get(plane):
                return arrived[chunk, b // NZ, b % NZ, plane].astype(jnp.int32).astype(F32)

            chan = get(6) * (1.0 / 256.0)
            fields[WATER, rows, lanes] = get(0) * 2.0**-14 + (get(1) + 32768.0) * 2.0**-30
            fields[FLOW_X, rows, lanes] = flow_value(get(2))
            fields[FLOW_Y, rows, lanes] = flow_value(get(3))
            fields[BED, rows, lanes] = floor_value(get(4)) - chan
            fields[WIDTH, rows, lanes] = get(5) * (1.0 / 256.0)
            fields[CHAN, rows, lanes] = chan
            fields[ROUGH, rows, lanes] = get(7) * (1.0 / 8192.0) * wet - (1.0 - wet)
            return 0

        lax.fori_loop(0, TILE // BLOCK, block, 0, unroll=4)

    def copies(stage, chunk, axis, source, target, taken, put):
        base = (stage * CHUNKS + chunk) * 8
        remote = []
        if axis == "y":
            me = col
            steps = [4, 5, 2, 3, 6, 7, 1]
            partners = [((col + (d // 2) * 2) % NC) // 2 * 2 + (col + d % 2) % 2 for d in steps]
            devices = [place(own_x, own_z, c) for c in partners]
        elif axis == "x":
            me = own_x
            partners = [(own_x + d) % NX for d in (2, 1, 3)]
            devices = [place(x, own_z, col) for x in partners]
        else:
            me = own_z
            partners = [(own_z + d) % NZ for d in (2, 1, 3)]
            devices = [place(own_x, z, col) for z in partners]
        for q, (partner, device) in enumerate(zip(partners, devices)):
            remote.append(
                pltpu.make_async_remote_copy(
                    src_ref=part(source, taken, axis, partner),
                    dst_ref=part(target, put, axis, me),
                    send_sem=send_sem.at[base + q],
                    recv_sem=recv_sem.at[base + q],
                    device_id=device,
                    device_id_type=pl.DeviceIdType.MESH,
                )
            )
        local = pltpu.make_async_copy(
            part(source, taken, axis, me),
            part(target, put, axis, me),
            local_sem.at[stage * CHUNKS + chunk],
        )
        return remote, local

    started = []

    def launch(stage, chunk, axis, source, target, put=None):
        put = chunk if put is None else put
        remote, local = copies(stage, chunk, axis, source, target, chunk, put)
        for copy in remote:
            copy.start()
        local.start()
        started.extend(remote)
        return remote, local

    def landed(pair):
        remote, local = pair
        for copy in remote:
            copy.wait_recv()
        local.wait()

    middles = (middle_l, middle_r)
    encode(chunks[0])
    pl.semaphore_wait(barrier, len(greeted))
    flying = {}
    for chunk in chunks:
        if chunk != chunks[0]:
            encode(chunk)
        flying[chunk] = launch(0, chunk, FIRST[chunk // HALVES][0], coded, first_a)
    route = route_ref[...]
    target = (route[0:1] * NC + route[1:2]) * SLOTS + route[2:3]
    target = jnp.transpose(jnp.broadcast_to(target, (8, SLOTS * DEVICES)))[:, 0:1]
    old = lax.broadcasted_iota(jnp.int32, (SLOTS * DEVICES, LANES), 0)
    new = lax.broadcasted_iota(jnp.int32, (SLOTS * DEVICES, LANES), 1) * SLOTS
    device = jnp.right_shift(old * 171, 9)
    where_held = (old - device * SLOTS) * DEVICES + device
    source_rows[...] = jnp.zeros_like(source_rows)
    for slot in range(SLOTS):
        found = jnp.sum(jnp.where(new + slot == target, where_held, 0), axis=0, keepdims=True)
        source_rows[slot : slot + 1, :] = jnp.minimum(found, SLOTS * DEVICES - 1)
    to_scalars = pltpu.make_async_copy(source_rows, source_ref, source_sem)
    to_scalars.start()
    to_scalars.wait()
    opening = list(started)
    started.clear()
    for chunk in chunks:
        landed(flying[chunk])
        flying[chunk] = launch(1, chunk, FIRST[chunk // HALVES][1], first_a, first_b)
    for chunk in chunks:
        landed(flying[chunk])
        flying[chunk] = launch(
            2, chunk, FIRST[chunk // HALVES][2], first_b, middles[chunk % HALVES], chunk // HALVES
        )
    for copy in opening:
        copy.wait_send()
    ordered = coded.reshape(CHUNKS * DEVICES, BLOCK, LANES)
    for half in range(HALVES):
        group = chunks[half * SLOTS : (half + 1) * SLOTS]
        held = middles[half].reshape(SLOTS * DEVICES, BLOCK, LANES)
        for chunk in group:
            landed(flying[chunk])
        for chunk in group:
            slot = chunk // HALVES

            def move(k, _):
                for u in range(8):
                    d = k * 8 + u
                    ordered[chunk * DEVICES + d] = held[source_ref[slot, d]]
                return 0

            lax.fori_loop(0, DEVICES // 8, move, 0)
            flying[chunk] = launch(3, chunk, SECOND[slot][0], coded, second_a)
    for stage, source, target in ((4, second_a, second_b), (5, second_b, arrived)):
        for chunk in chunks:
            landed(flying[chunk])
            flying[chunk] = launch(stage, chunk, SECOND[chunk // HALVES][stage - 3], source, target)
    for chunk in chunks:
        landed(flying[chunk])
        decode(chunk)

    def rim(number, source, target, device):
        copy = pltpu.make_async_remote_copy(
            src_ref=source, dst_ref=target, send_sem=rim_send.at[number],
            recv_sem=rim_recv.at[number], device_id=device,
            device_id_type=pl.DeviceIdType.MESH,
        )
        copy.start()
        started.append(copy)
        return copy

    inner = pl.ds(0, COLS)
    outer = pl.ds(COLS, LANES)
    upper = lax.broadcasted_iota(jnp.int32, (PAD, COLS), 0) < REACH
    top_rows, bottom_rows = pl.ds(PAD, PAD), pl.ds(TILE, PAD)
    for pair in range(PAIRS):
        f, g = 2 * pair, min(2 * pair + 1, FIELDS - 1)
        turned = pltpu.roll(fields[g, top_rows, inner], REACH, 0)
        sent_n[pair] = jnp.where(upper, fields[f, top_rows, inner], turned)
        turned = pltpu.roll(fields[g, bottom_rows, inner], REACH, 0)
        sent_s[pair] = jnp.where(upper, turned, fields[f, bottom_rows, inner])
    ends = [rim(2, sent_n, got_s, north), rim(3, sent_s, got_n, south)]

    lane = lax.broadcasted_iota(jnp.int32, (TALL, LANES), 1)
    left = jnp.zeros((TALL, LANES), F32)
    right = jnp.zeros((TALL, LANES), F32)
    for k in range(TILE // TALL):
        rows = pl.ds(PAD + k * TALL, TALL)
        for f in range(FIELDS):
            start = FOLD * k + REACH * f
            here = (lane >= start) & (lane < start + REACH)
            low = fields[f, rows, pl.ds(0, LANES)]
            high = fields[f, rows, pl.ds(COLS - LANES, LANES)]
            left = jnp.where(here, pltpu.roll(low, start, 1) if start else low, left)
            right = jnp.where(here, pltpu.roll(high, start + REACH, 1), right)
    sent_w[...] = left
    sent_e[...] = right
    early, late = pl.ds(0, PAD), pl.ds(PAD + TILE, PAD)
    middle_rows, last_rows, next_rows = pl.ds(PAD, TALL), pl.ds(TALL - PAD, PAD), pl.ds(PAD + TALL, PAD)
    side = [
        rim(0, sent_w, got_e.at[middle_rows], west),
        rim(1, sent_e, got_w.at[middle_rows], east),
        rim(4, sent_w.at[early], got_e.at[next_rows], corners[0]),
        rim(5, sent_e.at[early], got_w.at[next_rows], corners[1]),
        rim(6, sent_w.at[last_rows], got_e.at[early], corners[2]),
        rim(7, sent_e.at[last_rows], got_w.at[early], corners[3]),
    ]

    row_of = lax.broadcasted_iota(jnp.int32, (8, LANES), 0)
    bottom = row_of == 7
    top = row_of == 0
    lanes_high = lax.broadcasted_iota(jnp.int32, (HIGH, LANES), 1)
    right_end = lanes_high == LANES - 1
    left_end = lanes_high == 0

    def strip(k, high=HIGH):
        return pl.ds(pl.multiple_of(k * high, 8), high)

    def below_strip(k, high=HIGH):
        return pl.ds(pl.multiple_of(jnp.minimum((k + 1) * high, ROWS - 8), 8), 8)

    def from_south(values, after):
        high = values.shape[0]
        moved = pltpu.roll(values, high - 1, 0)
        end = jnp.where(bottom, pltpu.roll(after, 7, 0), moved[high - 8 :])
        return jnp.concatenate([moved[: high - 8], end], 0) if high > 8 else end

    def from_north(values, before):
        moved = pltpu.roll(values, 1, 0)
        start = jnp.where(top, before, moved[:8])
        return (jnp.concatenate([start, moved[8:]], 0) if HIGH > 8 else start), moved[:8]

    def block(c):
        return pl.ds((c % BLOCKS) * LANES, LANES)

    def faces(k, c):
        here = strip(k, FACE_HIGH)
        there = below_strip(k, FACE_HIGH)
        last_lane = lax.broadcasted_iota(jnp.int32, (FACE_HIGH, LANES), 1) == LANES - 1
        water = fields[WATER, here, block(c)]
        bed, width = fields[BED, here, block(c)], fields[WIDTH, here, block(c)]
        chan, rough = fields[CHAN, here, block(c)], fields[ROUGH, here, block(c)]
        level[here, block(c)] = bed + water
        volume[here, block(c)] = (CELL / STEP) * width * jnp.minimum(water, chan) + (
            CELL * CELL / STEP
        ) * jnp.maximum(water - chan, 0.0)
        cap[here, block(c)] = (CELL / STEP) * width * chan
        inverse[here, block(c)] = (STEP / CELL) / width - STEP / (CELL * CELL)

        def to_east(f, v):
            after = pltpu.roll(fields[f, here, block(c + 1)], LANES - 1, 1)
            return jnp.where(last_lane, after, pltpu.roll(v, LANES - 1, 1))

        def to_south(f, v):
            return from_south(v, fields[f, there, block(c)])

        for shift, bed_f, part_f, deep_f, drag_f, gate_f, f, flow in (
            (to_east, bed_x, part_x, deep_x, drag_x, gate_x, FLOW_X, flow_x),
            (to_south, bed_y, part_y, deep_y, drag_y, gate_y, FLOW_Y, flow_y),
        ):
            bed_f[here, block(c)] = jnp.maximum(bed, shift(BED, bed))
            part_f[here, block(c)] = 1.0 - jnp.minimum(width, shift(WIDTH, width)) * (1.0 / CELL)
            deep_f[here, block(c)] = jnp.minimum(chan, shift(CHAN, chan))
            rough_n = shift(ROUGH, rough)
            mean = 0.5 * (rough + rough_n)
            wet = jnp.minimum(rough, rough_n) > 0
            drag_f[here, block(c)] = jnp.where(wet, (GRAV * STEP / CELL) * mean * mean, 0.0)
            gate_f[here, block(c)] = jnp.where(wet, GRAV * STEP, 0.0)
            flow[here, block(c)] = jnp.where(wet, fields[f, here, block(c)], 0.0)

    def many_faces(start, stop, blocks):
        def one(k, _):
            for c in blocks:
                faces(k, c)
            return 0

        lax.fori_loop(start, stop, one, 0)

    many_faces(1, TILE // FACE_HIGH, range(BLOCKS - 2))

    for copy in side:
        copy.wait_recv()
    at_east = col == NC - 1
    at_west = col == 0

    segments = [(early, early, FOLD * (TILE // TALL - 1)), (late, next_rows, 0)]
    segments += [(pl.ds(PAD + k * TALL, TALL), middle_rows, FOLD * k) for k in range(TILE // TALL)]
    for rows, got, fold in segments:
        from_e, from_w = got_e[got, :], got_w[got, :]
        at = lax.broadcasted_iota(jnp.int32, from_e.shape, 1)
        for f in range(FIELDS):
            start = fold + REACH * f
            low = pltpu.roll(from_e, LANES - start, 1) if start else from_e
            high = pltpu.roll(from_w, LANES - REACH - start, 1) if start < LANES - REACH else from_w
            if f == ROUGH:
                low = jnp.where(at_east, -1.0, low)
                high = jnp.where(at_west, -1.0, high)
            fill = 1.0 if f in (WIDTH, CHAN) else (-1.0 if f == ROUGH else 0.0)
            mixed = jnp.where(at < REACH, low, jnp.where(at >= LANES - REACH, high, fill))
            fields[f, rows, outer] = mixed

    many_faces(1, TILE // FACE_HIGH, range(BLOCKS - 2, BLOCKS))
    for copy in ends:
        copy.wait_recv()
    for pair in range(PAIRS):
        for got, rows in ((got_n, early), (got_s, late)):
            fields[2 * pair, rows, inner] = got[pair]
            if 2 * pair + 1 < FIELDS:
                fields[2 * pair + 1, rows, inner] = pltpu.roll(got[pair], REACH, 0)
    first = fields[ROUGH, pl.ds(0, 8), :]
    fields[ROUGH, pl.ds(0, 8), :] = jnp.where(row == 0, -1.0, first)
    last = fields[ROUGH, pl.ds(PAD + TILE, 8), :]
    fields[ROUGH, pl.ds(PAD + TILE, 8), :] = jnp.where(row == NX * NZ - 1, -1.0, last)
    many_faces(0, 1, range(BLOCKS))
    many_faces(TILE // FACE_HIGH, ROWS // FACE_HIGH, range(BLOCKS))

    def face_flow(flow, surface, surface_n, bed_f, part_f, deep_f, drag_f, gate_f):
        crest = jnp.maximum(surface, surface_n) - bed_f
        depth = crest - part_f * jnp.minimum(crest, deep_f)
        power = jnp.exp2(jnp.log(jnp.maximum(depth, RMIN)) * (-7.0 / 3.0 * LOG2_E))
        below = 1.0 + drag_f * jnp.abs(flow) * power
        guess = pl.reciprocal(below, approx=True)
        guess = guess * (2.0 - below * guess)
        return (flow - gate_f * depth * (surface_n - surface)) * guess

    every = range(BLOCKS)
    for step in range(ITERS):
        final = step == ITERS - 1

        def sweep(k, above):
            here = strip(k)
            there = below_strip(k)
            surface = [level[here, block(c)] for c in every]
            turned = [pltpu.roll(v, LANES - 1, 1) for v in surface]
            new_x = []
            for c in every:
                b = block(c)
                surface_e = jnp.where(right_end, turned[(c + 1) % BLOCKS], turned[c])
                new_x.append(
                    face_flow(
                        flow_x[here, b], surface[c], surface_e, bed_x[here, b], part_x[here, b],
                        deep_x[here, b], drag_x[here, b], gate_x[here, b],
                    )
                )
            passed = [pltpu.roll(v, 1, 1) for v in new_x]
            sunk = []
            for c in every:
                b = block(c)
                surface_s = from_south(surface[c], level[there, b])
                new_y = face_flow(
                    flow_y[here, b], surface[c], surface_s, bed_y[here, b], part_y[here, b],
                    deep_y[here, b], drag_y[here, b], gate_y[here, b],
                )
                from_n, end = from_north(new_y, above[c])
                sunk.append(end)
                from_w = jnp.where(left_end, passed[c - 1], passed[c])
                inflow = from_w - new_x[c] + from_n - new_y
                held = jnp.maximum(volume[here, b] + inflow, 0.0)
                water = jnp.minimum(held, cap[here, b]) * inverse[here, b] + held * (
                    STEP / (CELL * CELL)
                )
                if not final:
                    flow_x[here, b] = new_x[c]
                    flow_y[here, b] = new_y
                    volume[here, b] = held
                    level[here, b] = fields[BED, here, b] + water
                elif c < BLOCKS - 1:
                    water_out[here, b] = water
                    fx_out[here, b] = new_x[c]
                    fy_out[here, b] = new_y
            return tuple(sunk)

        carry = tuple(jnp.zeros((8, LANES), F32) for c in every)
        if not final:
            lax.fori_loop(0, STRIPS, sweep, carry)

    stores = []
    begin = 0
    sent = 0
    for piece in range(PARTS):
        end = -(-(PAD + (piece + 1) * (TILE // PARTS)) // HIGH)
        carry = lax.fori_loop(begin, end, sweep, carry)
        begin = end
        until = min(TILE, end * HIGH - PAD) if piece < PARTS - 1 else TILE
        size = until - sent
        for n, (ref, hbm) in enumerate(
            ((water_out, water_hbm), (fx_out, fx_out_hbm), (fy_out, fy_out_hbm))
        ):
            copy = pltpu.make_async_copy(
                ref.at[pl.ds(PAD + sent, size)], hbm.at[pl.ds(sent, size)], out_sem.at[piece * 3 + n]
            )
            copy.start()
            stores.append(copy)
        sent = until
    for copy in stores:
        copy.wait()
    for copy in started:
        copy.wait_send()


def body(depth, flow_x, flow_y, floor, width, chan, rough, route, wet_tiles):
    whole = pl.BlockSpec(memory_space=pl.ANY)
    smem = pl.BlockSpec(memory_space=pltpu.SMEM)
    pieces = pltpu.VMEM(PIECES, jnp.int16)
    grid = pltpu.VMEM((ROWS, WIDE), F32)
    edge = pltpu.VMEM((TALL, LANES), F32)
    out = jax.ShapeDtypeStruct((TILE, COLS), F32)
    operands = (depth, flow_x, flow_y, floor, width, chan, rough)
    return pl.pallas_call(
        migrate_and_route,
        out_shape=(out, out, out),
        in_specs=[whole] * 7 + [pl.BlockSpec(memory_space=pltpu.VMEM), smem],
        out_specs=(whole, whole, whole),
        scratch_shapes=[pltpu.VMEM(a.shape, a.dtype) for a in operands]
        + [pltpu.VMEM((ROWS, COLS), F32)] * 3
        + [pieces] * 3
        + [pltpu.VMEM((SLOTS,) + PIECES[1:], jnp.int16)] * 2
        + [pieces] * 3
        + [pltpu.VMEM((FIELDS, ROWS, WIDE), F32)]
        + [edge] * 2
        + [pltpu.VMEM((TALL + 2 * PAD, LANES), F32)] * 2
        + [pltpu.VMEM((PAIRS, PAD, COLS), F32)] * 4
        + [grid] * 16
        + [pltpu.VMEM((8, LANES), jnp.int32), pltpu.SMEM((8, LANES), jnp.int32)]
        + [
            pltpu.SemaphoreType.DMA((6 * CHUNKS * 8,)),
            pltpu.SemaphoreType.DMA((6 * CHUNKS * 8,)),
            pltpu.SemaphoreType.DMA((6 * CHUNKS,)),
            pltpu.SemaphoreType.DMA((8,)),
            pltpu.SemaphoreType.DMA((8,)),
            pltpu.SemaphoreType.DMA((CHUNKS * FIELDS,)),
            pltpu.SemaphoreType.DMA((PARTS * 3,)),
            pltpu.SemaphoreType.DMA,
        ],
        compiler_params=pltpu.CompilerParams(
            collective_id=0, has_side_effects=True, vmem_limit_bytes=58 * 2**20
        ),
    )(*operands, route.T, wet_tiles)


def solution(mesh):
    tiles = P(("row", "col"), None, None)
    block = P("row", "col")
    return jax.shard_map(
        body,
        mesh=mesh,
        in_specs=(tiles,) * 7 + (P(), block),
        out_specs=(block, block, block),
        check_vma=False,
    )
```

```python
import jax
import jax.numpy as jnp
from jax import lax
from jax.experimental import pallas as pl
from jax.experimental.pallas import tpu as pltpu
from jax.sharding import PartitionSpec as P

ITERS = 4
GRAV = 9.81
CELL = 5.0
STEP = 0.1
RMIN = 0.1

NX, NZ, NC = 4, 4, 8
DEVICES = NX * NZ * NC
SLOTS = 3
HALVES = 2
CHUNKS = SLOTS * HALVES
TILE = 256
BLOCK = 16
LANES = 128
FIRST = ("yxz", "xzy", "zyx")
SECOND = ("zxy", "yzx", "xyz")
PIECES = (CHUNKS, NX, NZ, NC, BLOCK, LANES)

PAD = 8
HIGH = 96
STRIPS = -(-(TILE + 2 * PAD) // HIGH)
ROWS = STRIPS * HIGH
COLS = SLOTS * TILE
WIDE = COLS + LANES
REACH = 4
FIELDS = 7
BLOCKS = WIDE // LANES
PARTS = 2
TALL = 64
FOLD = 32
FACE_HIGH = 32
PAIRS = (FIELDS + 1) // 2
LOG2_E = 1.4426950408889634
WATER, FLOW_X, FLOW_Y, BED, WIDTH, CHAN, ROUGH = range(FIELDS)
F32 = jnp.float32


def to_code(values):
    return values.astype(jnp.int32).astype(jnp.int16)


def flow_code(flow):
    root = jnp.sqrt(jnp.sqrt(jnp.abs(flow) * 0.25))
    size = jnp.minimum(root * 32767.0 + 0.5, 32767.0).astype(jnp.int32)
    return jnp.where(flow < 0, -size, size).astype(jnp.int16)


def flow_value(code):
    return (code * code) * (code * jnp.abs(code)) * (4.0 / 32767.0**4)


def floor_code(floor):
    coarse = (floor * 65536.0).astype(jnp.int32)
    fine = -((floor * 16777216.0 + 0.5).astype(jnp.int32))
    return jnp.where(floor < 2.0**-9, fine, coarse).astype(jnp.int16)


def floor_value(code):
    return jnp.where(code < 0, code * -(2.0**-24), code * 2.0**-16)


def part(ref, chunk, axis, index):
    if axis == "x":
        return ref.at[chunk, index]
    if axis == "z":
        return ref.at[chunk, :, index]
    return ref.at[chunk, :, :, index]


def migrate_and_route(
    depth_hbm, fx_hbm, fy_hbm, floor_hbm, width_hbm, chan_hbm, rough_hbm, route_ref, wet_ref,
    water_hbm, fx_out_hbm, fy_out_hbm,
    depth_ref, fx_ref, fy_ref, floor_ref, width_ref, chan_ref, rough_ref,
    water_out, fx_out, fy_out,
    coded, first_a, first_b, middle_l, middle_r, second_a, second_b, arrived,
    fields, sent_w, sent_e, got_e, got_w, sent_n, sent_s, got_n, got_s, level, volume, cap, inverse, flow_x, flow_y,
    bed_x, part_x, deep_x, drag_x, gate_x, bed_y, part_y, deep_y, drag_y, gate_y,
    source_rows, source_ref, send_sem, recv_sem, local_sem, rim_send, rim_recv, in_sem, out_sem,
    source_sem,
):
    row = lax.axis_index("row")
    col = lax.axis_index("col")
    own_x = row // NZ
    own_z = row % NZ

    def place(x, z, c):
        return (x * NZ + z, c)

    west = (row, (col + NC - 1) % NC)
    east = (row, (col + 1) % NC)
    north = ((row + NX * NZ - 1) % (NX * NZ), col)
    south = ((row + 1) % (NX * NZ), col)

    corners = [(north[0], west[1]), (north[0], east[1]), (south[0], west[1]), (south[0], east[1])]

    barrier = pltpu.get_barrier_semaphore()
    greeted = [place((own_x + d) % NX, own_z, col) for d in (1, 2, 3)]
    greeted += [place(own_x, (own_z + d) % NZ, col) for d in (1, 2, 3)]
    greeted += [place(own_x, own_z, (col + d) % NC) for d in range(1, NC)]
    greeted += [north, south] + corners
    for device in greeted:
        pl.semaphore_signal(barrier, inc=1, device_id=device, device_id_type=pl.DeviceIdType.MESH)

    chunks = [slot * HALVES + half for half in range(HALVES) for slot in range(SLOTS)]
    pairs = (
        (depth_hbm, depth_ref), (fx_hbm, fx_ref), (fy_hbm, fy_ref), (floor_hbm, floor_ref),
        (width_hbm, width_ref), (chan_hbm, chan_ref), (rough_hbm, rough_ref),
    )
    loads = {}
    for chunk in chunks:
        slot, lanes = chunk // HALVES, pl.ds(chunk % HALVES * LANES, LANES)
        loads[chunk] = [
            pltpu.make_async_copy(
                hbm.at[slot, :, lanes], ref.at[slot, :, lanes], in_sem.at[chunk * FIELDS + n]
            )
            for n, (hbm, ref) in enumerate(pairs)
        ]
        for copy in loads[chunk]:
            copy.start()

    def encode(chunk):
        slot, half = chunk // HALVES, chunk % HALVES
        lanes = pl.ds(half * LANES, LANES)
        for copy in loads[chunk]:
            copy.wait()

        def block(b, _):
            rows = pl.ds(pl.multiple_of(b * BLOCK, BLOCK), BLOCK)

            def put(plane, code):
                coded[chunk, b // NZ, b % NZ, plane] = code

            depth = depth_ref[slot, rows, lanes] * 16384.0
            high = depth.astype(jnp.int32)
            low = ((depth - high.astype(F32)) * 65536.0).astype(jnp.int32) - 32768
            put(0, high.astype(jnp.int16))
            put(1, low.astype(jnp.int16))
            put(2, flow_code(fx_ref[slot, rows, lanes]))
            put(3, flow_code(fy_ref[slot, rows, lanes]))
            put(4, floor_code(floor_ref[slot, rows, lanes].astype(F32)))
            put(5, to_code(width_ref[slot, rows, lanes].astype(F32) * 256.0))
            put(6, to_code(chan_ref[slot, rows, lanes].astype(F32) * 256.0))
            put(7, to_code(rough_ref[slot, rows, lanes].astype(F32) * 8192.0))
            return 0

        lax.fori_loop(0, TILE // BLOCK, block, 0, unroll=2)

    def decode(chunk):
        slot, half = chunk // HALVES, chunk % HALVES
        lanes = pl.ds(slot * TILE + half * LANES, LANES)
        wet = wet_ref[0, slot].astype(F32)

        def block(b, _):
            rows = pl.ds(pl.multiple_of(PAD + b * BLOCK, 8), BLOCK)

            def get(plane):
                return arrived[chunk, b // NZ, b % NZ, plane].astype(jnp.int32).astype(F32)

            chan = get(6) * (1.0 / 256.0)
            fields[WATER, rows, lanes] = get(0) * 2.0**-14 + (get(1) + 32768.0) * 2.0**-30
            fields[FLOW_X, rows, lanes] = flow_value(get(2))
            fields[FLOW_Y, rows, lanes] = flow_value(get(3))
            fields[BED, rows, lanes] = floor_value(get(4)) - chan
            fields[WIDTH, rows, lanes] = get(5) * (1.0 / 256.0)
            fields[CHAN, rows, lanes] = chan
            fields[ROUGH, rows, lanes] = get(7) * (1.0 / 8192.0) * wet - (1.0 - wet)
            return 0

        lax.fori_loop(0, TILE // BLOCK, block, 0, unroll=4)

    def copies(stage, chunk, axis, source, target, taken, put):
        base = (stage * CHUNKS + chunk) * 8
        remote = []
        if axis == "y":
            me = col
            steps = [4, 5, 2, 3, 6, 7, 1]
            partners = [((col + (d // 2) * 2) % NC) // 2 * 2 + (col + d % 2) % 2 for d in steps]
            devices = [place(own_x, own_z, c) for c in partners]
        elif axis == "x":
            me = own_x
            partners = [(own_x + d) % NX for d in (2, 1, 3)]
            devices = [place(x, own_z, col) for x in partners]
        else:
            me = own_z
            partners = [(own_z + d) % NZ for d in (2, 1, 3)]
            devices = [place(own_x, z, col) for z in partners]
        for q, (partner, device) in enumerate(zip(partners, devices)):
            remote.append(
                pltpu.make_async_remote_copy(
                    src_ref=part(source, taken, axis, partner),
                    dst_ref=part(target, put, axis, me),
                    send_sem=send_sem.at[base + q],
                    recv_sem=recv_sem.at[base + q],
                    device_id=device,
                    device_id_type=pl.DeviceIdType.MESH,
                )
            )
        local = pltpu.make_async_copy(
            part(source, taken, axis, me),
            part(target, put, axis, me),
            local_sem.at[stage * CHUNKS + chunk],
        )
        return remote, local

    started = []

    def launch(stage, chunk, axis, source, target, put=None):
        put = chunk if put is None else put
        remote, local = copies(stage, chunk, axis, source, target, chunk, put)
        for copy in remote:
            copy.start()
        local.start()
        started.extend(remote)
        return remote, local

    def landed(pair):
        remote, local = pair
        for copy in remote:
            copy.wait_recv()
        local.wait()

    middles = (middle_l, middle_r)
    encode(chunks[0])
    pl.semaphore_wait(barrier, len(greeted))
    flying = {}
    for chunk in chunks:
        if chunk != chunks[0]:
            encode(chunk)
        flying[chunk] = launch(0, chunk, FIRST[chunk // HALVES][0], coded, first_a)
    route = route_ref[...]
    target = (route[0:1] * NC + route[1:2]) * SLOTS + route[2:3]
    target = jnp.transpose(jnp.broadcast_to(target, (8, SLOTS * DEVICES)))[:, 0:1]
    old = lax.broadcasted_iota(jnp.int32, (SLOTS * DEVICES, LANES), 0)
    new = lax.broadcasted_iota(jnp.int32, (SLOTS * DEVICES, LANES), 1) * SLOTS
    device = jnp.right_shift(old * 171, 9)
    where_held = (old - device * SLOTS) * DEVICES + device
    source_rows[...] = jnp.zeros_like(source_rows)
    for slot in range(SLOTS):
        found = jnp.sum(jnp.where(new + slot == target, where_held, 0), axis=0, keepdims=True)
        source_rows[slot : slot + 1, :] = jnp.minimum(found, SLOTS * DEVICES - 1)
    to_scalars = pltpu.make_async_copy(source_rows, source_ref, source_sem)
    to_scalars.start()
    to_scalars.wait()
    opening = list(started)
    started.clear()
    for chunk in chunks:
        landed(flying[chunk])
        flying[chunk] = launch(1, chunk, FIRST[chunk // HALVES][1], first_a, first_b)
    for chunk in chunks:
        landed(flying[chunk])
        flying[chunk] = launch(
            2, chunk, FIRST[chunk // HALVES][2], first_b, middles[chunk % HALVES], chunk // HALVES
        )
    for copy in opening:
        copy.wait_send()
    ordered = coded.reshape(CHUNKS * DEVICES, BLOCK, LANES)
    for half in range(HALVES):
        group = chunks[half * SLOTS : (half + 1) * SLOTS]
        held = middles[half].reshape(SLOTS * DEVICES, BLOCK, LANES)
        for chunk in group:
            landed(flying[chunk])
        for chunk in group:
            slot = chunk // HALVES

            def move(k, _):
                for u in range(8):
                    d = k * 8 + u
                    ordered[chunk * DEVICES + d] = held[source_ref[slot, d]]
                return 0

            lax.fori_loop(0, DEVICES // 8, move, 0)
            flying[chunk] = launch(3, chunk, SECOND[slot][0], coded, second_a)
    for stage, source, target in ((4, second_a, second_b), (5, second_b, arrived)):
        for chunk in chunks:
            landed(flying[chunk])
            flying[chunk] = launch(stage, chunk, SECOND[chunk // HALVES][stage - 3], source, target)
    for chunk in chunks:
        landed(flying[chunk])
        decode(chunk)

    def rim(number, source, target, device):
        copy = pltpu.make_async_remote_copy(
            src_ref=source, dst_ref=target, send_sem=rim_send.at[number],
            recv_sem=rim_recv.at[number], device_id=device,
            device_id_type=pl.DeviceIdType.MESH,
        )
        copy.start()
        started.append(copy)
        return copy

    inner = pl.ds(0, COLS)
    outer = pl.ds(COLS, LANES)
    lane = lax.broadcasted_iota(jnp.int32, (TALL, LANES), 1)
    left = jnp.zeros((TALL, LANES), F32)
    right = jnp.zeros((TALL, LANES), F32)
    for k in range(TILE // TALL):
        rows = pl.ds(PAD + k * TALL, TALL)
        for f in range(FIELDS):
            start = FOLD * k + REACH * f
            here = (lane >= start) & (lane < start + REACH)
            low = fields[f, rows, pl.ds(0, LANES)]
            high = fields[f, rows, pl.ds(COLS - LANES, LANES)]
            left = jnp.where(here, pltpu.roll(low, start, 1) if start else low, left)
            right = jnp.where(here, pltpu.roll(high, start + REACH, 1), right)
    sent_w[...] = left
    sent_e[...] = right
    early, late = pl.ds(0, PAD), pl.ds(PAD + TILE, PAD)
    middle_rows, last_rows, next_rows = pl.ds(PAD, TALL), pl.ds(TALL - PAD, PAD), pl.ds(PAD + TALL, PAD)
    side = [
        rim(0, sent_w, got_e.at[middle_rows], west),
        rim(1, sent_e, got_w.at[middle_rows], east),
        rim(4, sent_w.at[early], got_e.at[next_rows], corners[0]),
        rim(5, sent_e.at[early], got_w.at[next_rows], corners[1]),
        rim(6, sent_w.at[last_rows], got_e.at[early], corners[2]),
        rim(7, sent_e.at[last_rows], got_w.at[early], corners[3]),
    ]
    upper = lax.broadcasted_iota(jnp.int32, (PAD, COLS), 0) < REACH
    top_rows, bottom_rows = pl.ds(PAD, PAD), pl.ds(TILE, PAD)
    for pair in range(PAIRS):
        f, g = 2 * pair, min(2 * pair + 1, FIELDS - 1)
        turned = pltpu.roll(fields[g, top_rows, inner], REACH, 0)
        sent_n[pair] = jnp.where(upper, fields[f, top_rows, inner], turned)
        turned = pltpu.roll(fields[g, bottom_rows, inner], REACH, 0)
        sent_s[pair] = jnp.where(upper, turned, fields[f, bottom_rows, inner])
    ends = [rim(2, sent_n, got_s, north), rim(3, sent_s, got_n, south)]

    row_of = lax.broadcasted_iota(jnp.int32, (8, LANES), 0)
    bottom = row_of == 7
    top = row_of == 0
    lanes_high = lax.broadcasted_iota(jnp.int32, (HIGH, LANES), 1)
    right_end = lanes_high == LANES - 1
    left_end = lanes_high == 0

    def strip(k, high=HIGH):
        return pl.ds(pl.multiple_of(k * high, 8), high)

    def below_strip(k, high=HIGH):
        return pl.ds(pl.multiple_of(jnp.minimum((k + 1) * high, ROWS - 8), 8), 8)

    def from_south(values, after):
        high = values.shape[0]
        moved = pltpu.roll(values, high - 1, 0)
        end = jnp.where(bottom, pltpu.roll(after, 7, 0), moved[high - 8 :])
        return jnp.concatenate([moved[: high - 8], end], 0) if high > 8 else end

    def from_north(values, before):
        moved = pltpu.roll(values, 1, 0)
        start = jnp.where(top, before, moved[:8])
        return (jnp.concatenate([start, moved[8:]], 0) if HIGH > 8 else start), moved[:8]

    def block(c):
        return pl.ds((c % BLOCKS) * LANES, LANES)

    def faces(k, c):
        here = strip(k, FACE_HIGH)
        there = below_strip(k, FACE_HIGH)
        last_lane = lax.broadcasted_iota(jnp.int32, (FACE_HIGH, LANES), 1) == LANES - 1
        water = fields[WATER, here, block(c)]
        bed, width = fields[BED, here, block(c)], fields[WIDTH, here, block(c)]
        chan, rough = fields[CHAN, here, block(c)], fields[ROUGH, here, block(c)]
        level[here, block(c)] = bed + water
        volume[here, block(c)] = (CELL / STEP) * width * jnp.minimum(water, chan) + (
            CELL * CELL / STEP
        ) * jnp.maximum(water - chan, 0.0)
        cap[here, block(c)] = (CELL / STEP) * width * chan
        inverse[here, block(c)] = (STEP / CELL) / width - STEP / (CELL * CELL)

        def to_east(f, v):
            after = pltpu.roll(fields[f, here, block(c + 1)], LANES - 1, 1)
            return jnp.where(last_lane, after, pltpu.roll(v, LANES - 1, 1))

        def to_south(f, v):
            return from_south(v, fields[f, there, block(c)])

        for shift, bed_f, part_f, deep_f, drag_f, gate_f, f, flow in (
            (to_east, bed_x, part_x, deep_x, drag_x, gate_x, FLOW_X, flow_x),
            (to_south, bed_y, part_y, deep_y, drag_y, gate_y, FLOW_Y, flow_y),
        ):
            bed_f[here, block(c)] = jnp.maximum(bed, shift(BED, bed))
            part_f[here, block(c)] = 1.0 - jnp.minimum(width, shift(WIDTH, width)) * (1.0 / CELL)
            deep_f[here, block(c)] = jnp.minimum(chan, shift(CHAN, chan))
            rough_n = shift(ROUGH, rough)
            mean = 0.5 * (rough + rough_n)
            wet = jnp.minimum(rough, rough_n) > 0
            drag_f[here, block(c)] = jnp.where(wet, (GRAV * STEP / CELL) * mean * mean, 0.0)
            gate_f[here, block(c)] = jnp.where(wet, GRAV * STEP, 0.0)
            flow[here, block(c)] = jnp.where(wet, fields[f, here, block(c)], 0.0)

    def many_faces(start, stop, blocks):
        def one(k, _):
            for c in blocks:
                faces(k, c)
            return 0

        lax.fori_loop(start, stop, one, 0)

    many_faces(1, TILE // FACE_HIGH, range(BLOCKS - 2))

    for copy in side:
        copy.wait_recv()
    at_east = col == NC - 1
    at_west = col == 0

    segments = [(early, early, FOLD * (TILE // TALL - 1)), (late, next_rows, 0)]
    segments += [(pl.ds(PAD + k * TALL, TALL), middle_rows, FOLD * k) for k in range(TILE // TALL)]
    for rows, got, fold in segments:
        from_e, from_w = got_e[got, :], got_w[got, :]
        at = lax.broadcasted_iota(jnp.int32, from_e.shape, 1)
        for f in range(FIELDS):
            start = fold + REACH * f
            low = pltpu.roll(from_e, LANES - start, 1) if start else from_e
            high = pltpu.roll(from_w, LANES - REACH - start, 1) if start < LANES - REACH else from_w
            if f == ROUGH:
                low = jnp.where(at_east, -1.0, low)
                high = jnp.where(at_west, -1.0, high)
            fill = 1.0 if f in (WIDTH, CHAN) else (-1.0 if f == ROUGH else 0.0)
            mixed = jnp.where(at < REACH, low, jnp.where(at >= LANES - REACH, high, fill))
            fields[f, rows, outer] = mixed

    many_faces(1, TILE // FACE_HIGH, range(BLOCKS - 2, BLOCKS))
    for copy in ends:
        copy.wait_recv()
    for pair in range(PAIRS):
        for got, rows in ((got_n, early), (got_s, late)):
            fields[2 * pair, rows, inner] = got[pair]
            if 2 * pair + 1 < FIELDS:
                fields[2 * pair + 1, rows, inner] = pltpu.roll(got[pair], REACH, 0)
    first = fields[ROUGH, pl.ds(0, 8), :]
    fields[ROUGH, pl.ds(0, 8), :] = jnp.where(row == 0, -1.0, first)
    last = fields[ROUGH, pl.ds(PAD + TILE, 8), :]
    fields[ROUGH, pl.ds(PAD + TILE, 8), :] = jnp.where(row == NX * NZ - 1, -1.0, last)
    many_faces(0, 1, range(BLOCKS))
    many_faces(TILE // FACE_HIGH, ROWS // FACE_HIGH, range(BLOCKS))

    def face_flow(flow, surface, surface_n, bed_f, part_f, deep_f, drag_f, gate_f):
        crest = jnp.maximum(surface, surface_n) - bed_f
        depth = crest - part_f * jnp.minimum(crest, deep_f)
        power = jnp.exp2(jnp.log(jnp.maximum(depth, RMIN)) * (-7.0 / 3.0 * LOG2_E))
        below = 1.0 + drag_f * jnp.abs(flow) * power
        guess = pl.reciprocal(below, approx=True)
        guess = guess * (2.0 - below * guess)
        return (flow - gate_f * depth * (surface_n - surface)) * guess

    every = range(BLOCKS)
    for step in range(ITERS):
        final = step == ITERS - 1

        def sweep(k, above):
            here = strip(k)
            there = below_strip(k)
            surface = [level[here, block(c)] for c in every]
            turned = [pltpu.roll(v, LANES - 1, 1) for v in surface]
            new_x = []
            for c in every:
                b = block(c)
                surface_e = jnp.where(right_end, turned[(c + 1) % BLOCKS], turned[c])
                new_x.append(
                    face_flow(
                        flow_x[here, b], surface[c], surface_e, bed_x[here, b], part_x[here, b],
                        deep_x[here, b], drag_x[here, b], gate_x[here, b],
                    )
                )
            passed = [pltpu.roll(v, 1, 1) for v in new_x]
            sunk = []
            for c in every:
                b = block(c)
                surface_s = from_south(surface[c], level[there, b])
                new_y = face_flow(
                    flow_y[here, b], surface[c], surface_s, bed_y[here, b], part_y[here, b],
                    deep_y[here, b], drag_y[here, b], gate_y[here, b],
                )
                from_n, end = from_north(new_y, above[c])
                sunk.append(end)
                from_w = jnp.where(left_end, passed[c - 1], passed[c])
                inflow = from_w - new_x[c] + from_n - new_y
                held = jnp.maximum(volume[here, b] + inflow, 0.0)
                water = jnp.minimum(held, cap[here, b]) * inverse[here, b] + held * (
                    STEP / (CELL * CELL)
                )
                if not final:
                    flow_x[here, b] = new_x[c]
                    flow_y[here, b] = new_y
                    volume[here, b] = held
                    level[here, b] = fields[BED, here, b] + water
                elif c < BLOCKS - 1:
                    water_out[here, b] = water
                    fx_out[here, b] = new_x[c]
                    fy_out[here, b] = new_y
            return tuple(sunk)

        carry = tuple(jnp.zeros((8, LANES), F32) for c in every)
        if not final:
            lax.fori_loop(0, STRIPS, sweep, carry)

    stores = []
    begin = 0
    sent = 0
    for piece in range(PARTS):
        end = -(-(PAD + (piece + 1) * (TILE // PARTS)) // HIGH)
        carry = lax.fori_loop(begin, end, sweep, carry)
        begin = end
        until = min(TILE, end * HIGH - PAD) if piece < PARTS - 1 else TILE
        size = until - sent
        for n, (ref, hbm) in enumerate(
            ((water_out, water_hbm), (fx_out, fx_out_hbm), (fy_out, fy_out_hbm))
        ):
            copy = pltpu.make_async_copy(
                ref.at[pl.ds(PAD + sent, size)], hbm.at[pl.ds(sent, size)], out_sem.at[piece * 3 + n]
            )
            copy.start()
            stores.append(copy)
        sent = until
    for copy in stores:
        copy.wait()
    for copy in started:
        copy.wait_send()


def body(depth, flow_x, flow_y, floor, width, chan, rough, route, wet_tiles):
    whole = pl.BlockSpec(memory_space=pl.ANY)
    smem = pl.BlockSpec(memory_space=pltpu.SMEM)
    pieces = pltpu.VMEM(PIECES, jnp.int16)
    grid = pltpu.VMEM((ROWS, WIDE), F32)
    edge = pltpu.VMEM((TALL, LANES), F32)
    out = jax.ShapeDtypeStruct((TILE, COLS), F32)
    operands = (depth, flow_x, flow_y, floor, width, chan, rough)
    return pl.pallas_call(
        migrate_and_route,
        out_shape=(out, out, out),
        in_specs=[whole] * 7 + [pl.BlockSpec(memory_space=pltpu.VMEM), smem],
        out_specs=(whole, whole, whole),
        scratch_shapes=[pltpu.VMEM(a.shape, a.dtype) for a in operands]
        + [pltpu.VMEM((ROWS, COLS), F32)] * 3
        + [pieces] * 3
        + [pltpu.VMEM((SLOTS,) + PIECES[1:], jnp.int16)] * 2
        + [pieces] * 3
        + [pltpu.VMEM((FIELDS, ROWS, WIDE), F32)]
        + [edge] * 2
        + [pltpu.VMEM((TALL + 2 * PAD, LANES), F32)] * 2
        + [pltpu.VMEM((PAIRS, PAD, COLS), F32)] * 4
        + [grid] * 16
        + [pltpu.VMEM((8, LANES), jnp.int32), pltpu.SMEM((8, LANES), jnp.int32)]
        + [
            pltpu.SemaphoreType.DMA((6 * CHUNKS * 8,)),
            pltpu.SemaphoreType.DMA((6 * CHUNKS * 8,)),
            pltpu.SemaphoreType.DMA((6 * CHUNKS,)),
            pltpu.SemaphoreType.DMA((8,)),
            pltpu.SemaphoreType.DMA((8,)),
            pltpu.SemaphoreType.DMA((CHUNKS * FIELDS,)),
            pltpu.SemaphoreType.DMA((PARTS * 3,)),
            pltpu.SemaphoreType.DMA,
        ],
        compiler_params=pltpu.CompilerParams(
            collective_id=0, has_side_effects=True, vmem_limit_bytes=58 * 2**20
        ),
    )(*operands, route.T, wet_tiles)


def solution(mesh):
    tiles = P(("row", "col"), None, None)
    block = P("row", "col")
    return jax.shard_map(
        body,
        mesh=mesh,
        in_specs=(tiles,) * 7 + (P(), block),
        out_specs=(block, block, block),
        check_vma=False,
    )
```
